128 devices in a mesh: dp: 16 (over y, z_lo, core), row: 4 (over x), col: 2 (over z_hi).
Axes of the slice: x: 4, y: 4, z: 4 (z_hi: 2, z_lo: 2; z = z_hi * 2 + z_lo), core: 2. Of those that a mesh axis runs over, the one named last changes fastest.
Arguments:
- block_in: bfloat16 [8192, 2048], P('dp', ('row', 'col')), may hold values from -6 to 6
- segments: int32 [8192], P('dp'), may hold values from 0 to 31, never falling along the last dimension, each value on 1 to 1024 neighbouring positions
- ln1_gain: float32 [2048], P(('row', 'col')), may hold values from 0.5 to 1.5
- ln1_bias: float32 [2048], P(('row', 'col')), may hold values from -3 to 3
- qkv_weight: bfloat16 [2048, 6144], P('row', 'col'), may hold values from -0.125 to 0.125
- qkv_bias: float32 [6144], P(('col', 'row')), may hold values from -3 to 3
- out_weight: bfloat16 [2048, 2048], P('col', 'row'), may hold values from -0.5 to 0.5
- ln2_gain: float32 [2048], P(('row', 'col')), may hold values from 0.5 to 1.5
- ln2_bias: float32 [2048], P(('row', 'col')), may hold values from -3 to 3
- gate_up_weight: bfloat16 [2048, 2, 5632], P('row', None, 'col'), may hold values from -0.125 to 0.125
- down_weight: bfloat16 [5632, 2048], P('col', 'row'), may hold values from -0.078125 to 0.078125
- cotangent: bfloat16 [8192, 2048], P('dp', ('row', 'col')), may hold values from -6 to 6
Outputs:
- activations: bfloat16 [8192, 2048], P('dp', ('row', 'col'))
- input_grad: bfloat16 [8192, 2048], P('dp', ('row', 'col'))
- ln1_gain_grad: float32 [2048], P(('row', 'col'))
- ln1_bias_grad: float32 [2048], P(('row', 'col'))
- qkv_weight_grad: float32 [2048, 6144], P('row', 'col')
- qkv_bias_grad: float32 [6144], P(('col', 'row'))
- out_weight_grad: float32 [2048, 2048], P('col', 'row')
- ln2_gain_grad: float32 [2048], P(('row', 'col'))
- ln2_bias_grad: float32 [2048], P(('row', 'col'))
- gate_up_grad: float32 [2048, 2, 5632], P('row', None, 'col')
- down_grad: float32 [5632, 2048], P('col', 'row')
The draws below stay inside these ranges and needn't reach their ends.
Inputs may be any that keep to these rules, and one draw needn't show every extreme that they name: `segments`: segment numbers never fall along the tokens; tokens attend only within their own sequence of 512 and their own segment.
All inputs are finite; a program needn't handle non-finite values.
Results may differ from the reference program's by a relative error of at most 0.04.
Values may be sent and summed in bfloat16 or wider, within the bound.
A program may use at most 128 MiB of HBM per device.

```python
import math
import jax
import jax.numpy as jnp
import numpy as np
from jax import lax

D = 2048
H = 32
HD = 64
FF = 5632
ROT = 16
TOKG = 512
TOKENS = 8192
N_DP = 16


def level_of(rng, shape, split, least, high):
    level = 1.0
    for axis_at, blocks in split:
        steps = jax.random.uniform(jax.random.fold_in(jax.random.fold_in(rng, 6), axis_at), (blocks,), jnp.float32, least / len(split), high / len(split))
        level = level * jnp.repeat(jnp.exp(steps), shape[axis_at] // blocks).reshape((-1,) + (1,) * (len(shape) - 1 - axis_at))
    return level


def length_profile(amount, total, reach, slope):
    loads = [(1 << 20) // math.isqrt(rank ** slope) + 1 for rank in range(2, amount + 1)]
    surplus, given = total - reach - (amount - 1), [1] * (amount - 1)
    while surplus > 0:
        movable = [i for i in range(amount - 1) if given[i] < reach]
        mass, remaining = sum([loads[i] for i in movable]), surplus
        for i in movable:
            addition = min(reach - given[i], max(1, remaining * loads[i] // mass), surplus)
            given[i] = given[i] + addition
            surplus = surplus - addition
    return np.array([reach] + given)


def ragged(own_key, amount, total, limit, skew):
    if amount == 2:
        one = jax.random.randint(own_key, (), max(1, total - limit), min(limit, total - 1) + 1)
        return jnp.stack([one, total - one])
    sizes = jnp.asarray(length_profile(amount, total, limit, skew), jnp.int32)
    twos = (amount - 1) // 2
    giver, receiver = sizes[1:1 + 2 * twos:2], sizes[2:2 + 2 * twos:2]
    slack = jnp.minimum(giver - 1, limit - receiver)
    passed = jax.random.randint(jax.random.fold_in(own_key, 1), (twos,), 0, 1 << 20) % (slack + 1)
    sizes = sizes.at[1:1 + 2 * twos:2].set(giver - passed).at[2:2 + 2 * twos:2].set(receiver + passed)
    return sizes[jax.random.permutation(jax.random.fold_in(own_key, 2), amount)]


def normal_values(stream_key, dims, scale, limit, split=(), held_as=jnp.bfloat16):
    result = scale * jax.random.normal(stream_key, dims, jnp.float32)
    if split:
        result = result * level_of(stream_key, dims, split, -0.22, 0.18)
    return jnp.clip(result, -limit, limit).astype(held_as)


def setup_inputs(seed: int = 0) -> dict:
    arg_keys = jax.random.split(jax.random.key(seed), 13)
    block_in = normal_values(arg_keys[0], (TOKENS, D), 1.0, 6.0, ((0, 16), (1, 8)))
    segments = jnp.searchsorted(jnp.cumsum(ragged(arg_keys[1], 2 * N_DP, TOKENS, 2 * TOKG, 0)), jnp.arange(TOKENS), side="right").astype(jnp.int32)
    ln1_gain = jnp.clip(1.0 + 0.1 * jax.random.normal(arg_keys[2], (D,), jnp.float32), 0.5, 1.5)
    ln1_bias = normal_values(arg_keys[3], (D,), 0.5, 3.0, ((0, 8),), jnp.float32)
    qkv_weight = normal_values(arg_keys[4], (D, 3 * D), D ** -0.5, 0.125, ((0, 4), (1, 2)))
    qkv_bias = normal_values(arg_keys[5], (3 * D,), 0.5, 3.0, ((0, 8),), jnp.float32)
    out_weight = normal_values(arg_keys[6], (D, D), (D // 16) ** -0.5, 0.5, ((0, 2), (1, 4)))
    ln2_gain = jnp.clip(1.0 + 0.1 * jax.random.normal(arg_keys[7], (D,), jnp.float32), 0.5, 1.5)
    ln2_bias = normal_values(arg_keys[8], (D,), 0.5, 3.0, ((0, 8),), jnp.float32)
    gate_up_weight = normal_values(arg_keys[9], (D, 2, FF), D ** -0.5, 0.125, ((0, 4), (2, 2)))
    down_weight = normal_values(arg_keys[10], (FF, D), FF ** -0.5, 0.078125, ((0, 2), (1, 4)))
    cotangent = normal_values(arg_keys[11], (TOKENS, D), 1.0, 6.0, ((0, 16), (1, 8)))
    return dict(block_in=block_in, segments=segments, ln1_gain=ln1_gain, ln1_bias=ln1_bias, qkv_weight=qkv_weight, qkv_bias=qkv_bias, out_weight=out_weight, ln2_gain=ln2_gain, ln2_bias=ln2_bias, gate_up_weight=gate_up_weight, down_weight=down_weight, cotangent=cotangent)


EPSILON = 1e-05
HIGHEST_PRECISION = lax.Precision.HIGHEST

@jax.custom_vjp
def low(v):
    return lax.optimization_barrier(v.astype(jnp.bfloat16)).astype(jnp.float32)

@jax.custom_vjp
def low_back(v):
    return v

def low_keep(v):
    return (low(v), None)

def low_pass(kept, grad):
    return (grad,)

def back_keep(v):
    return (v, None)

def back_low(kept, grad):
    return (low(grad),)
low.defvjp(low_keep, low_pass)
low_back.defvjp(back_keep, back_low)

def matmul(left, right):
    return jnp.dot(left, right, precision=HIGHEST_PRECISION, preferred_element_type=jnp.float32)

def layer_norm(operand, norm_gain, norm_shift):
    feature_mean = lax.optimization_barrier(jnp.mean(operand, axis=-1, keepdims=True))
    square = lax.optimization_barrier(jnp.mean(operand * operand, axis=-1, keepdims=True))
    scaled = (operand - feature_mean) * lax.rsqrt(square - feature_mean * feature_mean + EPSILON)
    return scaled * norm_gain + norm_shift

def rotary_tables(segment):
    length = segment.shape[0]
    places = jnp.arange(length, dtype=jnp.int32)
    starts_flag = jnp.concatenate([jnp.array([True]), segment[1:] != segment[:-1]])
    starts = lax.cummax(jnp.where(starts_flag, places, 0), axis=0)
    offsets = (places - starts).astype(jnp.float32)
    half_width = ROT // 2
    frequencies = jnp.exp(jnp.arange(half_width, dtype=jnp.float32) * (-2.0 * math.log(10000.0) / ROT))
    angles = offsets[:, None] * frequencies[None, :]
    return (jnp.cos(angles)[:, None, :], jnp.sin(angles)[:, None, :])

def rotate(operand, cosine, sine_table):
    half_width = ROT // 2
    first_half = operand[..., :half_width]
    second_half = operand[..., half_width:ROT]
    return jnp.concatenate([first_half * cosine - second_half * sine_table, second_half * cosine + first_half * sine_table, operand[..., ROT:]], axis=-1)

def attend(queries, key_heads, values, segment):
    length = segment.shape[0]
    places = jnp.arange(length, dtype=jnp.int32)
    allowed = (places[None, :] <= places[:, None]) & (segment[None, :] == segment[:, None])
    scores = jnp.einsum('qhd,khd->hqk', queries, key_heads, precision=HIGHEST_PRECISION) * (1.0 / math.sqrt(HD))
    scores = low_back(jnp.where(allowed[None], scores, -1e+30))
    row_maximum = lax.optimization_barrier(jnp.max(scores, axis=-1, keepdims=True))
    raised = jnp.exp(scores - row_maximum)
    probs_low = low(raised / lax.optimization_barrier(jnp.sum(raised, axis=-1, keepdims=True)))
    return jnp.einsum('hqk,khd->qhd', probs_low, values, precision=HIGHEST_PRECISION)

def layer_forward(block_rows, segment, ln1_gain, ln1_bias, qkv_weight, qkv_bias, out_weight, ln2_gain, ln2_bias, gate_up_weight, down_weight):
    normed = low(layer_norm(block_rows, ln1_gain, ln1_bias))
    projected = low_back(matmul(normed, qkv_weight) + qkv_bias).reshape(-1, H, 3, HD)
    cosine, sine_table = rotary_tables(segment)
    queries = low(rotate(projected[:, :, 0], cosine, sine_table))
    key_heads = low(rotate(projected[:, :, 1], cosine, sine_table))
    values = low(projected[:, :, 2])
    attended = low(low_back(jax.checkpoint(attend)(queries, key_heads, values, segment))).reshape(-1, D)
    hidden_in = block_rows + low_back(matmul(attended, out_weight))
    normed_two = low(layer_norm(hidden_in, ln2_gain, ln2_bias))
    gate_up = low_back(matmul(normed_two, gate_up_weight.reshape(D, 2 * FF))).reshape(-1, 2, FF)
    gate_value = gate_up[:, 0]
    up_value = gate_up[:, 1]
    hidden = low(gate_value * jax.nn.sigmoid(gate_value) * up_value)
    return hidden_in + low_back(matmul(hidden, down_weight))

def reference(block_in, segments, ln1_gain, ln1_bias, qkv_weight, qkv_bias, out_weight, ln2_gain, ln2_bias, gate_up_weight, down_weight, cotangent):
    parameters = tuple((array_in.astype(jnp.float32) for array_in in (ln1_gain, ln1_bias, qkv_weight, qkv_bias, out_weight, ln2_gain, ln2_bias, gate_up_weight, down_weight)))
    inputs = block_in.astype(jnp.float32).reshape(N_DP, TOKG, D)
    upstream = cotangent.astype(jnp.float32).reshape(N_DP, TOKG, D)
    segment_rows = segments.reshape(N_DP, TOKG)

    def one_sequence(running, scan_item):
        rows_in, segment, grad_out = scan_item

        def forward(block_rows, *weights):
            return layer_forward(block_rows, segment, *weights)
        block_out, pullback = jax.vjp(forward, rows_in, *parameters)
        gradients = pullback(grad_out)
        running = tuple((earlier + addend for earlier, addend in zip(running, gradients[1:])))
        return (running, (block_out.astype(jnp.bfloat16), gradients[0].astype(jnp.bfloat16)))
    zero_grads = tuple((jnp.zeros_like(array_in) for array_in in parameters))
    totals, (outputs, input_grads) = lax.scan(one_sequence, zero_grads, (inputs, segment_rows, upstream))
    return (outputs.reshape(TOKENS, D), input_grads.reshape(TOKENS, D), totals[0], totals[1], totals[2], totals[3], totals[4], totals[5], totals[6], totals[7], totals[8])
```

```python
import math

import jax
import jax.numpy as jnp
from jax import lax
from jax.experimental import pallas as pl
from jax.experimental.pallas import tpu as pltpu
from jax.sharding import PartitionSpec as P

D = 2048
HD = 64
ROT = 16
HEADS = 4
TOK = 512
OWN = 64
WIDE = 768
EPSILON = 1e-05
BF = jnp.bfloat16
F32 = jnp.float32
MESH = pl.DeviceIdType.MESH
VMEM_LIMIT = 60 * 2**20
ROWS_BY_COLS = (((1,), (1,)), ((), ()))
OVER_ROWS = (((0,), (0,)), ((), ()))

IN_VMEM = pl.BlockSpec(memory_space=pltpu.VMEM)
IN_ANY = pl.BlockSpec(memory_space=pl.ANY)


class Place:
    def __init__(self):
        self.dp = lax.axis_index("dp")
        self.x = lax.axis_index("row")
        self.zh = lax.axis_index("col")
        self.y = self.dp // 4
        self.zl = (self.dp // 2) % 2
        self.core = self.dp % 2
        self.q = self.dp // 2
        self.g = self.x * 2 + self.zh

    def group(self, g):
        return (self.dp, g // 2, g % 2)

    def row(self, x):
        return (self.dp, x, self.zh)

    def chip(self, q):
        return (q * 2 + self.core, self.x, self.zh)

    def sibling(self):
        return (self.q * 2 + 1 - self.core, self.x, self.zh)

    def replica(self, dp):
        return (dp, self.x, self.zh)


def greet(partners):
    barrier = pltpu.get_barrier_semaphore()
    for partner in partners:
        pl.semaphore_signal(barrier, inc=1, device_id=partner, device_id_type=MESH)
    pl.semaphore_wait(barrier, len(partners))


def push(src, dst, sems, index, device):
    send, recv = sems
    copy = pltpu.make_async_remote_copy(
        src_ref=src,
        dst_ref=dst,
        send_sem=send.at[index],
        recv_sem=recv.at[index],
        device_id=device,
        device_id_type=MESH,
    )
    copy.start()
    return copy


def group_others(at):
    return [at.group((at.g + k) % 8) for k in range(1, 8)]


def chip_others(at):
    return [at.chip(at.q ^ k) for k in range(1, 8)]


def dma_sems(amount):
    return [pltpu.SemaphoreType.DMA((amount,)), pltpu.SemaphoreType.DMA((amount,))]


def params(collective_id):
    return pltpu.CompilerParams(
        collective_id=collective_id, has_side_effects=True, vmem_limit_bytes=VMEM_LIMIT
    )


def tile_start(x):
    return 5 * x + jnp.minimum(x, 1)


def gather_kernel(
    x_in, cot_in, par_in, qkv_w, out_w, gu_w, down_w,
    x_out, cot_out, par_out, qkv_s, out_s, gu_s, down_s,
    act_send, act_recv, a_send, a_recv, b_send, b_recv, c_send, c_recv, local,
):
    at = Place()
    greet(group_others(at) + chip_others(at) + [at.sibling()])
    act, step_a, step_b, step_c = (
        (act_send, act_recv), (a_send, a_recv), (b_send, b_recv), (c_send, c_recv)
    )
    dp, x, core, q = at.dp, at.x, at.core, at.q

    def source(k, xt):
        if k == 0:
            return qkv_w.at[pl.ds(dp * 32, 32), pl.ds(xt * WIDE, WIDE)]
        if k == 1:
            return out_w.at[pl.ds(xt * 256 + dp * 16, 16), :]
        if k == 2:
            return gu_w.at[:, pl.ds(dp * 32, 32), pl.ds(tile_start(xt) * 128, WIDE)]
        return down_w.at[pl.ds(tile_start(xt) * 128 + dp * 48, 48), :]

    def landing(k, xs):
        if k == 0:
            return qkv_s.at[xs, dp]
        if k == 1:
            return out_s.at[dp, :, pl.ds(xs * 512, 512)]
        if k == 2:
            return gu_s.at[:, xs, dp]
        return down_s.at[dp, :, pl.ds(xs * 512, 512)]

    def piece(k, p):
        if k == 0:
            return qkv_s.at[:, p]
        if k == 1:
            return out_s.at[p]
        if k == 2:
            return gu_s.at[:, :, p]
        return down_s.at[p]

    waits = []
    for k in range(4):
        for j in range(1, 4):
            xt = (x + j) % 4
            waits.append(push(source(k, xt), landing(k, x), step_a, k * 3 + j - 1, at.row(xt)))
    own = []
    for k in range(4):
        own.append(pltpu.make_async_copy(source(k, x), landing(k, x), local.at[k]))
    slot = pl.ds(at.g * 256, 256)
    own.append(pltpu.make_async_copy(x_in, x_out.at[:, slot], local.at[4]))
    own.append(pltpu.make_async_copy(cot_in, cot_out.at[:, slot], local.at[5]))
    own.append(pltpu.make_async_copy(par_in, par_out.at[:, slot], local.at[6]))
    for copy in own:
        copy.start()
    for j, device in enumerate(group_others(at)):
        waits.append(push(par_in, par_out.at[:, slot], act, 14 + j, device))
    for j, device in enumerate(group_others(at)):
        waits.append(push(x_in, x_out.at[:, slot], act, j, device))
    for j, device in enumerate(group_others(at)):
        waits.append(push(cot_in, cot_out.at[:, slot], act, 7 + j, device))
    for copy in own:
        copy.wait()
    second = []
    for k in range(4):
        for j in range(3):
            waits[k * 3 + j].wait_recv()
        for m, device in enumerate(chip_others(at)):
            second.append(push(piece(k, dp), piece(k, dp), step_b, k * 7 + m, device))
        third = push(piece(k, dp), piece(k, dp), step_c, k * 8, at.sibling())
        waits.append(third)
    for k in range(4):
        for m in range(1, 8):
            second[k * 7 + m - 1].wait_recv()
            p = (q ^ m) * 2 + core
            waits.append(push(piece(k, p), piece(k, p), step_c, k * 8 + m, at.sibling()))
    for index, copy in enumerate(waits):
        copy.wait_send()
        if index >= 12:
            copy.wait_recv()
    for copy in second:
        copy.wait_send()


def gather_inputs(x_in, cot_in, par_in, qkv_w, out_w, gu_w, down_w):
    shape = jax.ShapeDtypeStruct
    outs = pl.pallas_call(
        gather_kernel,
        out_shape=(
            shape((TOK, D), BF),
            shape((TOK, D), BF),
            shape((8, D), F32),
            shape((4, 16, 32, WIDE), BF),
            shape((16, 16, D), BF),
            shape((2, 4, 16, 32, WIDE), BF),
            shape((16, 48, D), BF),
        ),
        in_specs=[IN_ANY] * 7,
        out_specs=(IN_ANY,) * 7,
        scratch_shapes=dma_sems(21)
        + dma_sems(12)
        + dma_sems(28)
        + dma_sems(32)
        + [pltpu.SemaphoreType.DMA((7,))],
        compiler_params=params(1),
        name="gather_inputs",
    )(x_in, cot_in, par_in, qkv_w, out_w, gu_w, down_w)
    x_full, cot_full, par_full, qkv_s, out_s, gu_s, down_s = outs
    return (
        x_full,
        cot_full,
        par_full,
        qkv_s.reshape(D, WIDE),
        out_s.reshape(256, D),
        gu_s.reshape(2, D, WIDE),
        down_s.reshape(WIDE, D),
    )


def settle(src, sems, index, device):
    send, recv = sems
    return pltpu.make_async_remote_copy(
        src_ref=src,
        dst_ref=src,
        send_sem=send.at[index],
        recv_sem=recv.at[index],
        device_id=device,
        device_id_type=MESH,
    )


def scatter_sum(at, product, part, got, sems):
    def step(i, carry):
        xt = (at.x + i + 1) % 4
        part[pl.ds(pl.multiple_of(xt * 128, 128), 128), :] = product(xt).astype(BF)
        for half in range(2):
            g = xt * 2 + half
            index = (g - at.g + 15) % 8

            @pl.when(index < 7)
            def _():
                push(
                    part.at[pl.ds(pl.multiple_of(g * OWN, OWN), OWN)],
                    got.at[index],
                    sems,
                    index,
                    at.group(g),
                )

        return carry

    lax.fori_loop(0, 4, step, 0)


def own_rows(at):
    return pl.ds(pl.multiple_of(at.g * OWN, OWN), OWN)


def summed(at, part, got, sems):
    total = part[own_rows(at), :].astype(F32)
    for k in range(7):
        settle(got.at[k], sems, k, at.group(at.g)).wait_recv()
        total += got[k].astype(F32)
    return total


def sent(at, buffer, sems, amount=7):
    for k in range(amount):
        settle(buffer, sems, k, at.group(at.g)).wait_send()


def gather_rows(at, rows, full, sems, local):
    copy = pltpu.make_async_copy(rows, full.at[own_rows(at)], local)
    copy.start()
    for k in range(1, 8):
        push(rows, full.at[own_rows(at)], sems, k - 1, at.group((at.g + k) % 8))
    copy.wait()


def gather_columns(at, rows, full, sems, local):
    def columns(g):
        return rows.at[:, pl.ds(pl.multiple_of(g * 256, 256), 256)]

    copy = pltpu.make_async_copy(columns(at.g), full.at[own_rows(at)], local)
    copy.start()
    for k in range(1, 8):
        g = (at.g + k) % 8
        push(columns(g), full.at[own_rows(at)], sems, k - 1, at.group(g))
    copy.wait()


def settle_all(at, piece, sems, amount=7):
    for k in range(amount):
        copy = settle(piece, sems, k, at.group(at.g))
        copy.wait_send()
        copy.wait_recv()


def norm(value):
    mean = jnp.mean(value, axis=1, keepdims=True)
    square = jnp.mean(value * value, axis=1, keepdims=True)
    inverse = lax.rsqrt(square - mean * mean + EPSILON)
    return (value - mean) * inverse, inverse


def norm_back(grad, scaled, inverse, gain):
    inner = grad * gain
    mean = jnp.mean(inner, axis=1, keepdims=True)
    along = jnp.mean(inner * scaled, axis=1, keepdims=True)
    return inverse * (inner - mean - scaled * along)


def attend_out_kernel(
    attended, weight, x_full, par, hidden_out, normed_out,
    part, got, rows, rs_send, rs_recv, ag_send, ag_recv, local,
):
    at = Place()
    greet(group_others(at))
    rs, ag = (rs_send, rs_recv), (ag_send, ag_recv)

    def product(xt):
        block = attended[pl.ds(pl.multiple_of(xt * 128, 128), 128), :]
        return jnp.dot(block, weight[...], preferred_element_type=F32)

    scatter_sum(at, product, part, got, rs)
    hidden_in = summed(at, part, got, rs) + x_full[own_rows(at), :].astype(F32)
    hidden_out[...] = hidden_in
    scaled, _ = norm(hidden_in)
    rows[...] = (scaled * par[2:3, :] + par[3:4, :]).astype(BF)
    gather_rows(at, rows, normed_out, ag, local.at[0])
    sent(at, got.at[0], rs)
    settle_all(at, rows, ag)


def attend_out(attended, weight, x_full, par):
    return pl.pallas_call(
        attend_out_kernel,
        out_shape=(jax.ShapeDtypeStruct((OWN, D), F32), jax.ShapeDtypeStruct((TOK, D), BF)),
        in_specs=[IN_VMEM] * 4,
        out_specs=(IN_VMEM, IN_ANY),
        scratch_shapes=[
            pltpu.VMEM((TOK, D), BF),
            pltpu.VMEM((7, OWN, D), BF),
            pltpu.VMEM((OWN, D), BF),
        ]
        + dma_sems(7)
        + dma_sems(7)
        + [pltpu.SemaphoreType.DMA((1,))],
        compiler_params=params(2),
        name="attend_out",
    )(attended, weight, x_full, par)


def mlp_back_kernel(
    grad_gate, grad_up, gu_s, hidden, down_s, hidden_in, cot_full, par,
    grad_in_out, branch_out, act_out, sums_out,
    part, got, rows, part2, got2, rows2,
    rs_send, rs_recv, ag_send, ag_recv, rt_send, rt_recv, tr_send, tr_recv, local,
):
    at = Place()
    greet(group_others(at))
    rs, ag = (rs_send, rs_recv), (ag_send, ag_recv)
    rt, tr = (rt_send, rt_recv), (tr_send, tr_recv)

    def product(xt):
        block = pl.ds(pl.multiple_of(xt * 128, 128), 128)
        first = lax.dot_general(
            grad_gate[block, :], gu_s[0], ROWS_BY_COLS, preferred_element_type=F32
        )
        return first + lax.dot_general(
            grad_up[block, :], gu_s[1], ROWS_BY_COLS, preferred_element_type=F32
        )

    def product_two(xt):
        block = pl.ds(pl.multiple_of(xt * 128, 128), 128)
        return jnp.dot(hidden[block, :], down_s[...], preferred_element_type=F32)

    scatter_sum(at, product, part, got, rs)
    scaled, inverse = norm(hidden_in[...])
    grad = summed(at, part, got, rs)
    grad_in = cot_full[own_rows(at), :].astype(F32) + norm_back(
        grad, scaled, inverse, par[2:3, :]
    )
    grad_in_out[...] = grad_in
    rows[...] = grad_in.astype(BF)
    gather_rows(at, rows, branch_out, ag, local.at[0])
    sums_out[...] = jnp.zeros_like(sums_out)
    sums_out[0:1, :] = jnp.sum(grad * scaled, axis=0, keepdims=True)
    sums_out[1:2, :] = jnp.sum(grad, axis=0, keepdims=True)
    scatter_sum(at, product_two, part2, got2, rt)
    total = summed(at, part2, got2, rt) + hidden_in[...]
    rows2[...] = total.astype(BF)
    gather_columns(at, rows2, act_out, tr, local.at[1])
    sent(at, got.at[0], rs)
    sent(at, got.at[0], rt)
    settle_all(at, rows, ag)
    settle_all(at, rows2.at[:, pl.ds(0, 256)], tr)


def mlp_back(grad_gate, grad_up, gu_s, hidden, down_s, hidden_in, cot_full, par):
    shape = jax.ShapeDtypeStruct
    return pl.pallas_call(
        mlp_back_kernel,
        out_shape=(
            shape((OWN, D), F32),
            shape((TOK, D), BF),
            shape((TOK, 256), BF),
            shape((8, D), F32),
        ),
        in_specs=[IN_VMEM] * 8,
        out_specs=(IN_VMEM, IN_ANY, IN_ANY, IN_VMEM),
        scratch_shapes=[
            pltpu.VMEM((TOK, D), BF),
            pltpu.VMEM((7, OWN, D), BF),
            pltpu.VMEM((OWN, D), BF),
        ]
        * 2
        + dma_sems(7) * 4
        + [pltpu.SemaphoreType.DMA((2,))],
        compiler_params=params(3),
        name="mlp_back",
    )(grad_gate, grad_up, gu_s, hidden, down_s, hidden_in, cot_full, par)


def input_back_kernel(
    grad_proj, qkv_s, x_full, grad_in, par, out, sums_out,
    part, got, rows, rs_send, rs_recv, tr_send, tr_recv, local,
):
    at = Place()
    greet(group_others(at))
    rs, tr = (rs_send, rs_recv), (tr_send, tr_recv)

    def product(xt):
        block = pl.ds(pl.multiple_of(xt * 128, 128), 128)
        return lax.dot_general(
            grad_proj[block, :], qkv_s[...], ROWS_BY_COLS, preferred_element_type=F32
        )

    scatter_sum(at, product, part, got, rs)
    scaled, inverse = norm(x_full[own_rows(at), :].astype(F32))
    grad = summed(at, part, got, rs)
    total = grad_in[...] + norm_back(grad, scaled, inverse, par[0:1, :])
    rows[...] = total.astype(BF)
    gather_columns(at, rows, out, tr, local.at[0])
    sums_out[...] = jnp.zeros_like(sums_out)
    sums_out[0:1, :] = jnp.sum(grad * scaled, axis=0, keepdims=True)
    sums_out[1:2, :] = jnp.sum(grad, axis=0, keepdims=True)
    sent(at, got.at[0], rs)
    settle_all(at, rows.at[:, pl.ds(0, 256)], tr)


def input_back(grad_proj, qkv_s, x_full, grad_in, par):
    shape = jax.ShapeDtypeStruct
    return pl.pallas_call(
        input_back_kernel,
        out_shape=(shape((TOK, 256), BF), shape((8, D), F32)),
        in_specs=[IN_VMEM] * 5,
        out_specs=(IN_ANY, IN_VMEM),
        scratch_shapes=[
            pltpu.VMEM((TOK, D), BF),
            pltpu.VMEM((7, OWN, D), BF),
            pltpu.VMEM((OWN, D), BF),
        ]
        + dma_sems(7) * 2
        + [pltpu.SemaphoreType.DMA((1,))],
        compiler_params=params(4),
        name="input_back",
    )(grad_proj, qkv_s, x_full, grad_in, par)


def rotary(value, tables, sign):
    width = value.shape[1]
    return (
        value * tables[0]
        + pltpu.roll(value, width - 8, 1) * (sign * tables[1])
        + pltpu.roll(value, 8, 1) * (sign * tables[2])
    )


def head_part(value, head, kind):
    start = head * 3 * HD + kind * HD
    return value[:, start : start + HD]


def allowed(seg_col, seg_row, block, keys):
    start = block * 128
    rows = lax.broadcasted_iota(jnp.int32, (128, keys), 0) + start
    cols = lax.broadcasted_iota(jnp.int32, (128, keys), 1)
    same = seg_col[start : start + 128, :] == seg_row[0:1, :keys]
    return (cols <= rows) & same


def attention_kernel(proj, tables, seg_col, seg_row, qkv_out, att_out, max_out, sum_out):
    scale = 1.0 / math.sqrt(HD)
    for half in range(2):
        cols = pl.ds(half * 384, 384)
        tab = (tables[0], tables[1], tables[2])
        qkv_out[:, cols] = rotary(proj[:, cols], tab, 1.0).astype(BF)
    for block in range(4):
        keys = (block + 1) * 128
        rows = pl.ds(block * 128, 128)
        mask = allowed(seg_col, seg_row, block, keys)
        outs, maxima, totals = [], [], []
        for head in range(HEADS):
            q = head_part(qkv_out[rows, :], head, 0)
            k = head_part(qkv_out[pl.ds(0, keys), :], head, 1)
            v = head_part(qkv_out[pl.ds(0, keys), :], head, 2)
            score = lax.dot_general(q, k, ROWS_BY_COLS, preferred_element_type=F32) * scale
            score = jnp.where(mask, score, -1e30)
            top = jnp.max(score, axis=1, keepdims=True)
            raised = jnp.exp(score - top)
            total = jnp.sum(raised, axis=1, keepdims=True)
            low = (raised / total).astype(BF)
            outs.append(jnp.dot(low, v, preferred_element_type=F32))
            maxima.append(top)
            totals.append(total)
        att_out[rows, :] = jnp.concatenate(outs, axis=1).astype(BF)
        for head in range(HEADS):
            max_out[rows, head : head + 1] = maxima[head]
            sum_out[rows, head : head + 1] = totals[head]


def attention(proj, tables, seg_col, seg_row):
    shape = jax.ShapeDtypeStruct
    return pl.pallas_call(
        attention_kernel,
        out_shape=(
            shape((TOK, WIDE), BF),
            shape((TOK, 256), BF),
            shape((TOK, 128), F32),
            shape((TOK, 128), F32),
        ),
        in_specs=[IN_VMEM] * 4,
        out_specs=(IN_VMEM,) * 4,
        compiler_params=pltpu.CompilerParams(vmem_limit_bytes=VMEM_LIMIT),
        name="attention",
    )(proj, tables, seg_col, seg_row)


def attention_back_kernel(
    qkv, grad_att, tables, seg_col, seg_row, maxima, totals, grad_out, bias_out, pieces
):
    scale = 1.0 / math.sqrt(HD)
    pieces[...] = jnp.zeros_like(pieces)
    for block in range(4):
        keys = (block + 1) * 128
        rows = pl.ds(block * 128, 128)
        upto = pl.ds(0, keys)
        mask = allowed(seg_col, seg_row, block, keys)
        for head in range(HEADS):
            q = head_part(qkv[rows, :], head, 0)
            k = head_part(qkv[upto, :], head, 1)
            v = head_part(qkv[upto, :], head, 2)
            grad = grad_att[rows, :][:, head * HD : (head + 1) * HD]
            score = lax.dot_general(q, k, ROWS_BY_COLS, preferred_element_type=F32) * scale
            score = jnp.where(mask, score, -1e30)
            probs = jnp.exp(score - maxima[rows, head : head + 1]) / totals[rows, head : head + 1]
            grad_probs = lax.dot_general(grad, v, ROWS_BY_COLS, preferred_element_type=F32)
            delta = jnp.sum(probs * grad_probs, axis=1, keepdims=True)
            grad_score = (probs * (grad_probs - delta)).astype(BF)
            pieces[head, 0, rows, :] = (
                jnp.dot(grad_score, k, preferred_element_type=F32) * scale
            )
            pieces[head, 1, upto, :] += (
                lax.dot_general(grad_score, q, OVER_ROWS, preferred_element_type=F32) * scale
            )
            pieces[head, 2, upto, :] += lax.dot_general(
                probs.astype(BF), grad, OVER_ROWS, preferred_element_type=F32
            )
    tab = (tables[0], tables[1], tables[2])
    bias_out[...] = jnp.zeros_like(bias_out)
    for half in range(2):
        parts = [pieces[half * 2 + j // 3, j % 3] for j in range(6)]
        cols = pl.ds(half * 384, 384)
        low = rotary(jnp.concatenate(parts, axis=1), tab, -1.0).astype(BF)
        grad_out[:, cols] = low
        bias_out[0:1, cols] = jnp.sum(low.astype(F32), axis=0, keepdims=True)


def attention_back(qkv, grad_att, tables, seg_col, seg_row, maxima, totals):
    shape = jax.ShapeDtypeStruct
    return pl.pallas_call(
        attention_back_kernel,
        out_shape=(shape((TOK, WIDE), BF), shape((8, WIDE), F32)),
        in_specs=[IN_VMEM] * 7,
        out_specs=(IN_VMEM,) * 2,
        scratch_shapes=[pltpu.VMEM((HEADS, 3, TOK, HD), F32)],
        compiler_params=pltpu.CompilerParams(vmem_limit_bytes=VMEM_LIMIT),
        name="attention_back",
    )(qkv, grad_att, tables, seg_col, seg_row, maxima, totals)


def rotary_tables(segment):
    places = jnp.arange(TOK, dtype=jnp.int32)
    starts_flag = jnp.concatenate([jnp.array([True]), segment[1:] != segment[:-1]])
    starts = lax.cummax(jnp.where(starts_flag, places, 0), axis=0)
    offsets = (places - starts).astype(F32)
    half = ROT // 2
    frequencies = jnp.exp(jnp.arange(half, dtype=F32) * (-2.0 * math.log(10000.0) / ROT))
    angles = offsets[:, None] * frequencies[None, :]
    cosine, sine = jnp.cos(angles), jnp.sin(angles)
    one, zero = jnp.ones((TOK, HD), F32), jnp.zeros((TOK, HD), F32)
    rest = HD - ROT
    keep = jnp.concatenate([cosine, cosine, one[:, :rest]], axis=1)
    fore = jnp.concatenate([-sine, zero[:, : HD - half]], axis=1)
    back = jnp.concatenate([zero[:, :half], sine, zero[:, :rest]], axis=1)
    wide = [jnp.concatenate([t, t, e], axis=1) for t, e in ((keep, one), (fore, zero), (back, zero))]
    return jnp.stack([jnp.concatenate([t, t], axis=1) for t in wide])


def sum_grads_kernel(
    gu_p, qkv_p, down_p, out_p, ln_p, bias_p,
    gu_f, qkv_f, down_f, out_f, small_f,
    gu_a, gu_r, gu_t, gu_c, qkv_a, qkv_r, qkv_t, qkv_c,
    down_a, down_r, down_t, down_c, out_a, out_r, out_t, out_c,
    ln_t, small_t,
    a_send, a_recv, b_send, b_recv, c_send, c_recv, d_send, d_recv, e_send, e_recv,
    g_send, g_recv, h_send, h_recv, local,
):
    at = Place()
    others = [at.replica((at.dp + k) % 16) for k in range(1, 16)]
    greet(group_others(at) + others)
    step_a, step_b, step_c = (a_send, a_recv), (b_send, b_recv), (c_send, c_recv)
    step_d, step_e = (d_send, d_recv), (e_send, e_recv)
    step_g, step_h = (g_send, g_recv), (h_send, h_recv)
    core, q, x = at.core, at.q, at.x
    cq = core * 8 + q

    partial = (gu_p, qkv_p, down_p, out_p)
    accs = (gu_a, qkv_a, down_a, out_a)
    recvs = (gu_r, qkv_r, down_r, out_r)
    slots = (gu_t, qkv_t, down_t, out_t)
    packs = (gu_c, qkv_c, down_c, out_c)
    order = (0, 2, 3, 1)

    def half(k, c):
        if k == 0:
            return gu_p.at[:, :, c]
        if k == 1:
            return qkv_p.at[:, c]
        return partial[k].at[c]

    def chunk(k, p):
        if k == 0:
            return gu_a.at[:, :, p]
        if k == 1:
            return qkv_a.at[:, p]
        return accs[k].at[p]

    def blocks(k):
        if k == 0:
            return [(a, b) for a in range(2) for b in range(4)]
        if k == 1:
            return [(b,) for b in range(4)]
        return [()]

    def full(lead, p):
        return lead + (p,)

    def pack_for(k, xt):
        if k == 0:
            return gu_c.at[:, xt]
        if k == 1:
            return qkv_c.at[xt]
        return packs[k].at[:, pl.ds(pl.multiple_of(xt * 512, 512), 512)]

    def landing(k, xs, p):
        if k == 0:
            return gu_f.at[xs, :, p]
        if k == 1:
            return qkv_f.at[p, :, pl.ds(pl.multiple_of(xs * WIDE, WIDE), WIDE)]
        return (gu_f, qkv_f, down_f, out_f)[k].at[xs, p]

    def piece(k, p):
        if k == 0:
            return gu_f.at[:, :, p]
        if k == 1:
            return qkv_f.at[p]
        return (gu_f, qkv_f, down_f, out_f)[k].at[:, p]

    mine = pl.ds(pl.multiple_of(at.g * 256, 256), 256)
    for j in range(1, 8):
        g = (at.g + j) % 8
        push(
            ln_p.at[:, pl.ds(pl.multiple_of(g * 256, 256), 256)],
            ln_t.at[j - 1],
            step_g,
            j - 1,
            at.group(g),
        )
    first = {}
    for k in order:
        first[k] = push(half(k, 1 - core), recvs[k], step_a, k, at.sibling())
        copy = pltpu.make_async_copy(half(k, core), accs[k], local.at[k])
        copy.start()
        first[k + 4] = copy
    total = ln_p[:, mine] + bias_p[...]
    for j in range(7):
        settle(ln_t.at[j], step_g, j, at.group(at.g)).wait_recv()
        total += ln_t[j]
    small_t[pl.ds(at.dp, 1)] = total[None]
    for j, device in enumerate(others):
        push(small_t.at[at.dp], small_t.at[at.dp], step_h, j, device)
    second = {}
    for k in order:
        first[k].wait_recv()
        first[k + 4].wait()
        for lead in blocks(k):

            def add(p, carry):
                index = full(lead, p)
                accs[k][index] = (accs[k][index].astype(F32) + recvs[k][index].astype(F32)).astype(
                    BF
                )
                return carry

            lax.fori_loop(0, 8, add, 0)
        for m, device in enumerate(chip_others(at)):
            second[k, m] = push(chunk(k, q ^ (m + 1)), slots[k].at[m], step_b, k * 7 + m, device)
    third = {}
    for k in order:
        for m in range(7):
            second[k, m].wait_recv()
        for lead in blocks(k):
            value = accs[k][full(lead, q)].astype(F32)
            for m in range(7):
                value += slots[k][(m,) + lead].astype(F32)
            packs[k][lead + (Ellipsis,)] = value.astype(BF)
        for j in range(1, 4):
            xt = (x + j) % 4
            third[k, j] = push(
                pack_for(k, xt), landing(k, x, cq), step_c, k * 3 + j - 1, at.row(xt)
            )
        copy = pltpu.make_async_copy(pack_for(k, x), landing(k, x, cq), local.at[4 + k])
        copy.start()
        third[k, 0] = copy
    fourth, fifth = {}, {}
    for k in order:
        third[k, 0].wait()
        for j in range(1, 4):
            third[k, j].wait_recv()
        for m, device in enumerate(chip_others(at)):
            fourth[k, m] = push(piece(k, cq), piece(k, cq), step_d, k * 7 + m, device)
        fifth[k, 7] = push(piece(k, cq), piece(k, cq), step_e, k * 8 + 7, at.sibling())
    for k in order:
        for m in range(7):
            fourth[k, m].wait_recv()
            p = core * 8 + (q ^ (m + 1))
            fifth[k, m] = push(piece(k, p), piece(k, p), step_e, k * 8 + m, at.sibling())
    for j in range(15):
        settle(small_t.at[0], step_h, j, at.group(at.g)).wait_recv()
    result = small_t[0]
    for j in range(1, 16):
        result += small_t[j]
    small_f[...] = result
    for k in order:
        first[k].wait_send()
        for m in range(7):
            second[k, m].wait_send()
            fourth[k, m].wait_send()
        for j in range(1, 4):
            third[k, j].wait_send()
        for m in range(8):
            fifth[k, m].wait_send()
            fifth[k, m].wait_recv()
    for j in range(7):
        settle(ln_t.at[j], step_g, j, at.group(at.g)).wait_send()
    for j in range(15):
        settle(small_t.at[0], step_h, j, at.group(at.g)).wait_send()


def sum_grads(gu_p, qkv_p, down_p, out_p, ln_p, bias_p):
    shape = jax.ShapeDtypeStruct
    vmem = pltpu.VMEM
    return pl.pallas_call(
        sum_grads_kernel,
        out_shape=(
            shape((4, 2, 16, 32, WIDE), BF),
            shape((16, 32, 4 * WIDE), BF),
            shape((4, 16, 48, 512), BF),
            shape((4, 16, 16, 512), BF),
            shape((8, 256), F32),
        ),
        in_specs=[IN_ANY] * 4 + [IN_VMEM] * 2,
        out_specs=(IN_ANY,) * 4 + (IN_VMEM,),
        scratch_shapes=[
            vmem((2, 4, 8, 32, WIDE), BF),
            vmem((2, 4, 8, 32, WIDE), BF),
            vmem((7, 2, 4, 32, WIDE), BF),
            vmem((2, 4, 32, WIDE), BF),
            vmem((4, 8, 32, WIDE), BF),
            vmem((4, 8, 32, WIDE), BF),
            vmem((7, 4, 32, WIDE), BF),
            vmem((4, 32, WIDE), BF),
            vmem((8, 48, D), BF),
            vmem((8, 48, D), BF),
            vmem((7, 48, D), BF),
            vmem((48, D), BF),
            vmem((8, 16, D), BF),
            vmem((8, 16, D), BF),
            vmem((7, 16, D), BF),
            vmem((16, D), BF),
            vmem((7, 8, 256), F32),
            vmem((16, 8, 256), F32),
        ]
        + dma_sems(4)
        + dma_sems(28)
        + dma_sems(12)
        + dma_sems(28)
        + dma_sems(32)
        + dma_sems(7)
        + dma_sems(15)
        + [pltpu.SemaphoreType.DMA((8,))],
        compiler_params=params(5),
        name="sum_grads",
    )(gu_p, qkv_p, down_p, out_p, ln_p, bias_p)


def matmul(a, b):
    return jnp.dot(a, b, preferred_element_type=F32)


def matmul_t(a, b):
    return lax.dot_general(a, b, ROWS_BY_COLS, preferred_element_type=F32)


def outer(a, b):
    return lax.dot_general(a, b, OVER_ROWS, preferred_element_type=F32).astype(BF)


def on_device(
    block_in, segments, ln1_gain, ln1_bias, qkv_weight, qkv_bias, out_weight,
    ln2_gain, ln2_bias, gate_up_weight, down_weight, cotangent,
):
    zero = jnp.zeros((256,), F32)
    par = jnp.stack([ln1_gain, ln1_bias, ln2_gain, ln2_bias, zero, zero, zero, zero])
    gate_up = jnp.transpose(gate_up_weight, (1, 0, 2))
    x_full, cot_full, par, qkv_s, out_s, gu_s, down_s = gather_inputs(
        block_in, cotangent, par, qkv_weight, out_weight, gate_up, down_weight
    )
    tables = rotary_tables(segments)
    seg_col = segments[:, None]
    seg_row = segments[None, :]
    scaled, _ = norm(x_full.astype(F32))
    normed = (scaled * par[0:1] + par[1:2]).astype(BF)
    proj = matmul(normed, qkv_s) + qkv_bias[None, :]
    qkv, attended, maxima, totals = attention(proj, tables, seg_col, seg_row)
    hidden_in, normed_two = attend_out(attended, out_s, x_full, par)
    gate = matmul(normed_two, gu_s[0])
    up = matmul(normed_two, gu_s[1])
    sig = jax.nn.sigmoid(gate)
    lane = lax.broadcasted_iota(jnp.int32, (1, WIDE), 1)
    kept = (lane >= 128) | (lax.axis_index("row") < 2)
    act = gate * sig
    hidden = jnp.where(kept, act * up, 0.0).astype(BF)
    grad_hidden = jnp.where(kept, matmul_t(cot_full, down_s), 0.0)
    grad_gate = (grad_hidden * up * (sig * (1.0 + gate * (1.0 - sig)))).astype(BF)
    grad_up = (grad_hidden * act).astype(BF)
    grad_in, branch, activations, sums_two = mlp_back(
        grad_gate, grad_up, gu_s, hidden, down_s, hidden_in, cot_full, par
    )
    grad_att = matmul_t(branch, out_s).astype(BF)
    grad_proj, bias_sums = attention_back(
        qkv, grad_att, tables, seg_col, seg_row, maxima, totals
    )
    input_grad, sums_one = input_back(grad_proj, qkv_s, x_full, grad_in, par)
    gu_p = jnp.stack([outer(normed_two, grad_gate), outer(normed_two, grad_up)])
    qkv_p = outer(normed, grad_proj)
    down_p = outer(hidden, cot_full)
    out_p = outer(attended, branch)
    ln_p = jnp.concatenate([sums_one[0:2], sums_two[0:2], jnp.zeros((4, D), F32)])
    bias_p = jnp.concatenate(
        [jnp.zeros((4, 256), F32), bias_sums[0].reshape(3, 256), jnp.zeros((1, 256), F32)]
    )
    gu_f, qkv_f, down_f, out_f, small = sum_grads(
        gu_p.reshape(2, 4, 2, 8, 32, WIDE),
        qkv_p.reshape(4, 2, 8, 32, WIDE),
        down_p.reshape(2, 8, 48, D),
        out_p.reshape(2, 8, 16, D),
        ln_p,
        bias_p,
    )
    gu_f = gu_f.reshape(4, 2, 512, WIDE)
    gu_f = jnp.concatenate([gu_f[0], gu_f[1], gu_f[2, :, :, 128:], gu_f[3, :, :, 128:]], axis=2)
    gu_grad = jnp.transpose(gu_f, (1, 0, 2)).astype(F32)
    down_f = down_f.reshape(4, WIDE, 512)
    down_grad = jnp.concatenate(
        [down_f[0], down_f[1], down_f[2, 128:], down_f[3, 128:]], axis=0
    ).astype(F32)
    return (
        activations,
        input_grad,
        small[0],
        small[1],
        qkv_f.reshape(512, 4 * WIDE).astype(F32),
        small[4:7].reshape(WIDE),
        out_f.reshape(1024, 512).astype(F32),
        small[2],
        small[3],
        gu_grad,
        down_grad,
    )


def solution(mesh):
    wide = P("dp", ("row", "col"))
    vector = P(("row", "col"))
    return jax.shard_map(
        on_device,
        mesh=mesh,
        in_specs=(
            wide, P("dp"), vector, vector, P("row", "col"), P(("col", "row")), P("col", "row"),
            vector, vector, P("row", None, "col"), P("col", "row"), wide,
        ),
        out_specs=(
            wide, wide, vector, vector, P("row", "col"), P(("col", "row")), P("col", "row"),
            vector, vector, P("row", None, "col"), P("col", "row"),
        ),
        check_vma=False,
    )
```

```python
import math

import jax
import jax.numpy as jnp
from jax import lax
from jax.experimental import pallas as pl
from jax.experimental.pallas import tpu as pltpu
from jax.sharding import PartitionSpec as P

D = 2048
HD = 64
ROT = 16
HEADS = 4
TOK = 512
OWN = 64
WIDE = 768
EPSILON = 1e-05
BF = jnp.bfloat16
F32 = jnp.float32
MESH = pl.DeviceIdType.MESH
VMEM_LIMIT = 60 * 2**20
ROWS_BY_COLS = (((1,), (1,)), ((), ()))
OVER_ROWS = (((0,), (0,)), ((), ()))

IN_VMEM = pl.BlockSpec(memory_space=pltpu.VMEM)
IN_ANY = pl.BlockSpec(memory_space=pl.ANY)


class Place:
    def __init__(self):
        self.dp = lax.axis_index("dp")
        self.x = lax.axis_index("row")
        self.zh = lax.axis_index("col")
        self.y = self.dp // 4
        self.zl = (self.dp // 2) % 2
        self.core = self.dp % 2
        self.q = self.dp // 2
        self.g = self.x * 2 + self.zh

    def group(self, g):
        return (self.dp, g // 2, g % 2)

    def row(self, x):
        return (self.dp, x, self.zh)

    def chip(self, q):
        return (q * 2 + self.core, self.x, self.zh)

    def mate(self):
        return (self.dp, self.x, 1 - self.zh)

    def near_replicas(self):
        def chip(y, zl):
            return ((y * 2 + zl) * 2 + self.core, self.x, self.zh)

        return [
            chip((self.y + 1) % 4, self.zl),
            chip((self.y + 3) % 4, self.zl),
            chip(self.y, 1 - self.zl),
            self.sibling(),
        ]

    def sibling(self):
        return (self.q * 2 + 1 - self.core, self.x, self.zh)

    def replica(self, dp):
        return (dp, self.x, self.zh)


def greet(partners):
    barrier = pltpu.get_barrier_semaphore()
    for partner in partners:
        pl.semaphore_signal(barrier, inc=1, device_id=partner, device_id_type=MESH)
    pl.semaphore_wait(barrier, len(partners))


def push(src, dst, sems, index, device):
    send, recv = sems
    copy = pltpu.make_async_remote_copy(
        src_ref=src,
        dst_ref=dst,
        send_sem=send.at[index],
        recv_sem=recv.at[index],
        device_id=device,
        device_id_type=MESH,
    )
    copy.start()
    return copy


def group_others(at):
    return [at.group((at.g + k) % 8) for k in range(1, 8)]


def chip_others(at):
    return [at.chip(at.q ^ k) for k in range(1, 8)]


def dma_sems(amount):
    return [pltpu.SemaphoreType.DMA((amount,)), pltpu.SemaphoreType.DMA((amount,))]


def params(collective_id):
    return pltpu.CompilerParams(
        collective_id=collective_id, has_side_effects=True, vmem_limit_bytes=VMEM_LIMIT
    )


def tile_start(x):
    return 5 * x + jnp.minimum(x, 1)


def settle(ref, sems, index, device):
    send, recv = sems
    return pltpu.make_async_remote_copy(
        src_ref=ref,
        dst_ref=ref,
        send_sem=send.at[index],
        recv_sem=recv.at[index],
        device_id=device,
        device_id_type=MESH,
    )


class Gather:
    def __init__(self, pos, pair, device, whole, half, sems, base=0, on_piece=None):
        self.pos, self.pair, self.device = pos, pair, device
        self.whole, self.half, self.sems, self.base = whole, half, sems, base
        self.right, self.left, self.far = (pos + 1) % 4, (pos + 3) % 4, (pos + 2) % 4
        self.on_piece = on_piece or (lambda r, p, k: None)
        self.copies = {}

    def push(self, index, ref, device, src=None):
        copy = push(ref if src is None else src, ref, self.sems, self.base + index, device)
        self.copies[index] = copy

    def arrived(self, index, ref):
        settle(ref, self.sems, self.base + index, self.device(self.pos, self.pair)).wait_recv()

    def start(self, own=None):
        ref = self.whole(self.pos, self.pair)
        self.push(1, ref, self.device(self.right, self.pair), own)
        self.push(2, ref, self.device(self.left, self.pair), own)
        self.push(0, ref, self.device(self.pos, 1 - self.pair), own)
        self.on_piece(self.pos, self.pair, 0)

    def forward(self, first, pair, slot):
        self.arrived(first, self.whole(self.left, pair))
        self.push(first + 2, self.half(self.left, pair, 0), self.device(self.right, self.pair))
        self.on_piece(self.left, pair, slot)
        self.arrived(first + 1, self.whole(self.right, pair))
        self.push(first + 3, self.half(self.right, pair, 1), self.device(self.left, self.pair))
        self.on_piece(self.right, pair, slot + 1)

    def forward_ring(self):
        self.forward(1, self.pair, 1)

    def spread_pair(self):
        ref = self.whole(self.pos, 1 - self.pair)
        self.arrived(0, ref)
        self.push(5, ref, self.device(self.right, self.pair))
        self.push(6, ref, self.device(self.left, self.pair))
        self.on_piece(self.pos, 1 - self.pair, 3)

    def forward_pair(self):
        self.forward(5, 1 - self.pair, 4)

    def finish(self):
        for first, pair, slot in ((3, self.pair, 6), (7, 1 - self.pair, 7)):
            self.arrived(first, self.half(self.far, pair, 0))
            self.arrived(first + 1, self.half(self.far, pair, 1))
            self.on_piece(self.far, pair, slot)

    def drain(self):
        for copy in self.copies.values():
            copy.wait_send()


class RowScatter:
    def __init__(self, at, part, half_in, full_in, pair_in, pair_out, sems, base=0):
        self.at, self.part, self.half_in, self.full_in = at, part, half_in, full_in
        self.pair_in, self.pair_out, self.sems, self.base = pair_in, pair_out, sems, base
        self.right, self.left = (at.x + 1) % 4, (at.x + 3) % 4
        self.planes = (1 - at.zh, at.zh)
        self.copies = []

    def rows(self, x, plane, half=None):
        start = (x * 2 + plane) * OWN
        if half is None:
            return pl.ds(pl.multiple_of(start, OWN), OWN)
        return pl.ds(pl.multiple_of(start + half * (OWN // 2), OWN // 2), OWN // 2)

    def push(self, index, src, dst, device):
        self.copies.append(push(src, dst, self.sems, self.base + index, device))

    def arrived(self, index, ref):
        settle(ref, self.sems, self.base + index, self.at.row(self.at.x)).wait_recv()

    def first(self):
        far = (self.at.x + 2) % 4
        for role, plane in enumerate(self.planes):
            for side, x in enumerate((self.right, self.left)):
                self.push(
                    role * 4 + side,
                    self.part.at[self.rows(far, plane, side)],
                    self.half_in.at[role, side],
                    self.at.row(x),
                )

    def second(self, role):
        plane = self.planes[role]
        for side, x in enumerate((self.right, self.left)):
            box = self.half_in.at[role, side]
            self.arrived(role * 4 + side, box)
            rows = self.rows(x, plane, side)
            self.part[rows, :] = (self.part[rows, :].astype(F32) + box[...].astype(F32)).astype(BF)
            self.push(
                role * 4 + 2 + side,
                self.part.at[self.rows(x, plane)],
                self.full_in.at[role, side],
                self.at.row(x),
            )

    def own(self, role):
        for side in range(2):
            self.arrived(role * 4 + 2 + side, self.full_in.at[role, side])
        total = self.part[self.rows(self.at.x, self.planes[role]), :].astype(F32)
        return total + self.full_in[role, 0].astype(F32) + self.full_in[role, 1].astype(F32)

    def third(self):
        self.pair_out[...] = self.own(0).astype(BF)
        self.push(8, self.pair_out, self.pair_in, self.at.mate())

    def fourth(self):
        total = self.own(1)
        self.arrived(8, self.pair_in)
        return total + self.pair_in[...].astype(F32)

    def drain(self):
        for copy in self.copies:
            copy.wait_send()


def scatter_scratch():
    return [
        pltpu.VMEM((TOK, D), BF),
        pltpu.VMEM((2, 2, OWN // 2, D), BF),
        pltpu.VMEM((2, 2, OWN, D), BF),
        pltpu.VMEM((OWN, D), BF),
        pltpu.VMEM((OWN, D), BF),
    ] + dma_sems(9)


def row_gather(at, ref, sems, base=0):
    def whole(x, plane):
        return ref.at[pl.ds(pl.multiple_of((x * 2 + plane) * OWN, OWN), OWN)]

    def half(x, plane, side):
        start = (x * 2 + plane) * OWN + side * (OWN // 2)
        return ref.at[pl.ds(pl.multiple_of(start, OWN // 2), OWN // 2)]

    return Gather(at.x, at.zh, lambda x, plane: (at.dp, x, plane), whole, half, sems, base)


def column_gather(at, ref, sems, base=0):
    def columns(x, plane):
        return pl.ds(pl.multiple_of((x * 2 + plane) * 256, 256), 256)

    def whole(x, plane):
        return ref.at[:, columns(x, plane)]

    def half(x, plane, side):
        return ref.at[pl.ds(side * 256, 256), columns(x, plane)]

    return Gather(at.x, at.zh, lambda x, plane: (at.dp, x, plane), whole, half, sems, base)


def front_kernel(
    x_in, cot_in, par_in, bias_in, seg_col, seg_row, qkv_w, out_w, gu_w, down_w,
    cot_out, par_out, normed_out, qkv_out, att_out, max_out, sum_out, tab_out, own_out,
    hidden_out, normed2_out, qkv_s_out, out_s_out, gu_s, down_s,
    x_v, normed, par, proj, tables, qkv_s, out_s, normed2, rows,
    part, half_in, full_in, pair_in, pair_out, rs_send, rs_recv,
    par_send, par_recv, act_send, act_recv, a_send, a_recv, dp_send, dp_recv, core_send, core_recv,
    local,
):
    at = Place()
    greet(group_others(at) + at.near_replicas())
    dp, x, core = at.dp, at.x, at.core
    act, step_a, step_dp = (act_send, act_recv), (a_send, a_recv), (dp_send, dp_recv)
    step_core, step_par = (core_send, core_recv), (par_send, par_recv)
    slabs = (qkv_s, out_s, gu_s, down_s)

    def source(k, xt):
        if k == 0:
            return qkv_w.at[pl.ds(dp * 32, 32), pl.ds(pl.multiple_of(xt * WIDE, WIDE), WIDE)]
        if k == 1:
            return out_w.at[pl.ds(xt * 256 + dp * 16, 16), :]
        start = pl.multiple_of(tile_start(xt) * 128, 128)
        if k == 2:
            return gu_w.at[:, pl.ds(dp * 32, 32), pl.ds(start, WIDE)]
        return down_w.at[pl.ds(start + dp * 48, 48), :]

    def landing(k, xs, p):
        if k == 0:
            return qkv_s.at[xs, p]
        if k == 2:
            return gu_s.at[:, xs, p]
        return slabs[k].at[p, :, pl.ds(pl.multiple_of(xs * 512, 512), 512)]

    def replica(y, zl):
        return (y * 2 + zl) * 2 + core

    def whole(k):
        def of(y, zl):
            p = replica(y, zl)
            if k == 0:
                return qkv_s.at[:, p]
            if k == 2:
                return gu_s.at[:, :, p]
            return slabs[k].at[p]

        return of

    def half(k):
        def of(y, zl, side):
            p = replica(y, zl)
            if k == 0:
                return qkv_s.at[pl.ds(side * 2, 2), p]
            if k == 2:
                return gu_s.at[side, :, p]
            return slabs[k].at[p, :, pl.ds(side * 1024, 1024)]

        return of

    core_copies = []

    def to_sibling(k):
        def on_piece(y, zl, slot):
            ref = whole(k)(y, zl)
            core_copies.append(push(ref, ref, step_core, k * 8 + slot, at.sibling()))

        return on_piece

    first = {}

    def send_rows(k):
        for j in (2, 1, 3):
            xt = (x + j) % 4
            first[k, j] = push(
                source(k, xt), landing(k, x, dp), step_a, k * 3 + j - 1, at.row(xt)
            )
        first[k, 0] = pltpu.make_async_copy(source(k, x), landing(k, x, dp), local.at[k])
        first[k, 0].start()

    weights = [
        Gather(
            at.y, at.zl, lambda y, zl: (replica(y, zl), x, at.zh), whole(k), half(k), step_dp, k * 9,
            to_sibling(k),
        )
        for k in range(4)
    ]
    w_qkv, w_out, w_gu, w_down = weights

    def begin(k):
        first[k, 0].wait()
        for j in range(1, 4):
            first[k, j].wait_recv()
        weights[k].start()

    def from_sibling(k):
        ref = whole(k)(at.y, at.zl)
        for slot in range(8):
            settle(ref, step_core, k * 8 + slot, at.sibling()).wait_recv()

    slot = pl.ds(pl.multiple_of(at.g * 256, 256), 256)
    send_rows(0)
    gx = column_gather(at, x_v, act, 0)
    gx.start(x_in)
    par_copies = []
    for j, device in enumerate(group_others(at)):
        par_copies.append(push(par_in, par.at[:, slot], step_par, j, device))
    own = [
        pltpu.make_async_copy(x_in, x_v.at[:, slot], local.at[4]),
        pltpu.make_async_copy(par_in, par.at[:, slot], local.at[5]),
        pltpu.make_async_copy(cot_in, cot_out.at[:, slot], local.at[6]),
    ]
    for copy in own:
        copy.start()
    send_rows(1)
    send_rows(2)
    send_rows(3)
    begin(0)
    make_tables(seg_col, seg_row, tables)
    gx.forward_ring()
    gx.spread_pair()
    w_qkv.forward_ring()
    w_qkv.spread_pair()
    begin(1)
    gx.forward_pair()
    w_qkv.forward_pair()
    w_out.forward_ring()
    w_out.spread_pair()
    gx.finish()
    gcot = column_gather(at, cot_out, act, 9)
    gcot.start(cot_in)
    begin(2)
    for copy in own:
        copy.wait()
    for copy in par_copies:
        copy.wait_recv()

    def norm_rows(i, carry):
        block = pl.ds(pl.multiple_of(i * 32, 32), 32)
        scaled, _ = norm(x_v[block, :].astype(F32))
        normed[block, :] = (scaled * par[0:1, :] + par[1:2, :]).astype(BF)
        return carry

    lax.fori_loop(0, TOK // 32, norm_rows, 0)
    w_qkv.finish()
    w_out.forward_pair()
    from_sibling(0)
    outgoing = []

    def put(src, dst, index):
        copy = pltpu.make_async_copy(src, dst, local.at[index])
        copy.start()
        outgoing.append(copy)

    put(normed, normed_out, 7)
    put(qkv_s, qkv_s_out, 8)
    put(x_v.at[own_rows(at)], own_out, 9)
    put(par, par_out, 10)
    between = [
        lambda: (gcot.forward_ring(), w_out.finish()),
        lambda: (gcot.spread_pair(), w_gu.forward_ring(), w_gu.spread_pair()),
        lambda: (begin(3),),
        lambda: (gcot.forward_pair(), w_gu.forward_pair()),
        lambda: (w_down.forward_ring(), w_down.spread_pair()),
        lambda: (gcot.finish(), w_gu.finish()),
        lambda: (from_sibling(1),),
    ]
    for n in range(3):
        cols = pl.ds(n * 256, 256)
        weight = qkv_s[:, :, :, cols].reshape(D, 256)
        proj[:, cols] = (
            jnp.dot(normed[...], weight, preferred_element_type=F32) + bias_in[:, cols]
        )
        between[n]()
    attend(proj, tables, seg_col, seg_row, qkv_out, att_out, max_out, sum_out, between[3:])
    put(out_s, out_s_out, 11)
    put(tables, tab_out, 12)
    rs = RowScatter(at, part, half_in, full_in, pair_in, pair_out, (rs_send, rs_recv))
    weight = out_s[...].reshape(256, D)

    def product(xt):
        block = pl.ds(pl.multiple_of(xt * 128, 128), 128)
        part[block, :] = jnp.dot(att_out[block, :], weight, preferred_element_type=F32).astype(BF)

    product((x + 2) % 4)
    rs.first()
    product((x + 1) % 4)
    product((x + 3) % 4)
    rs.second(0)
    rs.second(1)
    product(x)
    w_down.forward_pair()
    rs.third()
    hidden_in = rs.fourth() + x_v[own_rows(at), :].astype(F32)
    hidden_out[...] = hidden_in
    scaled, _ = norm(hidden_in)
    rows[...] = (scaled * par[2:3, :] + par[3:4, :]).astype(BF)
    normed2[own_rows(at), :] = rows[...]
    gn = row_gather(at, normed2, act, 18)
    gn.start(rows)
    w_down.finish()
    gn.forward_ring()
    gn.spread_pair()
    gn.forward_pair()
    from_sibling(2)
    from_sibling(3)
    gn.finish()
    put(normed2, normed2_out, 13)
    for k in range(4):
        for j in range(1, 4):
            first[k, j].wait_send()
        weights[k].drain()
    for copy in core_copies + par_copies:
        copy.wait_send()
    for program in (gx, gcot, gn, rs):
        program.drain()
    for copy in outgoing:
        copy.wait()


def front(x_in, cot_in, par_in, bias_in, seg_col, seg_row, qkv_w, out_w, gu_w, down_w):
    shape = jax.ShapeDtypeStruct
    vmem = pltpu.VMEM
    return pl.pallas_call(
        front_kernel,
        out_shape=(
            shape((TOK, D), BF),
            shape((8, D), F32),
            shape((TOK, D), BF),
            shape((TOK, WIDE), BF),
            shape((TOK, 256), BF),
            shape((TOK, 128), F32),
            shape((TOK, 128), F32),
            shape((3, TOK, 384), F32),
            shape((OWN, D), BF),
            shape((OWN, D), F32),
            shape((TOK, D), BF),
            shape((4, 16, 32, WIDE), BF),
            shape((16, 16, D), BF),
            shape((2, 4, 16, 32, WIDE), BF),
            shape((16, 48, D), BF),
        ),
        in_specs=[IN_ANY] * 3 + [IN_VMEM] * 3 + [IN_ANY] * 4,
        out_specs=(IN_ANY,) * 3 + (IN_VMEM,) * 4 + (IN_ANY,) * 2 + (IN_VMEM,) + (IN_ANY,) * 5,
        scratch_shapes=[
            vmem((TOK, D), BF),
            vmem((TOK, D), BF),
            vmem((8, D), F32),
            vmem((TOK, WIDE), F32),
            vmem((3, TOK, 384), F32),
            vmem((4, 16, 32, WIDE), BF),
            vmem((16, 16, D), BF),
            vmem((TOK, D), BF),
            vmem((OWN, D), BF),
        ]
        + scatter_scratch()
        + dma_sems(7)
        + dma_sems(27)
        + dma_sems(12)
        + dma_sems(36)
        + dma_sems(32)
        + [pltpu.SemaphoreType.DMA((14,))],
        compiler_params=params(1),
        name="front",
    )(x_in, cot_in, par_in, bias_in, seg_col, seg_row, qkv_w, out_w, gu_w, down_w)


def scatter_sum(at, product, part, got, sems):
    def step(i, carry):
        xt = (at.x + i + 1) % 4
        part[pl.ds(pl.multiple_of(xt * 128, 128), 128), :] = product(xt).astype(BF)
        for half in range(2):
            g = xt * 2 + half
            index = (g - at.g + 15) % 8

            @pl.when(index < 7)
            def _():
                push(
                    part.at[pl.ds(pl.multiple_of(g * OWN, OWN), OWN)],
                    got.at[index],
                    sems,
                    index,
                    at.group(g),
                )

        return carry

    lax.fori_loop(0, 4, step, 0)


def own_rows(at):
    return pl.ds(pl.multiple_of(at.g * OWN, OWN), OWN)


def summed(at, part, got, sems):
    total = part[own_rows(at), :].astype(F32)
    for k in range(7):
        settle(got.at[k], sems, k, at.group(at.g)).wait_recv()
        total += got[k].astype(F32)
    return total


def sent(at, buffer, sems, amount=7):
    for k in range(amount):
        settle(buffer, sems, k, at.group(at.g)).wait_send()


def gather_rows(at, rows, full, sems, local):
    copy = pltpu.make_async_copy(rows, full.at[own_rows(at)], local)
    copy.start()
    for k in range(1, 8):
        push(rows, full.at[own_rows(at)], sems, k - 1, at.group((at.g + k) % 8))
    copy.wait()


def gather_columns(at, rows, full, sems, local):
    def columns(g):
        return rows.at[:, pl.ds(pl.multiple_of(g * 256, 256), 256)]

    copy = pltpu.make_async_copy(columns(at.g), full.at[own_rows(at)], local)
    copy.start()
    for k in range(1, 8):
        g = (at.g + k) % 8
        push(columns(g), full.at[own_rows(at)], sems, k - 1, at.group(g))
    copy.wait()


def settle_all(at, piece, sems, amount=7):
    for k in range(amount):
        copy = settle(piece, sems, k, at.group(at.g))
        copy.wait_send()
        copy.wait_recv()


def norm(value):
    mean = jnp.mean(value, axis=1, keepdims=True)
    square = jnp.mean(value * value, axis=1, keepdims=True)
    inverse = lax.rsqrt(square - mean * mean + EPSILON)
    return (value - mean) * inverse, inverse


def norm_back(grad, scaled, inverse, gain):
    inner = grad * gain
    mean = jnp.mean(inner, axis=1, keepdims=True)
    along = jnp.mean(inner * scaled, axis=1, keepdims=True)
    return inverse * (inner - mean - scaled * along)


def mlp_back_kernel(
    grad_gate, grad_up, gu_s, hidden, down_s, hidden_in, cot_full, par,
    grad_in_out, branch_out, act_out, sums_out,
    part, got, rows, part2, got2, rows2,
    rs_send, rs_recv, ag_send, ag_recv, rt_send, rt_recv, tr_send, tr_recv, local,
):
    at = Place()
    greet(group_others(at))
    rs, ag = (rs_send, rs_recv), (ag_send, ag_recv)
    rt, tr = (rt_send, rt_recv), (tr_send, tr_recv)

    def product(xt):
        block = pl.ds(pl.multiple_of(xt * 128, 128), 128)
        first = lax.dot_general(
            grad_gate[block, :], gu_s[0], ROWS_BY_COLS, preferred_element_type=F32
        )
        return first + lax.dot_general(
            grad_up[block, :], gu_s[1], ROWS_BY_COLS, preferred_element_type=F32
        )

    def product_two(xt):
        block = pl.ds(pl.multiple_of(xt * 128, 128), 128)
        return jnp.dot(hidden[block, :], down_s[...], preferred_element_type=F32)

    scatter_sum(at, product, part, got, rs)
    scaled, inverse = norm(hidden_in[...])
    grad = summed(at, part, got, rs)
    grad_in = cot_full[own_rows(at), :].astype(F32) + norm_back(
        grad, scaled, inverse, par[2:3, :]
    )
    grad_in_out[...] = grad_in
    rows[...] = grad_in.astype(BF)
    gather_rows(at, rows, branch_out, ag, local.at[0])
    sums_out[...] = jnp.zeros_like(sums_out)
    sums_out[0:1, :] = jnp.sum(grad * scaled, axis=0, keepdims=True)
    sums_out[1:2, :] = jnp.sum(grad, axis=0, keepdims=True)
    scatter_sum(at, product_two, part2, got2, rt)
    total = summed(at, part2, got2, rt) + hidden_in[...]
    rows2[...] = total.astype(BF)
    gather_columns(at, rows2, act_out, tr, local.at[1])
    sent(at, got.at[0], rs)
    sent(at, got.at[0], rt)
    settle_all(at, rows, ag)
    settle_all(at, rows2.at[:, pl.ds(0, 256)], tr)


def mlp_back(grad_gate, grad_up, gu_s, hidden, down_s, hidden_in, cot_full, par):
    shape = jax.ShapeDtypeStruct
    return pl.pallas_call(
        mlp_back_kernel,
        out_shape=(
            shape((OWN, D), F32),
            shape((TOK, D), BF),
            shape((TOK, 256), BF),
            shape((8, D), F32),
        ),
        in_specs=[IN_VMEM] * 8,
        out_specs=(IN_VMEM, IN_ANY, IN_ANY, IN_VMEM),
        scratch_shapes=[
            pltpu.VMEM((TOK, D), BF),
            pltpu.VMEM((7, OWN, D), BF),
            pltpu.VMEM((OWN, D), BF),
        ]
        * 2
        + dma_sems(7) * 4
        + [pltpu.SemaphoreType.DMA((2,))],
        compiler_params=params(3),
        name="mlp_back",
    )(grad_gate, grad_up, gu_s, hidden, down_s, hidden_in, cot_full, par)


def input_back_kernel(
    grad_proj, qkv_s, x_own, grad_in, par, out, sums_out,
    part, got, rows, rs_send, rs_recv, tr_send, tr_recv, local,
):
    at = Place()
    greet(group_others(at))
    rs, tr = (rs_send, rs_recv), (tr_send, tr_recv)

    def product(xt):
        block = pl.ds(pl.multiple_of(xt * 128, 128), 128)
        return lax.dot_general(
            grad_proj[block, :], qkv_s[...], ROWS_BY_COLS, preferred_element_type=F32
        )

    scatter_sum(at, product, part, got, rs)
    scaled, inverse = norm(x_own[...].astype(F32))
    grad = summed(at, part, got, rs)
    total = grad_in[...] + norm_back(grad, scaled, inverse, par[0:1, :])
    rows[...] = total.astype(BF)
    gather_columns(at, rows, out, tr, local.at[0])
    sums_out[...] = jnp.zeros_like(sums_out)
    sums_out[0:1, :] = jnp.sum(grad * scaled, axis=0, keepdims=True)
    sums_out[1:2, :] = jnp.sum(grad, axis=0, keepdims=True)
    sent(at, got.at[0], rs)
    settle_all(at, rows.at[:, pl.ds(0, 256)], tr)


def input_back(grad_proj, qkv_s, x_own, grad_in, par):
    shape = jax.ShapeDtypeStruct
    return pl.pallas_call(
        input_back_kernel,
        out_shape=(shape((TOK, 256), BF), shape((8, D), F32)),
        in_specs=[IN_VMEM] * 5,
        out_specs=(IN_ANY, IN_VMEM),
        scratch_shapes=[
            pltpu.VMEM((TOK, D), BF),
            pltpu.VMEM((7, OWN, D), BF),
            pltpu.VMEM((OWN, D), BF),
        ]
        + dma_sems(7) * 2
        + [pltpu.SemaphoreType.DMA((1,))],
        compiler_params=params(4),
        name="input_back",
    )(grad_proj, qkv_s, x_own, grad_in, par)


def rotary(value, tables, sign):
    width = value.shape[1]
    return (
        value * tables[0]
        + pltpu.roll(value, width - 8, 1) * (sign * tables[1])
        + pltpu.roll(value, 8, 1) * (sign * tables[2])
    )


def make_tables(seg_col, seg_row, tables):
    half = ROT // 2
    for block in range(4):
        rows = pl.ds(block * 128, 128)
        places = lax.broadcasted_iota(jnp.int32, (128, 128), 0) + block * 128
        before = jnp.where(seg_row[0:1, :] < seg_col[rows, :], 1.0, 0.0)
        starts = jnp.sum(before, axis=1, keepdims=True)
        offsets = places.astype(F32) - starts
        lane = lax.broadcasted_iota(jnp.int32, (128, 128), 1)
        entry = lane % HD
        power = (entry % half).astype(F32) * (-2.0 * math.log(10000.0) / ROT)
        angles = offsets * jnp.exp(power)
        cosine, sine = jnp.cos(angles), jnp.sin(angles)
        keep = jnp.where(entry < ROT, cosine, 1.0)
        fore = jnp.where(entry < half, -sine, 0.0)
        back = jnp.where((entry >= half) & (entry < ROT), sine, 0.0)
        for j, (table, rest) in enumerate(((keep, 1.0), (fore, 0.0), (back, 0.0))):
            low = lane < HD
            tables[j, rows, 0:128] = table
            tables[j, rows, 128:256] = jnp.where(low, rest, table)
            tables[j, rows, 256:384] = jnp.where(low, table, rest)


def head_part(value, head, kind):
    start = head * 3 * HD + kind * HD
    return value[:, start : start + HD]


def allowed(seg_col, seg_row, block, keys):
    start = block * 128
    rows = lax.broadcasted_iota(jnp.int32, (128, keys), 0) + start
    cols = lax.broadcasted_iota(jnp.int32, (128, keys), 1)
    same = seg_col[start : start + 128, :] == seg_row[0:1, :keys]
    return (cols <= rows) & same


def attend(proj, tables, seg_col, seg_row, qkv_out, att_out, max_out, sum_out, between):
    scale = 1.0 / math.sqrt(HD)
    for half in range(2):
        cols = pl.ds(half * 384, 384)
        tab = (tables[0], tables[1], tables[2])
        qkv_out[:, cols] = rotary(proj[:, cols], tab, 1.0).astype(BF)
    for block in range(4):
        keys = (block + 1) * 128
        rows = pl.ds(block * 128, 128)
        mask = allowed(seg_col, seg_row, block, keys)
        outs, maxima, totals = [], [], []
        for head in range(HEADS):
            q = head_part(qkv_out[rows, :], head, 0)
            k = head_part(qkv_out[pl.ds(0, keys), :], head, 1)
            v = head_part(qkv_out[pl.ds(0, keys), :], head, 2)
            score = lax.dot_general(q, k, ROWS_BY_COLS, preferred_element_type=F32) * scale
            score = jnp.where(mask, score, -1e30)
            top = jnp.max(score, axis=1, keepdims=True)
            raised = jnp.exp(score - top)
            total = jnp.sum(raised, axis=1, keepdims=True)
            low = (raised / total).astype(BF)
            outs.append(jnp.dot(low, v, preferred_element_type=F32))
            maxima.append(top)
            totals.append(total)
        att_out[rows, :] = jnp.concatenate(outs, axis=1).astype(BF)
        for head in range(HEADS):
            max_out[rows, head : head + 1] = maxima[head]
            sum_out[rows, head : head + 1] = totals[head]
        if block < len(between):
            between[block]()


def attention_back_kernel(
    qkv, grad_att, tables, seg_col, seg_row, maxima, totals, grad_out, bias_out, pieces
):
    scale = 1.0 / math.sqrt(HD)
    pieces[...] = jnp.zeros_like(pieces)
    for block in range(4):
        keys = (block + 1) * 128
        rows = pl.ds(block * 128, 128)
        upto = pl.ds(0, keys)
        mask = allowed(seg_col, seg_row, block, keys)
        for head in range(HEADS):
            q = head_part(qkv[rows, :], head, 0)
            k = head_part(qkv[upto, :], head, 1)
            v = head_part(qkv[upto, :], head, 2)
            grad = grad_att[rows, :][:, head * HD : (head + 1) * HD]
            score = lax.dot_general(q, k, ROWS_BY_COLS, preferred_element_type=F32) * scale
            score = jnp.where(mask, score, -1e30)
            probs = jnp.exp(score - maxima[rows, head : head + 1]) / totals[rows, head : head + 1]
            grad_probs = lax.dot_general(grad, v, ROWS_BY_COLS, preferred_element_type=F32)
            delta = jnp.sum(probs * grad_probs, axis=1, keepdims=True)
            grad_score = (probs * (grad_probs - delta)).astype(BF)
            pieces[head, 0, rows, :] = (
                jnp.dot(grad_score, k, preferred_element_type=F32) * scale
            )
            pieces[head, 1, upto, :] += (
                lax.dot_general(grad_score, q, OVER_ROWS, preferred_element_type=F32) * scale
            )
            pieces[head, 2, upto, :] += lax.dot_general(
                probs.astype(BF), grad, OVER_ROWS, preferred_element_type=F32
            )
    tab = (tables[0], tables[1], tables[2])
    bias_out[...] = jnp.zeros_like(bias_out)
    for half in range(2):
        parts = [pieces[half * 2 + j // 3, j % 3] for j in range(6)]
        cols = pl.ds(half * 384, 384)
        low = rotary(jnp.concatenate(parts, axis=1), tab, -1.0).astype(BF)
        grad_out[:, cols] = low
        bias_out[0:1, cols] = jnp.sum(low.astype(F32), axis=0, keepdims=True)


def attention_back(qkv, grad_att, tables, seg_col, seg_row, maxima, totals):
    shape = jax.ShapeDtypeStruct
    return pl.pallas_call(
        attention_back_kernel,
        out_shape=(shape((TOK, WIDE), BF), shape((8, WIDE), F32)),
        in_specs=[IN_VMEM] * 7,
        out_specs=(IN_VMEM,) * 2,
        scratch_shapes=[pltpu.VMEM((HEADS, 3, TOK, HD), F32)],
        compiler_params=pltpu.CompilerParams(vmem_limit_bytes=VMEM_LIMIT),
        name="attention_back",
    )(qkv, grad_att, tables, seg_col, seg_row, maxima, totals)


def sum_grads_kernel(
    gu_p, qkv_p, down_p, out_p, ln_p, bias_p,
    gu_f, qkv_f, down_f, out_f, small_f,
    gu_a, gu_r, gu_t, gu_c, qkv_a, qkv_r, qkv_t, qkv_c,
    down_a, down_r, down_t, down_c, out_a, out_r, out_t, out_c,
    ln_t, small_t,
    a_send, a_recv, b_send, b_recv, c_send, c_recv, d_send, d_recv, e_send, e_recv,
    g_send, g_recv, h_send, h_recv, local,
):
    at = Place()
    others = [at.replica((at.dp + k) % 16) for k in range(1, 16)]
    greet(group_others(at) + others)
    step_a, step_b, step_c = (a_send, a_recv), (b_send, b_recv), (c_send, c_recv)
    step_d, step_e = (d_send, d_recv), (e_send, e_recv)
    step_g, step_h = (g_send, g_recv), (h_send, h_recv)
    core, q, x = at.core, at.q, at.x
    cq = core * 8 + q

    partial = (gu_p, qkv_p, down_p, out_p)
    accs = (gu_a, qkv_a, down_a, out_a)
    recvs = (gu_r, qkv_r, down_r, out_r)
    slots = (gu_t, qkv_t, down_t, out_t)
    packs = (gu_c, qkv_c, down_c, out_c)
    order = (0, 2, 3, 1)

    def half(k, c):
        if k == 0:
            return gu_p.at[:, :, c]
        if k == 1:
            return qkv_p.at[:, c]
        return partial[k].at[c]

    def chunk(k, p):
        if k == 0:
            return gu_a.at[:, :, p]
        if k == 1:
            return qkv_a.at[:, p]
        return accs[k].at[p]

    def blocks(k):
        if k == 0:
            return [(a, b) for a in range(2) for b in range(4)]
        if k == 1:
            return [(b,) for b in range(4)]
        return [()]

    def full(lead, p):
        return lead + (p,)

    def pack_for(k, xt):
        if k == 0:
            return gu_c.at[:, xt]
        if k == 1:
            return qkv_c.at[xt]
        return packs[k].at[:, pl.ds(pl.multiple_of(xt * 512, 512), 512)]

    def landing(k, xs, p):
        if k == 0:
            return gu_f.at[xs, :, p]
        if k == 1:
            return qkv_f.at[p, :, pl.ds(pl.multiple_of(xs * WIDE, WIDE), WIDE)]
        return (gu_f, qkv_f, down_f, out_f)[k].at[xs, p]

    def piece(k, p):
        if k == 0:
            return gu_f.at[:, :, p]
        if k == 1:
            return qkv_f.at[p]
        return (gu_f, qkv_f, down_f, out_f)[k].at[:, p]

    mine = pl.ds(pl.multiple_of(at.g * 256, 256), 256)
    for j in range(1, 8):
        g = (at.g + j) % 8
        push(
            ln_p.at[:, pl.ds(pl.multiple_of(g * 256, 256), 256)],
            ln_t.at[j - 1],
            step_g,
            j - 1,
            at.group(g),
        )
    first = {}
    for k in order:
        first[k] = push(half(k, 1 - core), recvs[k], step_a, k, at.sibling())
        copy = pltpu.make_async_copy(half(k, core), accs[k], local.at[k])
        copy.start()
        first[k + 4] = copy
    total = ln_p[:, mine] + bias_p[...]
    for j in range(7):
        settle(ln_t.at[j], step_g, j, at.group(at.g)).wait_recv()
        total += ln_t[j]
    small_t[pl.ds(at.dp, 1)] = total[None]
    for j, device in enumerate(others):
        push(small_t.at[at.dp], small_t.at[at.dp], step_h, j, device)
    second = {}
    for k in order:
        first[k].wait_recv()
        first[k + 4].wait()
        for lead in blocks(k):

            def add(p, carry):
                index = full(lead, p)
                accs[k][index] = (accs[k][index].astype(F32) + recvs[k][index].astype(F32)).astype(
                    BF
                )
                return carry

            lax.fori_loop(0, 8, add, 0)
        for m, device in enumerate(chip_others(at)):
            second[k, m] = push(chunk(k, q ^ (m + 1)), slots[k].at[m], step_b, k * 7 + m, device)
    third = {}
    for k in order:
        for m in range(7):
            second[k, m].wait_recv()
        for lead in blocks(k):
            value = accs[k][full(lead, q)].astype(F32)
            for m in range(7):
                value += slots[k][(m,) + lead].astype(F32)
            packs[k][lead + (Ellipsis,)] = value.astype(BF)
        for j in range(1, 4):
            xt = (x + j) % 4
            third[k, j] = push(
                pack_for(k, xt), landing(k, x, cq), step_c, k * 3 + j - 1, at.row(xt)
            )
        copy = pltpu.make_async_copy(pack_for(k, x), landing(k, x, cq), local.at[4 + k])
        copy.start()
        third[k, 0] = copy
    fourth, fifth = {}, {}
    for k in order:
        third[k, 0].wait()
        for j in range(1, 4):
            third[k, j].wait_recv()
        for m, device in enumerate(chip_others(at)):
            fourth[k, m] = push(piece(k, cq), piece(k, cq), step_d, k * 7 + m, device)
        fifth[k, 7] = push(piece(k, cq), piece(k, cq), step_e, k * 8 + 7, at.sibling())
    for k in order:
        for m in range(7):
            fourth[k, m].wait_recv()
            p = core * 8 + (q ^ (m + 1))
            fifth[k, m] = push(piece(k, p), piece(k, p), step_e, k * 8 + m, at.sibling())
    for j in range(15):
        settle(small_t.at[0], step_h, j, at.group(at.g)).wait_recv()
    result = small_t[0]
    for j in range(1, 16):
        result += small_t[j]
    small_f[...] = result
    for k in order:
        first[k].wait_send()
        for m in range(7):
            second[k, m].wait_send()
            fourth[k, m].wait_send()
        for j in range(1, 4):
            third[k, j].wait_send()
        for m in range(8):
            fifth[k, m].wait_send()
            fifth[k, m].wait_recv()
    for j in range(7):
        settle(ln_t.at[j], step_g, j, at.group(at.g)).wait_send()
    for j in range(15):
        settle(small_t.at[0], step_h, j, at.group(at.g)).wait_send()


def sum_grads(gu_p, qkv_p, down_p, out_p, ln_p, bias_p):
    shape = jax.ShapeDtypeStruct
    vmem = pltpu.VMEM
    return pl.pallas_call(
        sum_grads_kernel,
        out_shape=(
            shape((4, 2, 16, 32, WIDE), BF),
            shape((16, 32, 4 * WIDE), BF),
            shape((4, 16, 48, 512), BF),
            shape((4, 16, 16, 512), BF),
            shape((8, 256), F32),
        ),
        in_specs=[IN_ANY] * 4 + [IN_VMEM] * 2,
        out_specs=(IN_ANY,) * 4 + (IN_VMEM,),
        scratch_shapes=[
            vmem((2, 4, 8, 32, WIDE), BF),
            vmem((2, 4, 8, 32, WIDE), BF),
            vmem((7, 2, 4, 32, WIDE), BF),
            vmem((2, 4, 32, WIDE), BF),
            vmem((4, 8, 32, WIDE), BF),
            vmem((4, 8, 32, WIDE), BF),
            vmem((7, 4, 32, WIDE), BF),
            vmem((4, 32, WIDE), BF),
            vmem((8, 48, D), BF),
            vmem((8, 48, D), BF),
            vmem((7, 48, D), BF),
            vmem((48, D), BF),
            vmem((8, 16, D), BF),
            vmem((8, 16, D), BF),
            vmem((7, 16, D), BF),
            vmem((16, D), BF),
            vmem((7, 8, 256), F32),
            vmem((16, 8, 256), F32),
        ]
        + dma_sems(4)
        + dma_sems(28)
        + dma_sems(12)
        + dma_sems(28)
        + dma_sems(32)
        + dma_sems(7)
        + dma_sems(15)
        + [pltpu.SemaphoreType.DMA((8,))],
        compiler_params=params(5),
        name="sum_grads",
    )(gu_p, qkv_p, down_p, out_p, ln_p, bias_p)


def matmul(a, b):
    return jnp.dot(a, b, preferred_element_type=F32)


def matmul_t(a, b):
    return lax.dot_general(a, b, ROWS_BY_COLS, preferred_element_type=F32)


def outer(a, b):
    return lax.dot_general(a, b, OVER_ROWS, preferred_element_type=F32).astype(BF)


def on_device(
    block_in, segments, ln1_gain, ln1_bias, qkv_weight, qkv_bias, out_weight,
    ln2_gain, ln2_bias, gate_up_weight, down_weight, cotangent,
):
    zero = jnp.zeros((256,), F32)
    par = jnp.stack([ln1_gain, ln1_bias, ln2_gain, ln2_bias, zero, zero, zero, zero])
    gate_up = jnp.transpose(gate_up_weight, (1, 0, 2))
    seg_col = segments[:, None]
    seg_row = segments[None, :]
    (
        cot_full, par, normed, qkv, attended, maxima, totals, tables, x_own,
        hidden_in, normed_two, qkv_s, out_s, gu_s, down_s,
    ) = front(
        block_in, cotangent, par, qkv_bias[None, :], seg_col, seg_row,
        qkv_weight, out_weight, gate_up, down_weight,
    )
    qkv_s, out_s = qkv_s.reshape(D, WIDE), out_s.reshape(256, D)
    gu_s, down_s = gu_s.reshape(2, D, WIDE), down_s.reshape(WIDE, D)
    gate = matmul(normed_two, gu_s[0])
    up = matmul(normed_two, gu_s[1])
    sig = jax.nn.sigmoid(gate)
    lane = lax.broadcasted_iota(jnp.int32, (1, WIDE), 1)
    kept = (lane >= 128) | (lax.axis_index("row") < 2)
    act = gate * sig
    hidden = jnp.where(kept, act * up, 0.0).astype(BF)
    grad_hidden = jnp.where(kept, matmul_t(cot_full, down_s), 0.0)
    grad_gate = (grad_hidden * up * (sig * (1.0 + gate * (1.0 - sig)))).astype(BF)
    grad_up = (grad_hidden * act).astype(BF)
    grad_in, branch, activations, sums_two = mlp_back(
        grad_gate, grad_up, gu_s, hidden, down_s, hidden_in, cot_full, par
    )
    grad_att = matmul_t(branch, out_s).astype(BF)
    grad_proj, bias_sums = attention_back(
        qkv, grad_att, tables, seg_col, seg_row, maxima, totals
    )
    input_grad, sums_one = input_back(grad_proj, qkv_s, x_own, grad_in, par)
    gu_p = jnp.stack([outer(normed_two, grad_gate), outer(normed_two, grad_up)])
    qkv_p = outer(normed, grad_proj)
    down_p = outer(hidden, cot_full)
    out_p = outer(attended, branch)
    ln_p = jnp.concatenate([sums_one[0:2], sums_two[0:2], jnp.zeros((4, D), F32)])
    bias_p = jnp.concatenate(
        [jnp.zeros((4, 256), F32), bias_sums[0].reshape(3, 256), jnp.zeros((1, 256), F32)]
    )
    gu_f, qkv_f, down_f, out_f, small = sum_grads(
        gu_p.reshape(2, 4, 2, 8, 32, WIDE),
        qkv_p.reshape(4, 2, 8, 32, WIDE),
        down_p.reshape(2, 8, 48, D),
        out_p.reshape(2, 8, 16, D),
        ln_p,
        bias_p,
    )
    gu_f = gu_f.reshape(4, 2, 512, WIDE)
    gu_f = jnp.concatenate([gu_f[0], gu_f[1], gu_f[2, :, :, 128:], gu_f[3, :, :, 128:]], axis=2)
    gu_grad = jnp.transpose(gu_f, (1, 0, 2)).astype(F32)
    down_f = down_f.reshape(4, WIDE, 512)
    down_grad = jnp.concatenate(
        [down_f[0], down_f[1], down_f[2, 128:], down_f[3, 128:]], axis=0
    ).astype(F32)
    return (
        activations,
        input_grad,
        small[0],
        small[1],
        qkv_f.reshape(512, 4 * WIDE).astype(F32),
        small[4:7].reshape(WIDE),
        out_f.reshape(1024, 512).astype(F32),
        small[2],
        small[3],
        gu_grad,
        down_grad,
    )


def solution(mesh):
    wide = P("dp", ("row", "col"))
    vector = P(("row", "col"))
    return jax.shard_map(
        on_device,
        mesh=mesh,
        in_specs=(
            wide, P("dp"), vector, vector, P("row", "col"), P(("col", "row")), P("col", "row"),
            vector, vector, P("row", None, "col"), P("col", "row"), wide,
        ),
        out_specs=(
            wide, wide, vector, vector, P("row", "col"), P(("col", "row")), P("col", "row"),
            vector, vector, P("row", None, "col"), P("col", "row"),
        ),
        check_vma=False,
    )
```

```python
import math

import jax
import jax.numpy as jnp
from jax import lax
from jax.experimental import pallas as pl
from jax.experimental.pallas import tpu as pltpu
from jax.sharding import PartitionSpec as P

D = 2048
HD = 64
ROT = 16
HEADS = 4
TOK = 512
OWN = 64
WIDE = 768
EPSILON = 1e-05
BF = jnp.bfloat16
F32 = jnp.float32
MESH = pl.DeviceIdType.MESH
VMEM_LIMIT = 59 * 2**20
ROWS_BY_COLS = (((1,), (1,)), ((), ()))
OVER_ROWS = (((0,), (0,)), ((), ()))

IN_VMEM = pl.BlockSpec(memory_space=pltpu.VMEM)
IN_ANY = pl.BlockSpec(memory_space=pl.ANY)


class Place:
    def __init__(self):
        self.dp = lax.axis_index("dp")
        self.x = lax.axis_index("row")
        self.zh = lax.axis_index("col")
        self.y = self.dp // 4
        self.zl = (self.dp // 2) % 2
        self.core = self.dp % 2
        self.q = self.dp // 2
        self.g = self.x * 2 + self.zh

    def group(self, g):
        return (self.dp, g // 2, g % 2)

    def row(self, x):
        return (self.dp, x, self.zh)

    def chip(self, q):
        return (q * 2 + self.core, self.x, self.zh)

    def mate(self):
        return (self.dp, self.x, 1 - self.zh)

    def near_replicas(self):
        def chip(y, zl):
            return ((y * 2 + zl) * 2 + self.core, self.x, self.zh)

        return [
            chip((self.y + 1) % 4, self.zl),
            chip((self.y + 3) % 4, self.zl),
            chip(self.y, 1 - self.zl),
            self.sibling(),
        ]

    def sibling(self):
        return (self.q * 2 + 1 - self.core, self.x, self.zh)

    def replica(self, dp):
        return (dp, self.x, self.zh)


def greet(partners):
    barrier = pltpu.get_barrier_semaphore()
    for partner in partners:
        pl.semaphore_signal(barrier, inc=1, device_id=partner, device_id_type=MESH)
    pl.semaphore_wait(barrier, len(partners))


def push(src, dst, sems, index, device):
    send, recv = sems
    copy = pltpu.make_async_remote_copy(
        src_ref=src,
        dst_ref=dst,
        send_sem=send.at[index],
        recv_sem=recv.at[index],
        device_id=device,
        device_id_type=MESH,
    )
    copy.start()
    return copy


def group_others(at):
    return [at.group((at.g + k) % 8) for k in range(1, 8)]


def chip_others(at):
    return [at.chip(at.q ^ k) for k in range(1, 8)]


def dma_sems(amount):
    return [pltpu.SemaphoreType.DMA((amount,)), pltpu.SemaphoreType.DMA((amount,))]


def params(collective_id):
    return pltpu.CompilerParams(
        collective_id=collective_id, has_side_effects=True, vmem_limit_bytes=VMEM_LIMIT
    )


def tile_start(x):
    return 5 * x + jnp.minimum(x, 1)


def settle(ref, sems, index, device):
    send, recv = sems
    return pltpu.make_async_remote_copy(
        src_ref=ref,
        dst_ref=ref,
        send_sem=send.at[index],
        recv_sem=recv.at[index],
        device_id=device,
        device_id_type=MESH,
    )


class Gather:
    def __init__(self, pos, pair, device, whole, half, sems, base=0, on_piece=None):
        self.pos, self.pair, self.device = pos, pair, device
        self.whole, self.half, self.sems, self.base = whole, half, sems, base
        self.right, self.left, self.far = (pos + 1) % 4, (pos + 3) % 4, (pos + 2) % 4
        self.on_piece = on_piece or (lambda r, p, k: None)

    def push(self, index, ref, device, src=None):
        push(ref if src is None else src, ref, self.sems, self.base + index, device)

    def arrived(self, index, ref):
        settle(ref, self.sems, self.base + index, self.device(self.pos, self.pair)).wait_recv()

    def start(self, own=None):
        ref = self.whole(self.pos, self.pair)
        self.push(1, ref, self.device(self.right, self.pair), own)
        self.push(2, ref, self.device(self.left, self.pair), own)
        self.push(0, ref, self.device(self.pos, 1 - self.pair), own)
        self.on_piece(self.pos, self.pair, 0)

    def forward(self, first, pair, slot):
        self.arrived(first, self.whole(self.left, pair))
        self.push(first + 2, self.half(self.left, pair, 0), self.device(self.right, self.pair))
        self.on_piece(self.left, pair, slot)
        self.arrived(first + 1, self.whole(self.right, pair))
        self.push(first + 3, self.half(self.right, pair, 1), self.device(self.left, self.pair))
        self.on_piece(self.right, pair, slot + 1)

    def forward_ring(self):
        self.forward(1, self.pair, 1)

    def spread_pair(self):
        ref = self.whole(self.pos, 1 - self.pair)
        self.arrived(0, ref)
        self.push(5, ref, self.device(self.right, self.pair))
        self.push(6, ref, self.device(self.left, self.pair))
        self.on_piece(self.pos, 1 - self.pair, 3)

    def forward_pair(self):
        self.forward(5, 1 - self.pair, 4)

    def finish(self):
        for first, pair, slot in ((3, self.pair, 6), (7, 1 - self.pair, 7)):
            self.arrived(first, self.half(self.far, pair, 0))
            self.arrived(first + 1, self.half(self.far, pair, 1))
            self.on_piece(self.far, pair, slot)

    def drain(self):
        for index in range(9):
            ref = self.whole(self.pos, self.pair)
            if index in (3, 4, 7, 8):
                ref = self.half(self.pos, self.pair, 0)
            settle(ref, self.sems, self.base + index, self.device(self.pos, self.pair)).wait_send()


class RowScatter:
    def __init__(self, at, part, half_in, full_in, pair_in, pair_out, sems, base=0):
        self.at, self.part, self.half_in, self.full_in = at, part, half_in, full_in
        self.pair_in, self.pair_out, self.sems, self.base = pair_in, pair_out, sems, base
        self.right, self.left = (at.x + 1) % 4, (at.x + 3) % 4
        self.planes = (1 - at.zh, at.zh)

    def rows(self, x, plane, half=None):
        start = (x * 2 + plane) * OWN
        if half is None:
            return pl.ds(pl.multiple_of(start, OWN), OWN)
        return pl.ds(pl.multiple_of(start + half * (OWN // 2), OWN // 2), OWN // 2)

    def push(self, index, src, dst, device):
        push(src, dst, self.sems, self.base + index, device)

    def arrived(self, index, ref):
        settle(ref, self.sems, self.base + index, self.at.row(self.at.x)).wait_recv()

    def first(self):
        far = (self.at.x + 2) % 4
        for role, plane in enumerate(self.planes):
            for side, x in enumerate((self.right, self.left)):
                self.push(
                    role * 4 + side,
                    self.part.at[self.rows(far, plane, side)],
                    self.half_in.at[role, side],
                    self.at.row(x),
                )

    def second(self, role):
        plane = self.planes[role]
        for side, x in enumerate((self.right, self.left)):
            box = self.half_in.at[role, side]
            self.arrived(role * 4 + side, box)
            rows = self.rows(x, plane, side)
            self.part[rows, :] = (self.part[rows, :].astype(F32) + box[...].astype(F32)).astype(BF)
            self.push(
                role * 4 + 2 + side,
                self.part.at[self.rows(x, plane)],
                self.full_in.at[role, side],
                self.at.row(x),
            )

    def own(self, role):
        for side in range(2):
            self.arrived(role * 4 + 2 + side, self.full_in.at[role, side])
        total = self.part[self.rows(self.at.x, self.planes[role]), :].astype(F32)
        return total + self.full_in[role, 0].astype(F32) + self.full_in[role, 1].astype(F32)

    def third(self):
        self.pair_out[...] = self.own(0).astype(BF)
        self.push(8, self.pair_out, self.pair_in, self.at.mate())

    def fourth(self):
        total = self.own(1)
        self.arrived(8, self.pair_in)
        return total + self.pair_in[...].astype(F32)

    def drain(self):
        for index in range(9):
            box = self.full_in.at[0, 0] if index % 4 > 1 else self.half_in.at[0, 0]
            if index == 8:
                box = self.pair_in
            settle(box, self.sems, self.base + index, self.at.row(self.at.x)).wait_send()


def scatter_scratch():
    return [
        pltpu.VMEM((TOK, D), BF),
        pltpu.VMEM((2, 2, OWN // 2, D), BF),
        pltpu.VMEM((2, 2, OWN, D), BF),
        pltpu.VMEM((OWN, D), BF),
        pltpu.VMEM((OWN, D), BF),
    ] + dma_sems(9)


class PieceScatter:
    def __init__(self, at, acc, boxes, sems, base):
        self.at, self.acc, self.sems, self.base = at, acc, sems, base
        self.half_in, self.full_in, self.pair_in, self.pair_out, self.pack = boxes
        self.right, self.left = (at.y + 1) % 4, (at.y + 3) % 4
        self.planes = (1 - at.zl, at.zl)

    def push(self, index, src, dst, y, zl):
        device = ((y * 2 + zl) * 2 + self.at.core, self.at.x, self.at.zh)
        push(src, dst, self.sems, self.base + index, device)

    def arrived(self, index, ref):
        settle(ref, self.sems, self.base + index, self.at.row(self.at.x)).wait_recv()

    def first(self):
        far = (self.at.y + 2) % 4
        for role, plane in enumerate(self.planes):
            for side, y in enumerate((self.right, self.left)):
                self.push(
                    role * 4 + side,
                    self.acc.at[side, :, far * 2 + plane],
                    self.half_in.at[role, side],
                    y,
                    self.at.zl,
                )

    def second(self, role):
        plane = self.planes[role]
        for side, y in enumerate((self.right, self.left)):
            self.arrived(role * 4 + side, self.half_in.at[role, side])
            q = y * 2 + plane
            for b in range(self.acc.shape[1]):
                self.acc[side, b, q] = (
                    self.acc[side, b, q].astype(F32) + self.half_in[role, side, b].astype(F32)
                ).astype(BF)
            self.push(
                role * 4 + 2 + side,
                self.acc.at[:, :, q],
                self.full_in.at[role, side],
                y,
                self.at.zl,
            )

    def total(self, role, out, extra=None):
        for side in range(2):
            self.arrived(role * 4 + 2 + side, self.full_in.at[role, side])
        q = self.at.y * 2 + self.planes[role]
        for a in range(2):
            for b in range(self.acc.shape[1]):
                value = self.acc[a, b, q].astype(F32)
                value += self.full_in[role, 0, a, b].astype(F32)
                value += self.full_in[role, 1, a, b].astype(F32)
                if extra is not None:
                    value += extra[a, b].astype(F32)
                out[a, b] = value.astype(BF)

    def third(self):
        self.total(0, self.pair_out)
        self.push(8, self.pair_out, self.pair_in, self.at.y, 1 - self.at.zl)

    def fourth(self):
        self.arrived(8, self.pair_in)
        self.total(1, self.pack, self.pair_in)

    def drain(self):
        for index in range(9):
            box = self.full_in.at[0, 0] if index % 4 > 1 else self.half_in.at[0, 0]
            if index == 8:
                box = self.pair_in
            settle(box, self.sems, self.base + index, self.at.row(self.at.x)).wait_send()


def piece_scratch(blocks, rows, width):
    vmem = pltpu.VMEM
    return [
        vmem((2, blocks, 8, rows, width), BF),
        vmem((2, 2, blocks, rows, width), BF),
        vmem((2, 2, 2, blocks, rows, width), BF),
        vmem((2, blocks, rows, width), BF),
        vmem((2, blocks, rows, width), BF),
        vmem((2, blocks, rows, width), BF),
    ]


def row_gather(at, ref, sems, base=0):
    def whole(x, plane):
        return ref.at[pl.ds(pl.multiple_of((x * 2 + plane) * OWN, OWN), OWN)]

    def half(x, plane, side):
        start = (x * 2 + plane) * OWN + side * (OWN // 2)
        return ref.at[pl.ds(pl.multiple_of(start, OWN // 2), OWN // 2)]

    return Gather(at.x, at.zh, lambda x, plane: (at.dp, x, plane), whole, half, sems, base)


def column_gather(at, ref, sems, base=0):
    def columns(x, plane):
        return pl.ds(pl.multiple_of((x * 2 + plane) * 256, 256), 256)

    def whole(x, plane):
        return ref.at[:, columns(x, plane)]

    def half(x, plane, side):
        return ref.at[pl.ds(side * 256, 256), columns(x, plane)]

    return Gather(at.x, at.zh, lambda x, plane: (at.dp, x, plane), whole, half, sems, base)


def front_kernel(
    x_in, cot_in, par_in, bias_in, seg_col, seg_row, qkv_w, out_w, gu_w, down_w,
    cot_out, par_out, normed_out, qkv_out, att_out, max_out, sum_out, tab_out, own_out,
    hidden_out, normed2_out, qkv_s_out, out_s_out, gu_s, down_s, norm_sib, cot_sib, att_sib,
    x_v, normed, par, proj, tables, qkv_s, out_s, normed2, rows,
    part, half_in, full_in, pair_in, pair_out, rs_send, rs_recv,
    par_send, par_recv, act_send, act_recv, a_send, a_recv, dp_send, dp_recv, core_send, core_recv,
    sib_send, sib_recv, local,
):
    at = Place()
    greet(group_others(at) + at.near_replicas())
    dp, x, core = at.dp, at.x, at.core
    act, step_a, step_dp = (act_send, act_recv), (a_send, a_recv), (dp_send, dp_recv)
    step_core, step_par = (core_send, core_recv), (par_send, par_recv)
    slabs = (qkv_s, out_s, gu_s, down_s)

    def source(k, xt):
        if k == 0:
            return qkv_w.at[pl.ds(dp * 32, 32), pl.ds(pl.multiple_of(xt * WIDE, WIDE), WIDE)]
        if k == 1:
            return out_w.at[pl.ds(xt * 256 + dp * 16, 16), :]
        start = pl.multiple_of(tile_start(xt) * 128, 128)
        if k == 2:
            return gu_w.at[:, pl.ds(dp * 32, 32), pl.ds(start, WIDE)]
        return down_w.at[pl.ds(start + dp * 48, 48), :]

    def landing(k, xs, p):
        if k == 0:
            return qkv_s.at[xs, p]
        if k == 2:
            return gu_s.at[:, xs, p]
        return slabs[k].at[p, :, pl.ds(pl.multiple_of(xs * 512, 512), 512)]

    def replica(y, zl):
        return (y * 2 + zl) * 2 + core

    def whole(k):
        def of(y, zl):
            p = replica(y, zl)
            if k == 0:
                return qkv_s.at[:, p]
            if k == 2:
                return gu_s.at[:, :, p]
            return slabs[k].at[p]

        return of

    def half(k):
        def of(y, zl, side):
            p = replica(y, zl)
            if k == 0:
                return qkv_s.at[pl.ds(side * 2, 2), p]
            if k == 2:
                return gu_s.at[side, :, p]
            return slabs[k].at[p, :, pl.ds(side * 1024, 1024)]

        return of

    core_copies = []

    def to_sibling(k):
        def on_piece(y, zl, slot):
            ref = whole(k)(y, zl)
            core_copies.append(push(ref, ref, step_core, k * 8 + slot, at.sibling()))

        return on_piece

    first = {}

    def send_rows(k):
        for j in (2, 1, 3):
            xt = (x + j) % 4
            first[k, j] = push(
                source(k, xt), landing(k, x, dp), step_a, k * 3 + j - 1, at.row(xt)
            )
        first[k, 0] = pltpu.make_async_copy(source(k, x), landing(k, x, dp), local.at[k])
        first[k, 0].start()

    weights = [
        Gather(
            at.y, at.zl, lambda y, zl: (replica(y, zl), x, at.zh), whole(k), half(k), step_dp, k * 9,
            to_sibling(k),
        )
        for k in range(4)
    ]
    w_qkv, w_out, w_gu, w_down = weights

    def begin(k):
        first[k, 0].wait()
        for j in range(1, 4):
            first[k, j].wait_recv()
        weights[k].start()

    def from_sibling(k):
        ref = whole(k)(at.y, at.zl)
        for slot in range(8):
            settle(ref, step_core, k * 8 + slot, at.sibling()).wait_recv()

    slot = pl.ds(pl.multiple_of(at.g * 256, 256), 256)
    send_rows(0)
    gx = column_gather(at, x_v, act, 0)
    gx.start(x_in)
    par_copies = []
    for j, device in enumerate(group_others(at)):
        par_copies.append(push(par_in, par.at[:, slot], step_par, j, device))
    own = [
        pltpu.make_async_copy(x_in, x_v.at[:, slot], local.at[4]),
        pltpu.make_async_copy(par_in, par.at[:, slot], local.at[5]),
        pltpu.make_async_copy(cot_in, cot_out.at[:, slot], local.at[6]),
    ]
    for copy in own:
        copy.start()
    send_rows(1)
    send_rows(2)
    send_rows(3)
    begin(0)
    make_tables(seg_col, seg_row, tables)
    gx.forward_ring()
    gx.spread_pair()
    w_qkv.forward_ring()
    w_qkv.spread_pair()
    begin(1)
    gx.forward_pair()
    w_qkv.forward_pair()
    w_out.forward_ring()
    w_out.spread_pair()
    gx.finish()
    gcot = column_gather(at, cot_out, act, 9)
    gcot.start(cot_in)
    begin(2)
    for copy in own:
        copy.wait()
    for copy in par_copies:
        copy.wait_recv()

    def norm_rows(i, carry):
        block = pl.ds(pl.multiple_of(i * 32, 32), 32)
        scaled, _ = norm(x_v[block, :].astype(F32))
        normed[block, :] = (scaled * par[0:1, :] + par[1:2, :]).astype(BF)
        return carry

    lax.fori_loop(0, TOK // 32, norm_rows, 0)
    w_qkv.finish()
    w_out.forward_pair()
    from_sibling(0)
    outgoing = []

    def put(src, dst, index):
        copy = pltpu.make_async_copy(src, dst, local.at[index])
        copy.start()
        outgoing.append(copy)

    put(normed, normed_out, 7)
    sib = (sib_send, sib_recv)
    sib_copies = []
    for xt in range(4):
        cols = pl.ds(xt * 512 + pl.multiple_of((1 - core) * 256, 256), 256)
        sib_copies.append(push(normed.at[:, cols], norm_sib.at[xt], sib, xt, at.sibling()))
    put(qkv_s, qkv_s_out, 8)
    put(x_v.at[own_rows(at)], own_out, 9)
    put(par, par_out, 10)
    between = [
        lambda: (gcot.forward_ring(), w_out.finish()),
        lambda: (gcot.spread_pair(), w_gu.forward_ring(), w_gu.spread_pair()),
        lambda: (begin(3),),
        lambda: (gcot.forward_pair(), w_gu.forward_pair()),
        lambda: (w_down.forward_ring(), w_down.spread_pair()),
        lambda: (gcot.finish(), w_gu.finish()),
        lambda: (from_sibling(1),),
    ]
    for n in range(3):
        cols = pl.ds(n * 256, 256)
        weight = qkv_s[:, :, :, cols].reshape(D, 256)
        proj[:, cols] = (
            jnp.dot(normed[...], weight, preferred_element_type=F32) + bias_in[:, cols]
        )
        between[n]()
    attend(proj, tables, seg_col, seg_row, qkv_out, att_out, max_out, sum_out, between[3:])
    put(out_s, out_s_out, 11)
    sib_copies.append(push(cot_out, cot_sib, sib, 4, at.sibling()))
    cols = pl.ds(pl.multiple_of((1 - core) * 128, 128), 128)
    sib_copies.append(push(att_out.at[:, cols], att_sib, sib, 5, at.sibling()))
    put(tables, tab_out, 12)
    rs = RowScatter(at, part, half_in, full_in, pair_in, pair_out, (rs_send, rs_recv))

    def product(xt):
        weight = out_s[...].reshape(256, D)
        block = pl.ds(pl.multiple_of(xt * 128, 128), 128)
        part[block, :] = jnp.dot(att_out[block, :], weight, preferred_element_type=F32).astype(BF)

    product((x + 2) % 4)
    rs.first()
    product((x + 1) % 4)
    product((x + 3) % 4)
    rs.second(0)
    rs.second(1)
    product(x)
    w_down.forward_pair()
    rs.third()
    hidden_in = rs.fourth() + x_v[own_rows(at), :].astype(F32)
    hidden_out[...] = hidden_in
    scaled, _ = norm(hidden_in)
    rows[...] = (scaled * par[2:3, :] + par[3:4, :]).astype(BF)
    normed2[own_rows(at), :] = rows[...]
    gn = row_gather(at, normed2, act, 18)
    gn.start(rows)
    w_down.finish()
    gn.forward_ring()
    gn.spread_pair()
    gn.forward_pair()
    from_sibling(2)
    from_sibling(3)
    gn.finish()
    put(normed2, normed2_out, 13)
    for k in range(4):
        for j in range(1, 4):
            first[k, j].wait_send()
        weights[k].drain()
    for copy in core_copies + par_copies:
        copy.wait_send()
    for copy in sib_copies:
        copy.wait()
    for program in (gx, gcot, gn, rs):
        program.drain()
    for copy in outgoing:
        copy.wait()


def front(x_in, cot_in, par_in, bias_in, seg_col, seg_row, qkv_w, out_w, gu_w, down_w):
    shape = jax.ShapeDtypeStruct
    vmem = pltpu.VMEM
    return pl.pallas_call(
        front_kernel,
        out_shape=(
            shape((TOK, D), BF),
            shape((8, D), F32),
            shape((TOK, D), BF),
            shape((TOK, WIDE), BF),
            shape((TOK, 256), BF),
            shape((TOK, 128), F32),
            shape((TOK, 128), F32),
            shape((3, TOK, 384), F32),
            shape((OWN, D), BF),
            shape((OWN, D), F32),
            shape((TOK, D), BF),
            shape((4, 16, 32, WIDE), BF),
            shape((16, 16, D), BF),
            shape((2, 4, 16, 32, WIDE), BF),
            shape((16, 48, D), BF),
            shape((4, TOK, 256), BF),
            shape((TOK, D), BF),
            shape((TOK, 128), BF),
        ),
        in_specs=[IN_ANY] * 3 + [IN_VMEM] * 3 + [IN_ANY] * 4,
        out_specs=(IN_ANY,) * 3 + (IN_VMEM,) * 4 + (IN_ANY,) * 2 + (IN_VMEM,) + (IN_ANY,) * 8,
        scratch_shapes=[
            vmem((TOK, D), BF),
            vmem((TOK, D), BF),
            vmem((8, D), F32),
            vmem((TOK, WIDE), F32),
            vmem((3, TOK, 384), F32),
            vmem((4, 16, 32, WIDE), BF),
            vmem((16, 16, D), BF),
            vmem((TOK, D), BF),
            vmem((OWN, D), BF),
        ]
        + scatter_scratch()
        + dma_sems(7)
        + dma_sems(27)
        + dma_sems(12)
        + dma_sems(36)
        + dma_sems(32)
        + dma_sems(6)
        + [pltpu.SemaphoreType.DMA((14,))],
        compiler_params=params(1),
        name="front",
    )(x_in, cot_in, par_in, bias_in, seg_col, seg_row, qkv_w, out_w, gu_w, down_w)


def own_rows(at):
    return pl.ds(pl.multiple_of(at.g * OWN, OWN), OWN)


def gather_columns(at, rows, full, sems, local):
    def columns(g):
        return rows.at[:, pl.ds(pl.multiple_of(g * 256, 256), 256)]

    copy = pltpu.make_async_copy(columns(at.g), full.at[own_rows(at)], local)
    copy.start()
    for k in range(1, 8):
        g = (at.g + k) % 8
        push(columns(g), full.at[own_rows(at)], sems, k - 1, at.group(g))
    copy.wait()


def settle_all(at, piece, sems, amount=7):
    for k in range(amount):
        copy = settle(piece, sems, k, at.group(at.g))
        copy.wait_send()
        copy.wait_recv()


def norm(value):
    mean = jnp.mean(value, axis=1, keepdims=True)
    square = jnp.mean(value * value, axis=1, keepdims=True)
    inverse = lax.rsqrt(square - mean * mean + EPSILON)
    return (value - mean) * inverse, inverse


def norm_back(grad, scaled, inverse, gain):
    inner = grad * gain
    mean = jnp.mean(inner, axis=1, keepdims=True)
    along = jnp.mean(inner * scaled, axis=1, keepdims=True)
    return inverse * (inner - mean - scaled * along)


def rotary(value, tables, sign):
    width = value.shape[1]
    return (
        value * tables[0]
        + pltpu.roll(value, width - 8, 1) * (sign * tables[1])
        + pltpu.roll(value, 8, 1) * (sign * tables[2])
    )


def make_tables(seg_col, seg_row, tables):
    half = ROT // 2
    for block in range(4):
        rows = pl.ds(block * 128, 128)
        places = lax.broadcasted_iota(jnp.int32, (128, 128), 0) + block * 128
        before = jnp.where(seg_row[0:1, :] < seg_col[rows, :], 1.0, 0.0)
        starts = jnp.sum(before, axis=1, keepdims=True)
        offsets = places.astype(F32) - starts
        lane = lax.broadcasted_iota(jnp.int32, (128, 128), 1)
        entry = lane % HD
        power = (entry % half).astype(F32) * (-2.0 * math.log(10000.0) / ROT)
        angles = offsets * jnp.exp(power)
        cosine, sine = jnp.cos(angles), jnp.sin(angles)
        keep = jnp.where(entry < ROT, cosine, 1.0)
        fore = jnp.where(entry < half, -sine, 0.0)
        back = jnp.where((entry >= half) & (entry < ROT), sine, 0.0)
        for j, (table, rest) in enumerate(((keep, 1.0), (fore, 0.0), (back, 0.0))):
            low = lane < HD
            tables[j, rows, 0:128] = table
            tables[j, rows, 128:256] = jnp.where(low, rest, table)
            tables[j, rows, 256:384] = jnp.where(low, table, rest)


def head_part(value, head, kind):
    start = head * 3 * HD + kind * HD
    return value[:, start : start + HD]


def allowed(seg_col, seg_row, block, keys):
    start = block * 128
    rows = lax.broadcasted_iota(jnp.int32, (128, keys), 0) + start
    cols = lax.broadcasted_iota(jnp.int32, (128, keys), 1)
    same = seg_col[start : start + 128, :] == seg_row[0:1, :keys]
    return (cols <= rows) & same


def attend(proj, tables, seg_col, seg_row, qkv_out, att_out, max_out, sum_out, between):
    scale = 1.0 / math.sqrt(HD)
    for half in range(2):
        cols = pl.ds(half * 384, 384)
        tab = (tables[0], tables[1], tables[2])
        qkv_out[:, cols] = rotary(proj[:, cols], tab, 1.0).astype(BF)
    for block in range(4):
        keys = (block + 1) * 128
        rows = pl.ds(block * 128, 128)
        mask = allowed(seg_col, seg_row, block, keys)
        outs, maxima, totals = [], [], []
        for head in range(HEADS):
            q = head_part(qkv_out[rows, :], head, 0)
            k = head_part(qkv_out[pl.ds(0, keys), :], head, 1)
            v = head_part(qkv_out[pl.ds(0, keys), :], head, 2)
            score = lax.dot_general(q, k, ROWS_BY_COLS, preferred_element_type=F32) * scale
            score = jnp.where(mask, score, -1e30)
            top = jnp.max(score, axis=1, keepdims=True)
            raised = jnp.exp(score - top)
            total = jnp.sum(raised, axis=1, keepdims=True)
            low = (raised / total).astype(BF)
            outs.append(jnp.dot(low, v, preferred_element_type=F32))
            maxima.append(top)
            totals.append(total)
        att_out[rows, :] = jnp.concatenate(outs, axis=1).astype(BF)
        for head in range(HEADS):
            max_out[rows, head : head + 1] = maxima[head]
            sum_out[rows, head : head + 1] = totals[head]
        if block < len(between):
            between[block]()


def attend_back(
    qkv, grad_att, tables, seg_col, seg_row, maxima, totals, grad_out, pieces, between
):
    scale = 1.0 / math.sqrt(HD)
    pieces[...] = jnp.zeros_like(pieces)
    for block in range(4):
        keys = (block + 1) * 128
        rows = pl.ds(block * 128, 128)
        upto = pl.ds(0, keys)
        mask = allowed(seg_col, seg_row, block, keys)
        for head in range(HEADS):
            q = head_part(qkv[rows, :], head, 0)
            k = head_part(qkv[upto, :], head, 1)
            v = head_part(qkv[upto, :], head, 2)
            grad = grad_att[rows, :][:, head * HD : (head + 1) * HD]
            score = lax.dot_general(q, k, ROWS_BY_COLS, preferred_element_type=F32) * scale
            score = jnp.where(mask, score, -1e30)
            probs = jnp.exp(score - maxima[rows, head : head + 1]) / totals[rows, head : head + 1]
            grad_probs = lax.dot_general(grad, v, ROWS_BY_COLS, preferred_element_type=F32)
            delta = jnp.sum(probs * grad_probs, axis=1, keepdims=True)
            grad_score = (probs * (grad_probs - delta)).astype(BF)
            pieces[head, 0, rows, :] = (
                jnp.dot(grad_score, k, preferred_element_type=F32) * scale
            )
            pieces[head, 1, upto, :] += (
                lax.dot_general(grad_score, q, OVER_ROWS, preferred_element_type=F32) * scale
            )
            pieces[head, 2, upto, :] += lax.dot_general(
                probs.astype(BF), grad, OVER_ROWS, preferred_element_type=F32
            )
        between[block]()
    tab = (tables[0], tables[1], tables[2])
    sums = []
    for half in range(2):
        parts = [pieces[half * 2 + j // 3, j % 3] for j in range(6)]
        cols = pl.ds(half * 384, 384)
        low = rotary(jnp.concatenate(parts, axis=1), tab, -1.0).astype(BF)
        grad_out[:, cols] = low
        sums.append(jnp.sum(low.astype(F32), axis=0, keepdims=True))
    return jnp.concatenate(sums, axis=1)


def back_kernel(
    n2_h, gu_h, down_h, out_h, qkvs_h, cot_h, normed_h, tab_h, norm_sib_h, cot_sib_h, att_sib_h,
    hidden_in, par, att, qkv, seg_col, seg_row, maxima, totals, x_own,
    act_out, input_out, gu_f, qkv_f, down_f, out_f, small_f,
    n2, n2_sib, cot, cot_sib, gb, gb_sib, att_sib,
    hidden, hidden_sib, gg, gg_sib, gate_up_sib, grad_up, gp_sib, grad_att, grad_in,
    out_s, rows, sums, ln_t, small_t,
    part, part2,
    *rest,
):
    at = Place()
    others = [at.replica((at.dp + k) % 16) for k in range(1, 16)]
    greet(group_others(at) + others)
    core, q, x = at.core, at.q, at.x
    cq = core * 8 + q
    rest = list(rest)

    def take(amount):
        head, rest[:] = rest[:amount], rest[amount:]
        return head

    boxes = [take(4) for _ in range(2)]
    boxes.append(boxes[0])
    arrays = [take(6) for _ in range(4)]
    (gu_a, qkv_a, down_a, out_a) = [a[0] for a in arrays]
    packs = [a[5] for a in arrays]
    rs_sems, act_sems, sib_sems = take(2), take(2), take(2)
    dps_sems, row_sems, dpg_sems, core_sems = take(2), take(2), take(2), take(2)
    ln_sems, small_sems = take(2), take(2)
    (local,) = take(1)
    finals = (gu_f, qkv_f, down_f, out_f)

    loads = {}

    def load(name, src, dst, index):
        loads[name] = lambda: pltpu.make_async_copy(src, dst, local.at[index])
        loads[name]().start()

    def columns(c, xt):
        return pl.ds(pl.multiple_of(xt * 512 + c * 256, 256), 256)

    exchange = {}

    def to_sibling(name, src, dst, index):
        exchange[name] = (dst, index)
        push(src, inbox(name), sib_sems, index, at.sibling())

    def inbox(name):
        ref = exchange[name][0]
        return ref.at[name[1]] if isinstance(name, tuple) else ref

    def exchanged(name):
        settle(inbox(name), sib_sems, exchange[name][1], at.sibling()).wait_recv()

    load("n2", n2_h, n2, 0)
    load("cot", cot_h, cot, 1)
    load("out_s", out_h, out_s, 2)

    def pack_for(k, xt):
        if k == 0:
            return packs[0].at[:, xt]
        if k == 1:
            return packs[1].at[xt // 2, xt % 2]
        return packs[k].at[xt // 2, 0, :, pl.ds(pl.multiple_of((xt % 2) * 512, 512), 512)]

    def landing(k, xs, p):
        if k == 0:
            return gu_f.at[xs, :, p]
        if k == 1:
            return qkv_f.at[p, :, pl.ds(pl.multiple_of(xs * WIDE, WIDE), WIDE)]
        return finals[k].at[xs, p]

    def slot(y, zl):
        return core * 8 + y * 2 + zl

    def whole(k):
        def of(y, zl):
            p = slot(y, zl)
            if k == 0:
                return gu_f.at[:, :, p]
            if k == 1:
                return qkv_f.at[p]
            return finals[k].at[:, p]

        return of

    def half(k):
        def of(y, zl, side):
            p = slot(y, zl)
            if k == 0:
                return gu_f.at[pl.ds(side * 2, 2), :, p]
            if k == 1:
                return qkv_f.at[p, :, pl.ds(side * 2 * WIDE, 2 * WIDE)]
            return finals[k].at[pl.ds(side * 2, 2), p]

        return of

    def share(k):
        def on_piece(y, zl, index):
            ref = whole(k)(y, zl)
            push(ref, ref, core_sems, k * 8 + index, at.sibling())

        return on_piece

    scatters = [
        PieceScatter(at, arrays[k][0], arrays[k][1:], dps_sems, k * 9) for k in range(4)
    ]
    s_gu, s_qkv, s_down, s_out = scatters
    gathers = [
        Gather(
            at.y, at.zl, lambda y, zl: ((y * 2 + zl) * 2 + core, x, at.zh), whole(k), half(k),
            dpg_sems, k * 9, share(k),
        )
        for k in range(4)
    ]
    g_gu, g_qkv, g_down, g_out = gathers
    def send_rows(k):
        scatters[k].fourth()
        for j in (2, 1, 3):
            xt = (x + j) % 4
            push(pack_for(k, xt), landing(k, x, cq), row_sems, k * 3 + j - 1, at.row(xt))
        pltpu.make_async_copy(pack_for(k, x), landing(k, x, cq), local.at[12 + k]).start()

    def begin(k):
        pltpu.make_async_copy(pack_for(k, x), landing(k, x, cq), local.at[12 + k]).wait()
        for j in range(3):
            settle(pack_for(k, x), row_sems, k * 3 + j, at.row(x)).wait_recv()
        gathers[k].start()

    rs1, rs2, rs3 = [
        RowScatter(at, p, *boxes[j], rs_sems, j * 9) for j, p in enumerate((part, part2, part))
    ]
    block_of = lambda xt: pl.ds(pl.multiple_of(xt * 128, 128), 128)
    far, right, left = (x + 2) % 4, (x + 1) % 4, (x + 3) % 4
    g_branch = row_gather(at, gb, act_sems, 0)

    def feed_forward(gu_s, down_s):
        load("gate", gu_h.at[0], gu_s.at[0], 7)
        load("up", gu_h.at[1], gu_s.at[1], 8)
        load("down", down_h, down_s, 9)
        for xt in range(4):
            to_sibling(("n2", xt), n2_h.at[:, columns(1 - core, xt)], n2_sib, xt)
        for name in ("n2", "gate", "up", "cot", "down"):
            loads[name]().wait()
        lane = lax.broadcasted_iota(jnp.int32, (1, 256), 1)

        def chunk(n, carry):
            cols = pl.ds(pl.multiple_of(n * 256, 256), 256)
            gate = jnp.dot(n2[...], gu_s[0, :, cols], preferred_element_type=F32)
            up = jnp.dot(n2[...], gu_s[1, :, cols], preferred_element_type=F32)
            grad = lax.dot_general(
                cot[...], down_s[cols, :], ROWS_BY_COLS, preferred_element_type=F32
            )
            kept = (lane >= 128) | (x < 2) | (n > 0)
            sig = jax.nn.sigmoid(gate)
            act = gate * sig
            grad = jnp.where(kept, grad, 0.0)
            hidden[:, cols] = jnp.where(kept, act * up, 0.0).astype(BF)
            gg[:, cols] = (grad * up * (sig * (1.0 + gate * (1.0 - sig)))).astype(BF)
            grad_up[:, cols] = (grad * act).astype(BF)
            return carry

        lax.fori_loop(0, 3, chunk, 0)
        to_sibling(
            "hidden",
            hidden.at[:, pl.ds(pl.multiple_of((1 - core) * 384, 128), 384)],
            hidden_sib,
            5,
        )
        to_sibling("gg", gg, gg_sib, 6)
        to_sibling("up", grad_up, gate_up_sib, 7)

        def product(xt):
            block = block_of(xt)
            value = lax.dot_general(
                gg[block, :], gu_s[0], ROWS_BY_COLS, preferred_element_type=F32
            ) + lax.dot_general(
                grad_up[block, :], gu_s[1], ROWS_BY_COLS, preferred_element_type=F32
            )
            part[block, :] = value.astype(BF)

        product(far)
        rs1.first()
        product(right)
        product(left)
        product(x)

        def product_two(i, carry):
            block = block_of(i)
            part2[block, :] = jnp.dot(
                hidden[block, :], down_s[...], preferred_element_type=F32
            ).astype(BF)
            return carry

        lax.fori_loop(0, 4, product_two, 0)

    pl.run_scoped(
        feed_forward, pltpu.VMEM((2, D, WIDE), BF), pltpu.VMEM((WIDE, D), BF)
    )

    def outer_sum(a, b, a_sib, b_sib):
        return lax.dot_general(
            a, b, OVER_ROWS, preferred_element_type=F32
        ) + lax.dot_general(a_sib, b_sib, OVER_ROWS, preferred_element_type=F32)

    load(("cot_sib", 0), cot_sib_h.at[:, pl.ds(0, 256)], cot_sib.at[0], 3)
    exchanged("hidden")
    mine = hidden[:, pl.ds(pl.multiple_of(core * 384, 128), 384)]
    for a in range(8):
        cols = pl.ds(a * 256, 256)
        loads["cot_sib", a]().wait()
        if a < 7:
            load(("cot_sib", a + 1), cot_sib_h.at[:, pl.ds((a + 1) * 256, 256)], cot_sib.at[(a + 1) % 2], 3 if a % 2 else 18)
        down_a[a // 4, 0, :, :, pl.ds((a % 4) * 256, 256)] = (
            outer_sum(mine, cot[:, cols], hidden_sib[...], cot_sib[a % 2])
            .astype(BF)
            .reshape(8, 48, 256)
        )
    s_down.first()
    rs1.second(0)
    rs1.second(1)
    exchanged("gg")
    exchanged("up")
    for xt in range(4):
        exchanged(("n2", xt))

    def gate_up_grad(xt, carry):
        own, sib = n2[:, columns(core, xt)], n2_sib[xt]
        gu_a[0, xt] = outer_sum(own, gg[...], sib, gg_sib[...]).astype(BF).reshape(8, 32, WIDE)
        gu_a[1, xt] = (
            outer_sum(own, grad_up[...], sib, gate_up_sib[...]).astype(BF).reshape(8, 32, WIDE)
        )
        return carry

    lax.fori_loop(0, 4, gate_up_grad, 0)
    load("nh", normed_h, n2, 4)
    load("nh_sib", norm_sib_h, n2_sib, 5)
    load("att_sib", att_sib_h, att_sib, 6)
    s_gu.first()
    s_down.second(0)
    s_down.second(1)
    rs1.third()
    scaled, inverse = norm(hidden_in[...])
    grad = rs1.fourth()
    value = cot[own_rows(at), :].astype(F32) + norm_back(grad, scaled, inverse, par[2:3, :])
    grad_in[...] = value
    rows[0] = value.astype(BF)
    gb[own_rows(at), :] = value.astype(BF)
    g_branch.start(rows.at[0])
    sums[...] = jnp.zeros_like(sums)
    sums[2:3, :] = jnp.sum(grad * scaled, axis=0, keepdims=True)
    sums[3:4, :] = jnp.sum(grad, axis=0, keepdims=True)
    g_branch.forward_ring()
    s_gu.second(0)
    g_branch.spread_pair()
    s_gu.second(1)
    s_down.third()
    g_branch.forward_pair()
    send_rows(2)
    g_branch.finish()
    to_sibling("gb", gb, gb_sib, 13)

    settle(inbox("gg"), sib_sems, exchange["gg"][1], at.sibling()).wait_send()
    gp = gg

    def attention(tables, pieces, qkv_s):
        load("tab", tab_h, tables, 10)
        load("qkv_s", qkvs_h, qkv_s, 11)
        loads["out_s"]().wait()
        grad_att[...] = lax.dot_general(
            gb[...], out_s[...].reshape(256, D), ROWS_BY_COLS, preferred_element_type=F32
        ).astype(BF)
        rs2.first()
        loads["tab"]().wait()

        def after_two():
            total = rs2.fourth() + hidden_in[...]
            rows[1] = total.astype(BF)
            gather_columns(at, rows.at[1], act_out, (act_sems[0].at[pl.ds(9, 7)], act_sems[1].at[pl.ds(9, 7)]), local.at[16])

        between = [
            lambda: (rs2.second(0), rs2.second(1), s_gu.third()),
            lambda: (rs2.third(), begin(2)),
            lambda: (send_rows(0), g_down.forward_ring(), g_down.spread_pair()),
            lambda: (after_two(), begin(0)),
        ]
        bias_sums = attend_back(
            qkv, grad_att, tables, seg_col, seg_row, maxima, totals, gp, pieces, between
        )
        to_sibling("gp", gp, gp_sib, 14)
        loads["qkv_s"]().wait()
        rs1.drain()

        def product(xt):
            block = block_of(xt)
            weight = qkv_s[...].reshape(D, WIDE)
            part[block, :] = lax.dot_general(
                gp[block, :], weight, ROWS_BY_COLS, preferred_element_type=F32
            ).astype(BF)

        product(far)
        rs3.first()
        product(right)
        product(left)
        product(x)
        sums[4:7, 0:256] = jnp.concatenate([bias_sums[:, j * 256 : (j + 1) * 256] for j in range(3)])

    pl.run_scoped(
        attention,
        pltpu.VMEM((3, TOK, 384), F32),
        pltpu.VMEM((HEADS, 3, TOK, HD), F32),
        pltpu.VMEM((4, 16, 32, WIDE), BF),
    )
    exchanged("gb")
    loads["att_sib"]().wait()
    mine = att[:, pl.ds(pl.multiple_of(core * 128, 128), 128)]
    for a in range(2):
        cols = pl.ds(a * 1024, 1024)
        out_a[a, 0] = (
            outer_sum(mine, gb[:, cols], att_sib[...], gb_sib[:, cols])
            .astype(BF)
            .reshape(8, 16, 1024)
        )
    rs3.second(0)
    rs3.second(1)
    s_out.first()
    exchanged("gp")
    loads["nh"]().wait()
    loads["nh_sib"]().wait()

    def qkv_grad(xt, carry):
        qkv_a[xt // 2, xt % 2] = (
            outer_sum(n2[:, columns(core, xt)], gp[...], n2_sib[xt], gp_sib[...]).astype(BF).reshape(8, 32, WIDE)
        )
        return carry

    lax.fori_loop(0, 4, qkv_grad, 0)
    s_qkv.first()
    rs3.third()
    g_down.forward_pair()
    g_gu.forward_ring()
    s_out.second(0)
    s_out.second(1)
    scaled, inverse = norm(x_own[...].astype(F32))
    grad = rs3.fourth()
    value = grad_in[...] + norm_back(grad, scaled, inverse, par[0:1, :])
    rows[2] = value.astype(BF)
    gather_columns(at, rows.at[2], input_out, (act_sems[0].at[pl.ds(16, 7)], act_sems[1].at[pl.ds(16, 7)]), local.at[17])
    sums[0:1, :] = jnp.sum(grad * scaled, axis=0, keepdims=True)
    sums[1:2, :] = jnp.sum(grad, axis=0, keepdims=True)
    own_columns = pl.ds(pl.multiple_of(at.g * 256, 256), 256)
    ln_copies = []
    for j in range(1, 8):
        g = (at.g + j) % 8
        ln_copies.append(
            push(
                sums.at[pl.ds(0, 4), pl.ds(pl.multiple_of(g * 256, 256), 256)],
                ln_t.at[j - 1],
                ln_sems,
                j - 1,
                at.group(g),
            )
        )
    s_qkv.second(0)
    s_qkv.second(1)
    g_gu.spread_pair()
    s_out.third()
    s_qkv.third()
    send_rows(3)
    send_rows(1)
    total = sums[0:4, own_columns]
    for j in range(7):
        ln_copies[j].wait_recv()
        total += ln_t[j]
    small_t[pl.ds(at.dp, 1), 0:4] = total[None]
    small_t[pl.ds(at.dp, 1), 4:8] = sums[4:8, 0:256][None]
    small_copies = [
        push(small_t.at[at.dp], small_t.at[at.dp], small_sems, j, device)
        for j, device in enumerate(others)
    ]
    begin(3)
    begin(1)
    g_down.finish()
    g_gu.forward_pair()
    g_out.forward_ring()
    g_out.spread_pair()
    g_qkv.forward_ring()
    g_qkv.spread_pair()
    g_gu.finish()
    g_out.forward_pair()
    g_qkv.forward_pair()
    for copy in small_copies:
        copy.wait_recv()
    result = small_t[0]
    for j in range(1, 16):
        result += small_t[j]
    small_f[...] = result
    g_out.finish()
    g_qkv.finish()
    for k in range(4):
        ref = whole(k)(at.y, at.zl)
        for index in range(8):
            settle(ref, core_sems, k * 8 + index, at.sibling()).wait_recv()
            settle(ref, core_sems, k * 8 + index, at.sibling()).wait_send()
        scatters[k].drain()
        gathers[k].drain()
        for j in range(3):
            settle(pack_for(k, x), row_sems, k * 3 + j, at.row(x)).wait_send()
    for copy in ln_copies + small_copies:
        copy.wait_send()
    for name in exchange:
        if name == "gg":
            continue
        settle(inbox(name), sib_sems, exchange[name][1], at.sibling()).wait_send()
    g_branch.drain()
    rs2.drain()
    rs3.drain()
    for j in (9, 16):
        settle_all(at, rows.at[1, :, pl.ds(0, 256)], (act_sems[0].at[pl.ds(j, 7)], act_sems[1].at[pl.ds(j, 7)]))


def back(
    n2, gu_s, down_s, out_s, qkv_s, cot, normed, tables, norm_sib, cot_sib, att_sib,
    hidden_in, par, att, qkv, seg_col, seg_row, maxima, totals, x_own,
):
    shape = jax.ShapeDtypeStruct
    vmem = pltpu.VMEM
    wide = vmem((TOK, D), BF)
    inner = vmem((TOK, WIDE), BF)
    quarters = vmem((4, TOK, 256), BF)
    box = scatter_scratch()[1:5]
    return pl.pallas_call(
        back_kernel,
        out_shape=(
            shape((TOK, 256), BF),
            shape((TOK, 256), BF),
            shape((4, 2, 16, 32, WIDE), BF),
            shape((16, 32, 4 * WIDE), BF),
            shape((4, 16, 48, 512), BF),
            shape((4, 16, 16, 512), BF),
            shape((8, 256), F32),
        ),
        in_specs=[IN_ANY] * 11 + [IN_VMEM] * 9,
        out_specs=(IN_ANY,) * 6 + (IN_VMEM,),
        scratch_shapes=[
            wide, quarters, wide, vmem((2, TOK, 256), BF), wide, wide, vmem((TOK, 128), BF),
            inner, vmem((TOK, 384), BF), inner, inner, inner, inner, inner,
            vmem((TOK, 256), BF), vmem((OWN, D), F32),
            vmem((16, 16, D), BF), vmem((3, OWN, D), BF), vmem((8, D), F32),
            vmem((7, 4, 256), F32), vmem((16, 8, 256), F32),
            wide, wide,
        ]
        + box * 2
        + piece_scratch(4, 32, WIDE)
        + piece_scratch(2, 32, WIDE)
        + piece_scratch(1, 48, 1024)
        + piece_scratch(1, 16, 1024)
        + dma_sems(27)
        + dma_sems(23)
        + dma_sems(15)
        + dma_sems(36)
        + dma_sems(12)
        + dma_sems(36)
        + dma_sems(32)
        + dma_sems(7)
        + dma_sems(15)
        + [pltpu.SemaphoreType.DMA((19,))],
        compiler_params=params(2),
        name="back",
    )(
        n2, gu_s, down_s, out_s, qkv_s, cot, normed, tables, norm_sib, cot_sib, att_sib,
        hidden_in, par, att, qkv, seg_col, seg_row, maxima, totals, x_own,
    )


def on_device(
    block_in, segments, ln1_gain, ln1_bias, qkv_weight, qkv_bias, out_weight,
    ln2_gain, ln2_bias, gate_up_weight, down_weight, cotangent,
):
    zero = jnp.zeros((256,), F32)
    par = jnp.stack([ln1_gain, ln1_bias, ln2_gain, ln2_bias, zero, zero, zero, zero])
    gate_up = jnp.transpose(gate_up_weight, (1, 0, 2))
    seg_col = segments[:, None]
    seg_row = segments[None, :]
    (
        cot_full, par, normed, qkv, attended, maxima, totals, tables, x_own,
        hidden_in, normed_two, qkv_s, out_s, gu_s, down_s, norm_sib, cot_sib, att_sib,
    ) = front(
        block_in, cotangent, par, qkv_bias[None, :], seg_col, seg_row,
        qkv_weight, out_weight, gate_up, down_weight,
    )
    activations, input_grad, gu_f, qkv_f, down_f, out_f, small = back(
        normed_two, gu_s.reshape(2, D, WIDE), down_s.reshape(WIDE, D), out_s, qkv_s, cot_full,
        normed, tables, norm_sib, cot_sib, att_sib, hidden_in, par, attended, qkv, seg_col, seg_row, maxima, totals, x_own,
    )
    gu_f = gu_f.reshape(4, 2, 512, WIDE)
    gu_f = jnp.concatenate([gu_f[0], gu_f[1], gu_f[2, :, :, 128:], gu_f[3, :, :, 128:]], axis=2)
    gu_grad = jnp.transpose(gu_f, (1, 0, 2)).astype(F32)
    down_f = down_f.reshape(4, WIDE, 512)
    down_grad = jnp.concatenate(
        [down_f[0], down_f[1], down_f[2, 128:], down_f[3, 128:]], axis=0
    ).astype(F32)
    return (
        activations,
        input_grad,
        small[0],
        small[1],
        qkv_f.reshape(512, 4 * WIDE).astype(F32),
        small[4:7].reshape(WIDE),
        out_f.reshape(1024, 512).astype(F32),
        small[2],
        small[3],
        gu_grad,
        down_grad,
    )


def solution(mesh):
    wide = P("dp", ("row", "col"))
    vector = P(("row", "col"))
    return jax.shard_map(
        on_device,
        mesh=mesh,
        in_specs=(
            wide, P("dp"), vector, vector, P("row", "col"), P(("col", "row")), P("col", "row"),
            vector, vector, P("row", None, "col"), P("col", "row"), wide,
        ),
        out_specs=(
            wide, wide, vector, vector, P("row", "col"), P(("col", "row")), P("col", "row"),
            vector, vector, P("row", None, "col"), P("col", "row"),
        ),
        check_vma=False,
    )
```

```python
import math

import jax
import jax.numpy as jnp
from jax import lax
from jax.experimental import pallas as pl
from jax.experimental.pallas import tpu as pltpu
from jax.sharding import PartitionSpec as P

D = 2048
HD = 64
ROT = 16
HEADS = 4
TOK = 512
OWN = 64
WIDE = 768
EPSILON = 1e-05
BF = jnp.bfloat16
F32 = jnp.float32
MESH = pl.DeviceIdType.MESH
VMEM_LIMIT = 59 * 2**20
ROWS_BY_COLS = (((1,), (1,)), ((), ()))
OVER_ROWS = (((0,), (0,)), ((), ()))

IN_VMEM = pl.BlockSpec(memory_space=pltpu.VMEM)
IN_ANY = pl.BlockSpec(memory_space=pl.ANY)


class Place:
    def __init__(self):
        self.dp = lax.axis_index("dp")
        self.x = lax.axis_index("row")
        self.zh = lax.axis_index("col")
        self.y = self.dp // 4
        self.zl = (self.dp // 2) % 2
        self.core = self.dp % 2
        self.q = self.dp // 2
        self.g = self.x * 2 + self.zh

    def group(self, g):
        return (self.dp, g // 2, g % 2)

    def row(self, x):
        return (self.dp, x, self.zh)

    def chip(self, q):
        return (q * 2 + self.core, self.x, self.zh)

    def mate(self):
        return (self.dp, self.x, 1 - self.zh)

    def near_replicas(self):
        def chip(y, zl):
            return ((y * 2 + zl) * 2 + self.core, self.x, self.zh)

        return [
            chip((self.y + 1) % 4, self.zl),
            chip((self.y + 3) % 4, self.zl),
            chip(self.y, 1 - self.zl),
            self.sibling(),
        ]

    def sibling(self):
        return (self.q * 2 + 1 - self.core, self.x, self.zh)

    def replica(self, dp):
        return (dp, self.x, self.zh)


def greet(partners):
    barrier = pltpu.get_barrier_semaphore()
    for partner in partners:
        pl.semaphore_signal(barrier, inc=1, device_id=partner, device_id_type=MESH)
    pl.semaphore_wait(barrier, len(partners))


def push(src, dst, sems, index, device):
    send, recv = sems
    copy = pltpu.make_async_remote_copy(
        src_ref=src,
        dst_ref=dst,
        send_sem=send.at[index],
        recv_sem=recv.at[index],
        device_id=device,
        device_id_type=MESH,
    )
    copy.start()
    return copy


def group_others(at):
    return [at.group((at.g + k) % 8) for k in range(1, 8)]


def chip_others(at):
    return [at.chip(at.q ^ k) for k in range(1, 8)]


def dma_sems(amount):
    return [pltpu.SemaphoreType.DMA((amount,)), pltpu.SemaphoreType.DMA((amount,))]


def params(collective_id):
    return pltpu.CompilerParams(
        collective_id=collective_id, has_side_effects=True, vmem_limit_bytes=VMEM_LIMIT
    )


def tile_start(x):
    return 5 * x + jnp.minimum(x, 1)


def settle(ref, sems, index, device):
    send, recv = sems
    return pltpu.make_async_remote_copy(
        src_ref=ref,
        dst_ref=ref,
        send_sem=send.at[index],
        recv_sem=recv.at[index],
        device_id=device,
        device_id_type=MESH,
    )


class Gather:
    def __init__(self, pos, pair, device, whole, half, sems, base=0, on_piece=None):
        self.pos, self.pair, self.device = pos, pair, device
        self.whole, self.half, self.sems, self.base = whole, half, sems, base
        self.right, self.left, self.far = (pos + 1) % 4, (pos + 3) % 4, (pos + 2) % 4
        self.on_piece = on_piece or (lambda r, p, k: None)

    def push(self, index, ref, device, src=None):
        push(ref if src is None else src, ref, self.sems, self.base + index, device)

    def arrived(self, index, ref):
        settle(ref, self.sems, self.base + index, self.device(self.pos, self.pair)).wait_recv()

    def start(self, own=None):
        ref = self.whole(self.pos, self.pair)
        self.push(1, ref, self.device(self.right, self.pair), own)
        self.push(2, ref, self.device(self.left, self.pair), own)
        self.push(0, ref, self.device(self.pos, 1 - self.pair), own)
        self.on_piece(self.pos, self.pair, 0)

    def forward(self, first, pair, slot):
        self.arrived(first, self.whole(self.left, pair))
        self.push(first + 2, self.half(self.left, pair, 0), self.device(self.right, self.pair))
        self.on_piece(self.left, pair, slot)
        self.arrived(first + 1, self.whole(self.right, pair))
        self.push(first + 3, self.half(self.right, pair, 1), self.device(self.left, self.pair))
        self.on_piece(self.right, pair, slot + 1)

    def forward_ring(self):
        self.forward(1, self.pair, 1)

    def spread_pair(self):
        ref = self.whole(self.pos, 1 - self.pair)
        self.arrived(0, ref)
        self.push(5, ref, self.device(self.right, self.pair))
        self.push(6, ref, self.device(self.left, self.pair))
        self.on_piece(self.pos, 1 - self.pair, 3)

    def forward_pair(self):
        self.forward(5, 1 - self.pair, 4)

    def finish(self):
        for first, pair, slot in ((3, self.pair, 6), (7, 1 - self.pair, 7)):
            self.arrived(first, self.half(self.far, pair, 0))
            self.arrived(first + 1, self.half(self.far, pair, 1))
            self.on_piece(self.far, pair, slot)

    def drain(self):
        for index in range(9):
            ref = self.whole(self.pos, self.pair)
            if index in (3, 4, 7, 8):
                ref = self.half(self.pos, self.pair, 0)
            settle(ref, self.sems, self.base + index, self.device(self.pos, self.pair)).wait_send()


class RingGather(Gather):
    def start(self, own=None):
        ref = self.whole(self.pos, self.pair)
        self.push(1, ref, self.device(self.right, self.pair), own)
        self.push(2, ref, self.device(self.left, self.pair), own)
        self.push(0, ref, self.device(self.pos, 1 - self.pair), own)
        self.on_piece(self.pos, self.pair, 0)

    def forward_ring(self):
        mate = self.device(self.pos, 1 - self.pair)
        self.arrived(1, self.whole(self.left, self.pair))
        self.push(3, self.half(self.left, self.pair, 0), self.device(self.right, self.pair))
        self.push(5, self.whole(self.left, self.pair), mate)
        self.on_piece(self.left, self.pair, 1)
        self.arrived(2, self.whole(self.right, self.pair))
        self.push(4, self.half(self.right, self.pair, 1), self.device(self.left, self.pair))
        self.push(6, self.whole(self.right, self.pair), mate)
        self.on_piece(self.right, self.pair, 2)

    def spread_far(self):
        self.arrived(3, self.half(self.far, self.pair, 0))
        self.arrived(4, self.half(self.far, self.pair, 1))
        ref = self.whole(self.far, self.pair)
        self.push(7, ref, self.device(self.pos, 1 - self.pair))
        self.on_piece(self.far, self.pair, 3)

    def finish(self):
        pieces = ((0, self.pos), (5, self.left), (6, self.right), (7, self.far))
        for slot, (index, r) in enumerate(pieces):
            self.arrived(index, self.whole(r, 1 - self.pair))
            self.on_piece(r, 1 - self.pair, 4 + slot)

    def drain(self):
        for index in range(8):
            ref = self.whole(self.pos, self.pair)
            if index in (3, 4):
                ref = self.half(self.pos, self.pair, 0)
            settle(ref, self.sems, self.base + index, self.device(self.pos, self.pair)).wait_send()


class MixedGather(RingGather):
    def forward_ring(self):
        self.arrived(1, self.whole(self.left, self.pair))
        self.push(3, self.half(self.left, self.pair, 0), self.device(self.right, self.pair))
        self.arrived(2, self.whole(self.right, self.pair))
        self.push(4, self.half(self.right, self.pair, 1), self.device(self.left, self.pair))

    def spread_pair(self):
        ref = self.whole(self.pos, 1 - self.pair)
        self.arrived(0, ref)
        self.push(5, ref, self.device(self.right, self.pair))
        self.push(6, ref, self.device(self.left, self.pair))

    def finish(self):
        for index, r in ((5, self.left), (6, self.right), (7, self.far)):
            self.arrived(index, self.whole(r, 1 - self.pair))


class RowScatter:
    def __init__(self, at, part, far_in, other_in, half_in, full_in, pair_in, pair_out, sems, base=0):
        self.at, self.part, self.sems, self.base = at, part, sems, base
        self.far_in, self.other_in, self.half_in, self.full_in = far_in, other_in, half_in, full_in
        self.pair_in, self.pair_out = pair_in, pair_out
        self.right, self.left, self.far = (at.x + 1) % 4, (at.x + 3) % 4, (at.x + 2) % 4

    def rows(self, x, plane, half=None):
        start = (x * 2 + plane) * OWN
        if half is None:
            return pl.ds(pl.multiple_of(start, OWN), OWN)
        return pl.ds(pl.multiple_of(start + half * (OWN // 2), OWN // 2), OWN // 2)

    def push(self, index, src, dst, device):
        push(src, dst, self.sems, self.base + index, device)

    def arrived(self, index, ref):
        settle(ref, self.sems, self.base + index, self.at.row(self.at.x)).wait_recv()

    def add(self, rows, box):
        self.part[rows, :] = (self.part[rows, :].astype(F32) + box[...].astype(F32)).astype(BF)

    def zero(self):
        other = 1 - self.at.zh
        self.push(0, self.part.at[self.rows(self.far, other)], self.far_in, self.at.mate())

    def sides(self):
        other = 1 - self.at.zh
        for side, x in enumerate((self.right, self.left)):
            src = self.part.at[self.rows(x, other)]
            self.push(1 + side, src, self.other_in.at[side], self.at.row(x))

    def first(self):
        plane = self.at.zh
        self.arrived(0, self.far_in)
        self.add(self.rows(self.far, plane), self.far_in)
        for side, x in enumerate((self.right, self.left)):
            src = self.part.at[self.rows(self.far, plane, side)]
            self.push(3 + side, src, self.half_in.at[side], self.at.row(x))

    def second(self):
        plane = self.at.zh
        for side, x in enumerate((self.right, self.left)):
            box = self.half_in.at[side]
            self.arrived(3 + side, box)
            self.add(self.rows(x, plane, side), box)
            src = self.part.at[self.rows(x, plane)]
            self.push(5 + side, src, self.full_in.at[side], self.at.row(x))

    def own(self, plane, boxes, index):
        for side in range(2):
            self.arrived(index + side, boxes.at[side])
        total = self.part[self.rows(self.at.x, plane), :].astype(F32)
        return total + boxes[0].astype(F32) + boxes[1].astype(F32)

    def third(self):
        self.pair_out[...] = self.own(1 - self.at.zh, self.other_in, 1).astype(BF)
        self.push(7, self.pair_out, self.pair_in, self.at.mate())

    def fourth(self):
        total = self.own(self.at.zh, self.full_in, 5)
        self.arrived(7, self.pair_in)
        return total + self.pair_in[...].astype(F32)

    def drain(self):
        for index in range(8):
            box = self.half_in.at[0] if index in (3, 4) else self.pair_in
            settle(box, self.sems, self.base + index, self.at.row(self.at.x)).wait_send()


def scatter_scratch():
    vmem = pltpu.VMEM
    return [
        vmem((TOK, D), BF),
        vmem((OWN, D), BF),
        vmem((2, OWN, D), BF),
        vmem((2, OWN // 2, D), BF),
        vmem((2, OWN, D), BF),
        vmem((OWN, D), BF),
        vmem((OWN, D), BF),
    ] + dma_sems(9)


class PieceScatter:
    def __init__(self, at, acc, boxes, sems, base):
        self.at, self.acc, self.sems, self.base = at, acc, sems, base
        self.half_in, self.full_in, self.pair_in, self.pair_out, self.pack = boxes
        self.right, self.left = (at.y + 1) % 4, (at.y + 3) % 4
        self.planes = (1 - at.zl, at.zl)

    def push(self, index, src, dst, y, zl):
        device = ((y * 2 + zl) * 2 + self.at.core, self.at.x, self.at.zh)
        push(src, dst, self.sems, self.base + index, device)

    def arrived(self, index, ref):
        settle(ref, self.sems, self.base + index, self.at.row(self.at.x)).wait_recv()

    def first(self):
        far = (self.at.y + 2) % 4
        for role, plane in enumerate(self.planes):
            for side, y in enumerate((self.right, self.left)):
                self.push(
                    role * 4 + side,
                    self.acc.at[side, :, far * 2 + plane],
                    self.half_in.at[role, side],
                    y,
                    self.at.zl,
                )

    def second(self, role):
        plane = self.planes[role]
        for side, y in enumerate((self.right, self.left)):
            self.arrived(role * 4 + side, self.half_in.at[role, side])
            q = y * 2 + plane
            for b in range(self.acc.shape[1]):
                self.acc[side, b, q] = (
                    self.acc[side, b, q].astype(F32) + self.half_in[role, side, b].astype(F32)
                ).astype(BF)
            self.push(
                role * 4 + 2 + side,
                self.acc.at[:, :, q],
                self.full_in.at[role, side],
                y,
                self.at.zl,
            )

    def total(self, role, out, extra=None):
        for side in range(2):
            self.arrived(role * 4 + 2 + side, self.full_in.at[role, side])
        q = self.at.y * 2 + self.planes[role]
        for a in range(2):
            for b in range(self.acc.shape[1]):
                value = self.acc[a, b, q].astype(F32)
                value += self.full_in[role, 0, a, b].astype(F32)
                value += self.full_in[role, 1, a, b].astype(F32)
                if extra is not None:
                    value += extra[a, b].astype(F32)
                out[a, b] = value.astype(BF)

    def third(self):
        self.total(0, self.pair_out)
        self.push(8, self.pair_out, self.pair_in, self.at.y, 1 - self.at.zl)

    def fourth(self):
        self.arrived(8, self.pair_in)
        self.total(1, self.pack, self.pair_in)

    def drain(self):
        for index in range(9):
            box = self.full_in.at[0, 0] if index % 4 > 1 else self.half_in.at[0, 0]
            if index == 8:
                box = self.pair_in
            settle(box, self.sems, self.base + index, self.at.row(self.at.x)).wait_send()


def piece_scratch(blocks, rows, width):
    vmem = pltpu.VMEM
    return [
        vmem((2, blocks, 8, rows, width), BF),
        vmem((2, 2, blocks, rows, width), BF),
        vmem((2, 2, 2, blocks, rows, width), BF),
        vmem((2, blocks, rows, width), BF),
        vmem((2, blocks, rows, width), BF),
        vmem((2, blocks, rows, width), BF),
    ]


def row_gather(at, ref, sems, base=0, kind=MixedGather):
    def whole(x, plane):
        return ref.at[pl.ds(pl.multiple_of((x * 2 + plane) * OWN, OWN), OWN)]

    def half(x, plane, side):
        start = (x * 2 + plane) * OWN + side * (OWN // 2)
        return ref.at[pl.ds(pl.multiple_of(start, OWN // 2), OWN // 2)]

    return kind(at.x, at.zh, lambda x, plane: (at.dp, x, plane), whole, half, sems, base)


def column_gather(at, ref, sems, base=0, kind=MixedGather):
    def columns(x, plane):
        return pl.ds(pl.multiple_of((x * 2 + plane) * 256, 256), 256)

    def whole(x, plane):
        return ref.at[:, columns(x, plane)]

    def half(x, plane, side):
        return ref.at[pl.ds(side * 256, 256), columns(x, plane)]

    return kind(at.x, at.zh, lambda x, plane: (at.dp, x, plane), whole, half, sems, base)


def front_kernel(
    x_in, cot_in, gain1, shift1, gain2, shift2, bias, seg, qkv_w, out_w, gu_w, down_w,
    cot_out, par_out, normed_out, qkv_out, att_out, max_out, sum_out, tab_out, own_out,
    seg_col, seg_row, grad_hidden,
    hidden_out, normed2_out, qkv_s_out, out_s_out, gu_s, down_s_out, norm_sib, cot_sib, att_sib,
    x_v, normed, par, par_in, proj, tables, qkv_s, out_s, down_s, cot, normed2, rows, raw, split,
    part, far_in, other_in, half_in, full_in, pair_in, pair_out, rs_send, rs_recv,
    par_send, par_recv, act_send, act_recv, a_send, a_recv, dp_send, dp_recv, core_send, core_recv,
    sib_send, sib_recv, local,
):
    at = Place()
    dp, x, core = at.dp, at.x, at.core
    raw_copy = pltpu.make_async_copy(gu_w.at[pl.ds(dp * 32, 32)], raw, local.at[13])
    raw_copy.start()
    par_in[...] = jnp.zeros_like(par_in)
    for j, vector in enumerate((gain1, shift1, gain2, shift2)):
        par_in[j : j + 1, :] = vector[...].reshape(1, 256)
    greet(group_others(at) + at.near_replicas())
    act, step_a, step_dp = (act_send, act_recv), (a_send, a_recv), (dp_send, dp_recv)
    step_core, step_par = (core_send, core_recv), (par_send, par_recv)
    slabs = (qkv_s, out_s, gu_s, down_s)

    def source(k, xt):
        if k == 0:
            return qkv_w.at[pl.ds(dp * 32, 32), pl.ds(pl.multiple_of(xt * WIDE, WIDE), WIDE)]
        if k == 1:
            return out_w.at[pl.ds(xt * 256 + dp * 16, 16), :]
        start = pl.multiple_of(tile_start(xt) * 128, 128)
        if k == 2:
            return split.at[:, :, pl.ds(start, WIDE)]
        return down_w.at[pl.ds(start + dp * 48, 48), :]

    def landing(k, xs, p):
        if k == 0:
            return qkv_s.at[xs, p]
        if k == 2:
            return gu_s.at[:, xs, p]
        return slabs[k].at[p, :, pl.ds(pl.multiple_of(xs * 512, 512), 512)]

    def replica(y, zl):
        return (y * 2 + zl) * 2 + core

    def whole(k):
        def of(y, zl):
            p = replica(y, zl)
            if k == 0:
                return qkv_s.at[:, p]
            if k == 2:
                return gu_s.at[:, :, p]
            return slabs[k].at[p]

        return of

    def half(k):
        def of(y, zl, side):
            p = replica(y, zl)
            if k == 0:
                return qkv_s.at[pl.ds(side * 2, 2), p]
            if k == 2:
                return gu_s.at[side, :, p]
            return slabs[k].at[p, :, pl.ds(side * 1024, 1024)]

        return of

    core_copies = []

    def to_sibling(k):
        def on_piece(y, zl, slot):
            ref = whole(k)(y, zl)
            core_copies.append(push(ref, ref, step_core, k * 8 + slot, at.sibling()))

        return on_piece

    first = {}

    def send_rows(k):
        for j in (2, 1, 3):
            xt = (x + j) % 4
            first[k, j] = push(
                source(k, xt), landing(k, x, dp), step_a, k * 3 + j - 1, at.row(xt)
            )
        first[k, 0] = pltpu.make_async_copy(source(k, x), landing(k, x, dp), local.at[k])
        first[k, 0].start()

    weights = [
        Gather(
            at.y, at.zl, lambda y, zl: (replica(y, zl), x, at.zh), whole(k), half(k), step_dp, k * 9,
            to_sibling(k),
        )
        for k in range(4)
    ]
    w_qkv, w_out, w_gu, w_down = weights

    def begin(k):
        first[k, 0].wait()
        for j in range(1, 4):
            first[k, j].wait_recv()
        weights[k].start()

    def from_sibling(k):
        ref = whole(k)(at.y, at.zl)
        for slot in range(8):
            settle(ref, step_core, k * 8 + slot, at.sibling()).wait_recv()

    slot = pl.ds(pl.multiple_of(at.g * 256, 256), 256)
    send_rows(0)
    gx = column_gather(at, x_v, act, 0)
    gx.start(x_in)
    par_copies = []
    for j, device in enumerate(group_others(at)):
        par_copies.append(push(par_in, par.at[:, slot], step_par, j, device))
    own = [
        pltpu.make_async_copy(x_in, x_v.at[:, slot], local.at[4]),
        pltpu.make_async_copy(par_in, par.at[:, slot], local.at[5]),
        pltpu.make_async_copy(cot_in, cot.at[:, slot], local.at[6]),
    ]
    for copy in own:
        copy.start()
    line = seg[...].reshape(1, TOK).astype(F32)
    seg_row[...] = jnp.broadcast_to(line, (8, TOK))
    seg_col[...] = jnp.transpose(jnp.broadcast_to(line, (128, TOK)))
    begin(0)
    make_tables(seg_col, seg_row, tables)
    raw_copy.wait()
    both = raw[...]
    split[0] = both[:, 0, :]
    split[1] = both[:, 1, :]
    gx.forward_ring()
    gx.spread_pair()
    w_qkv.forward_ring()
    w_qkv.spread_pair()
    send_rows(1)
    gx.spread_far()
    w_qkv.forward_pair()
    begin(1)
    gx.finish()
    gcot = column_gather(at, cot, act, 9)
    gcot.start(cot_in)
    send_rows(3)
    send_rows(2)
    for copy in own:
        copy.wait()
    for copy in par_copies:
        copy.wait_recv()

    def norm_rows(i, carry):
        block = pl.ds(pl.multiple_of(i * 32, 32), 32)
        scaled, _ = norm(x_v[block, :].astype(F32))
        normed[block, :] = (scaled * par[0:1, :] + par[1:2, :]).astype(BF)
        return carry

    lax.fori_loop(0, TOK // 32, norm_rows, 0)
    w_qkv.finish()
    w_out.forward_ring()
    w_out.spread_pair()
    from_sibling(0)
    outgoing = []

    def put(src, dst, index):
        copy = pltpu.make_async_copy(src, dst, local.at[index])
        copy.start()
        outgoing.append(copy)

    for n in range(3):
        cols = pl.ds(n * 256, 256)
        weight = qkv_s[:, :, :, cols].reshape(D, 256)
        proj[:, cols] = jnp.dot(normed[...], weight, preferred_element_type=F32) + bias[
            cols
        ].reshape(1, 256)
    put(normed, normed_out, 7)
    put(qkv_s, qkv_s_out, 8)
    put(x_v.at[own_rows(at)], own_out, 9)
    put(par, par_out, 10)
    sib = (sib_send, sib_recv)
    sib_copies = []
    for xt in range(4):
        cols = pl.ds(xt * 512 + pl.multiple_of((1 - core) * 256, 256), 256)
        sib_copies.append(push(normed.at[:, cols], norm_sib.at[xt], sib, xt, at.sibling()))
    between = [
        lambda: (w_out.forward_pair(), gcot.forward_ring(), gcot.spread_pair()),
        lambda: (begin(3),),
        lambda: (w_out.finish(),),
        lambda: (gcot.spread_far(),),
    ]
    attend(proj, tables, seg_col, seg_row, qkv_out, att_out, max_out, sum_out, between)
    from_sibling(1)
    put(out_s, out_s_out, 11)
    put(tables, tab_out, 12)
    rs = RowScatter(
        at, part, far_in, other_in, half_in, full_in, pair_in, pair_out, (rs_send, rs_recv)
    )

    def product(xt):
        weight = out_s[...].reshape(256, D)
        block = pl.ds(pl.multiple_of(xt * 128, 128), 128)
        part[block, :] = jnp.dot(att_out[block, :], weight, preferred_element_type=F32).astype(BF)

    product((x + 2) % 4)
    rs.zero()
    product((x + 1) % 4)
    product((x + 3) % 4)
    rs.sides()
    product(x)
    begin(2)
    w_down.forward_ring()
    rs.first()
    w_down.spread_pair()
    rs.third()
    rs.second()
    w_gu.forward_ring()
    w_gu.spread_pair()
    gcot.finish()
    put(cot, cot_out, 14)
    sib_copies.append(push(cot, cot_sib, sib, 4, at.sibling()))
    cols = pl.ds(pl.multiple_of((1 - core) * 128, 128), 128)
    sib_copies.append(push(att_out.at[:, cols], att_sib, sib, 5, at.sibling()))
    hidden_in = rs.fourth() + x_v[own_rows(at), :].astype(F32)
    hidden_out[...] = hidden_in
    scaled, _ = norm(hidden_in)
    rows[...] = (scaled * par[2:3, :] + par[3:4, :]).astype(BF)
    normed2[own_rows(at), :] = rows[...]
    gn = row_gather(at, normed2, act, 18)
    gn.start(rows)
    w_down.forward_pair()
    gn.forward_ring()
    gn.spread_pair()
    w_gu.forward_pair()
    w_down.finish()
    from_sibling(3)
    put(down_s, down_s_out, 15)
    for n in range(3):
        weight = down_s[...].reshape(WIDE, D)[n * 256 : (n + 1) * 256]
        grad_hidden[:, pl.ds(n * 256, 256)] = lax.dot_general(
            cot[...], weight, ROWS_BY_COLS, preferred_element_type=F32
        ).astype(BF)
    gn.spread_far()
    w_gu.finish()
    from_sibling(2)
    gn.finish()
    put(normed2, normed2_out, 16)
    for k in range(4):
        for j in range(1, 4):
            first[k, j].wait_send()
        weights[k].drain()
    for copy in core_copies + par_copies:
        copy.wait_send()
    for copy in sib_copies:
        copy.wait()
    for program in (gx, gcot, gn, rs):
        program.drain()
    for copy in outgoing:
        copy.wait()


def front(*operands):
    shape = jax.ShapeDtypeStruct
    vmem = pltpu.VMEM
    return pl.pallas_call(
        front_kernel,
        out_shape=(
            shape((TOK, D), BF),
            shape((8, D), F32),
            shape((TOK, D), BF),
            shape((TOK, WIDE), BF),
            shape((TOK, 256), BF),
            shape((TOK, 128), F32),
            shape((TOK, 128), F32),
            shape((3, TOK, 384), F32),
            shape((OWN, D), BF),
            shape((TOK, 128), F32),
            shape((8, TOK), F32),
            shape((TOK, WIDE), BF),
            shape((OWN, D), F32),
            shape((TOK, D), BF),
            shape((4, 16, 32, WIDE), BF),
            shape((16, 16, D), BF),
            shape((2, 4, 16, 32, WIDE), BF),
            shape((16, 48, D), BF),
            shape((4, TOK, 256), BF),
            shape((TOK, D), BF),
            shape((TOK, 128), BF),
        ),
        in_specs=[IN_ANY] * 2 + [IN_VMEM] * 6 + [IN_ANY] * 4,
        out_specs=(IN_ANY,) * 3
        + (IN_VMEM,) * 4
        + (IN_ANY,) * 2
        + (IN_VMEM,) * 4
        + (IN_ANY,) * 8,
        scratch_shapes=[
            vmem((TOK, D), BF),
            vmem((TOK, D), BF),
            vmem((8, D), F32),
            vmem((8, 256), F32),
            vmem((TOK, WIDE), F32),
            vmem((3, TOK, 384), F32),
            vmem((4, 16, 32, WIDE), BF),
            vmem((16, 16, D), BF),
            vmem((16, 48, D), BF),
            vmem((TOK, D), BF),
            vmem((TOK, D), BF),
            vmem((OWN, D), BF),
            vmem((32, 2, 2816), BF),
            vmem((2, 32, 2816), BF),
        ]
        + scatter_scratch()
        + dma_sems(7)
        + dma_sems(27)
        + dma_sems(12)
        + dma_sems(36)
        + dma_sems(32)
        + dma_sems(6)
        + [pltpu.SemaphoreType.DMA((17,))],
        compiler_params=params(1),
        name="front",
    )(*operands)


def own_rows(at):
    return pl.ds(pl.multiple_of(at.g * OWN, OWN), OWN)


def columns_of(rows, g):
    return rows.at[:, pl.ds(pl.multiple_of(g * 256, 256), 256)]


def start_columns(at, rows, full, sems, base, local):
    pltpu.make_async_copy(columns_of(rows, at.g), full.at[own_rows(at)], local).start()
    for k in range(1, 8):
        g = (at.g + k) % 8
        push(columns_of(rows, g), full.at[own_rows(at)], sems, base + k - 1, at.group(g))


def finish_columns(at, rows, full, sems, base, local):
    pltpu.make_async_copy(columns_of(rows, at.g), full.at[own_rows(at)], local).wait()
    for k in range(7):
        copy = settle(columns_of(rows, at.g), sems, base + k, at.group(at.g))
        copy.wait_send()
        copy.wait_recv()


def norm(value):
    mean = jnp.mean(value, axis=1, keepdims=True)
    square = jnp.mean(value * value, axis=1, keepdims=True)
    inverse = lax.rsqrt(square - mean * mean + EPSILON)
    return (value - mean) * inverse, inverse


def norm_back(grad, scaled, inverse, gain):
    inner = grad * gain
    mean = jnp.mean(inner, axis=1, keepdims=True)
    along = jnp.mean(inner * scaled, axis=1, keepdims=True)
    return inverse * (inner - mean - scaled * along)


def rotary(value, tables, sign):
    width = value.shape[1]
    return (
        value * tables[0]
        + pltpu.roll(value, width - 8, 1) * (sign * tables[1])
        + pltpu.roll(value, 8, 1) * (sign * tables[2])
    )


def make_tables(seg_col, seg_row, tables):
    half = ROT // 2
    for block in range(4):
        rows = pl.ds(block * 128, 128)
        places = lax.broadcasted_iota(jnp.int32, (128, 128), 0) + block * 128
        before = jnp.where(seg_row[0:1, :] < seg_col[rows, 0:1], 1.0, 0.0)
        starts = jnp.sum(before, axis=1, keepdims=True)
        offsets = places.astype(F32) - starts
        lane = lax.broadcasted_iota(jnp.int32, (128, 128), 1)
        entry = lane % HD
        power = (entry % half).astype(F32) * (-2.0 * math.log(10000.0) / ROT)
        angles = offsets * jnp.exp(power)
        cosine, sine = jnp.cos(angles), jnp.sin(angles)
        keep = jnp.where(entry < ROT, cosine, 1.0)
        fore = jnp.where(entry < half, -sine, 0.0)
        back = jnp.where((entry >= half) & (entry < ROT), sine, 0.0)
        for j, (table, rest) in enumerate(((keep, 1.0), (fore, 0.0), (back, 0.0))):
            low = lane < HD
            tables[j, rows, 0:128] = table
            tables[j, rows, 128:256] = jnp.where(low, rest, table)
            tables[j, rows, 256:384] = jnp.where(low, table, rest)


def head_part(value, head, kind):
    start = head * 3 * HD + kind * HD
    return value[:, start : start + HD]


def allowed(seg_col, seg_row, block, keys):
    start = block * 128
    rows = lax.broadcasted_iota(jnp.int32, (128, keys), 0) + start
    cols = lax.broadcasted_iota(jnp.int32, (128, keys), 1)
    same = seg_col[start : start + 128, 0:1] == seg_row[0:1, :keys]
    return (cols <= rows) & same


def attend(proj, tables, seg_col, seg_row, qkv_out, att_out, max_out, sum_out, between):
    scale = 1.0 / math.sqrt(HD)
    for half in range(2):
        cols = pl.ds(half * 384, 384)
        tab = (tables[0], tables[1], tables[2])
        qkv_out[:, cols] = rotary(proj[:, cols], tab, 1.0).astype(BF)
    for block in range(4):
        keys = (block + 1) * 128
        rows = pl.ds(block * 128, 128)
        mask = allowed(seg_col, seg_row, block, keys)
        outs, maxima, totals = [], [], []
        for head in range(HEADS):
            q = head_part(qkv_out[rows, :], head, 0)
            k = head_part(qkv_out[pl.ds(0, keys), :], head, 1)
            v = head_part(qkv_out[pl.ds(0, keys), :], head, 2)
            score = lax.dot_general(q, k, ROWS_BY_COLS, preferred_element_type=F32) * scale
            score = jnp.where(mask, score, -1e30)
            top = jnp.max(score, axis=1, keepdims=True)
            raised = jnp.exp(score - top)
            total = jnp.sum(raised, axis=1, keepdims=True)
            low = (raised / total).astype(BF)
            outs.append(jnp.dot(low, v, preferred_element_type=F32))
            maxima.append(top)
            totals.append(total)
        att_out[rows, :] = jnp.concatenate(outs, axis=1).astype(BF)
        for head in range(HEADS):
            max_out[rows, head : head + 1] = maxima[head]
            sum_out[rows, head : head + 1] = totals[head]
        if block < len(between):
            between[block]()


def attend_back(
    qkv, grad_att, tables, seg_col, seg_row, maxima, totals, grad_out, pieces, between
):
    scale = 1.0 / math.sqrt(HD)
    pieces[...] = jnp.zeros_like(pieces)
    for block in range(4):
        keys = (block + 1) * 128
        rows = pl.ds(block * 128, 128)
        upto = pl.ds(0, keys)
        mask = allowed(seg_col, seg_row, block, keys)
        for head in range(HEADS):
            q = head_part(qkv[rows, :], head, 0)
            k = head_part(qkv[upto, :], head, 1)
            v = head_part(qkv[upto, :], head, 2)
            grad = grad_att[rows, :][:, head * HD : (head + 1) * HD]
            score = lax.dot_general(q, k, ROWS_BY_COLS, preferred_element_type=F32) * scale
            score = jnp.where(mask, score, -1e30)
            probs = jnp.exp(score - maxima[rows, head : head + 1]) / totals[rows, head : head + 1]
            grad_probs = lax.dot_general(grad, v, ROWS_BY_COLS, preferred_element_type=F32)
            delta = jnp.sum(probs * grad_probs, axis=1, keepdims=True)
            grad_score = (probs * (grad_probs - delta)).astype(BF)
            pieces[head, 0, rows, :] = (
                jnp.dot(grad_score, k, preferred_element_type=F32) * scale
            )
            pieces[head, 1, upto, :] += (
                lax.dot_general(grad_score, q, OVER_ROWS, preferred_element_type=F32) * scale
            )
            pieces[head, 2, upto, :] += lax.dot_general(
                probs.astype(BF), grad, OVER_ROWS, preferred_element_type=F32
            )
        between[block]()
    tab = (tables[0], tables[1], tables[2])
    sums = []
    for half in range(2):
        parts = [pieces[half * 2 + j // 3, j % 3] for j in range(6)]
        cols = pl.ds(half * 384, 384)
        low = rotary(jnp.concatenate(parts, axis=1), tab, -1.0).astype(BF)
        grad_out[:, cols] = low
        sums.append(jnp.sum(low.astype(F32), axis=0, keepdims=True))
    return jnp.concatenate(sums, axis=1)


def back_kernel(
    n2_h, gu_h, down_h, out_h, qkvs_h, cot_h, normed_h, tab_h, norm_sib_h, cot_sib_h, att_sib_h,
    hidden_in, par, att, qkv, seg_col, seg_row, maxima, totals, x_own, grad_hidden,
    act_out, input_out, gu_f, qkv_f, down_f, out_f, small_f,
    n2, n2_sib, cot, cot_sib, gb, gb_sib, att_sib,
    hidden, hidden_sib, gg, gg_sib, gate_up_sib, grad_up, gp_sib, grad_att, grad_in,
    out_s, rows, sums, ln_t, small_t,
    part, part2,
    *rest,
):
    at = Place()
    others = [at.replica((at.dp + k) % 16) for k in range(1, 16)]
    core, q, x = at.core, at.q, at.x
    cq = core * 8 + q
    rest = list(rest)

    def take(amount):
        head, rest[:] = rest[:amount], rest[amount:]
        return head

    boxes = [take(6) for _ in range(2)]
    boxes.append(boxes[0])
    arrays = [take(6) for _ in range(4)]
    (gu_a, qkv_a, down_a, out_a) = [a[0] for a in arrays]
    packs = [a[-1] for a in arrays]
    rs_sems, act_sems, sib_sems = take(2), take(2), take(2)
    dps_sems, row_sems, dpg_sems, core_sems = take(2), take(2), take(2), take(2)
    ln_sems, small_sems = take(2), take(2)
    (local,) = take(1)
    finals = (gu_f, qkv_f, down_f, out_f)

    loads = {}

    def load(name, src, dst, index):
        loads[name] = lambda: pltpu.make_async_copy(src, dst, local.at[index])
        loads[name]().start()

    def columns(c, xt):
        return pl.ds(pl.multiple_of(xt * 512 + c * 256, 256), 256)

    exchange = {}

    def to_sibling(name, src, dst, index):
        exchange[name] = (dst, index)
        push(src, inbox(name), sib_sems, index, at.sibling())

    def inbox(name):
        ref = exchange[name][0]
        return ref.at[name[1]] if isinstance(name, tuple) else ref

    def exchanged(name):
        settle(inbox(name), sib_sems, exchange[name][1], at.sibling()).wait_recv()

    def load_cot_sib(a):
        cols = pl.ds(a * 512, 512)
        load(("cot_sib", a), cot_sib_h.at[:, cols], cot_sib.at[a % 2], 3 if a % 2 else 18)

    load("n2", n2_h, n2, 0)
    def pack_for(k, xt):
        if k == 0:
            return packs[0].at[:, xt]
        if k == 1:
            return packs[1].at[xt // 2, xt % 2]
        return packs[k].at[xt // 2, 0, :, pl.ds(pl.multiple_of((xt % 2) * 512, 512), 512)]

    def landing(k, xs, p):
        if k == 0:
            return gu_f.at[xs, :, p]
        if k == 1:
            return qkv_f.at[p, :, pl.ds(pl.multiple_of(xs * WIDE, WIDE), WIDE)]
        return finals[k].at[xs, p]

    def slot(y, zl):
        return core * 8 + y * 2 + zl

    def whole(k):
        def of(y, zl):
            p = slot(y, zl)
            if k == 0:
                return gu_f.at[:, :, p]
            if k == 1:
                return qkv_f.at[p]
            return finals[k].at[:, p]

        return of

    def half(k):
        def of(y, zl, side):
            p = slot(y, zl)
            if k == 0:
                return gu_f.at[pl.ds(side * 2, 2), :, p]
            if k == 1:
                return qkv_f.at[p, :, pl.ds(side * 2 * WIDE, 2 * WIDE)]
            return finals[k].at[pl.ds(side * 2, 2), p]

        return of

    def share(k):
        def on_piece(y, zl, index):
            ref = whole(k)(y, zl)
            push(ref, ref, core_sems, k * 8 + index, at.sibling())

        return on_piece

    scatters = [
        PieceScatter(at, arrays[k][0], arrays[k][1:], dps_sems, k * 9) for k in range(4)
    ]
    s_gu, s_qkv, s_down, s_out = scatters
    gathers = [
        (RingGather if k == 2 else Gather)(
            at.y, at.zl, lambda y, zl: ((y * 2 + zl) * 2 + core, x, at.zh), whole(k), half(k),
            dpg_sems, k * 9, share(k),
        )
        for k in range(4)
    ]
    g_gu, g_qkv, g_down, g_out = gathers
    def send_rows(k):
        scatters[k].fourth()
        for j in (2, 1, 3):
            xt = (x + j) % 4
            push(pack_for(k, xt), landing(k, x, cq), row_sems, k * 3 + j - 1, at.row(xt))
        pltpu.make_async_copy(pack_for(k, x), landing(k, x, cq), local.at[12 + k]).start()

    def begin(k):
        pltpu.make_async_copy(pack_for(k, x), landing(k, x, cq), local.at[12 + k]).wait()
        for j in range(3):
            settle(pack_for(k, x), row_sems, k * 3 + j, at.row(x)).wait_recv()
        gathers[k].start()

    rs1, rs2, rs3 = [
        RowScatter(at, p, *boxes[j], rs_sems, j * 9) for j, p in enumerate((part, part2, part))
    ]
    block_of = lambda xt: pl.ds(pl.multiple_of(xt * 128, 128), 128)
    far, right, left = (x + 2) % 4, (x + 1) % 4, (x + 3) % 4
    g_branch = row_gather(at, gb, act_sems, 0)

    def outer_sum(a, b, a_sib, b_sib):
        return lax.dot_general(
            a, b, OVER_ROWS, preferred_element_type=F32
        ) + lax.dot_general(a_sib, b_sib, OVER_ROWS, preferred_element_type=F32)

    def down_grad(a):
        cols = pl.ds(a * 512, 512)
        mine = hidden[:, pl.ds(pl.multiple_of(core * 384, 128), 384)]
        loads["cot_sib", a]().wait()
        down_a[a // 2, 0, :, :, pl.ds((a % 2) * 512, 512)] = (
            outer_sum(mine, cot[:, cols], hidden_sib[...], cot_sib[a % 2])
            .astype(BF)
            .reshape(8, 48, 512)
        )
        if a < 2:
            load_cot_sib(a + 2)

    def feed_forward(gu_s, gate_v, up_v):
        load("gate", gu_h.at[0], gu_s.at[0], 7)
        load("up", gu_h.at[1], gu_s.at[1], 8)
        load("cot", cot_h, cot, 1)
        load("out_s", out_h, out_s, 2)
        greet(group_others(at) + others)
        for xt in range(4):
            to_sibling(("n2", xt), n2_h.at[:, columns(1 - core, xt)], n2_sib, xt)
        for name in ("n2", "gate", "up"):
            loads[name]().wait()
        lane = lax.broadcasted_iota(jnp.int32, (1, 256), 1)

        def chunk(n):
            cols = pl.ds(n * 256, 256)
            gate_v[...] = jnp.dot(n2[...], gu_s[0, :, cols], preferred_element_type=F32)
            up_v[...] = jnp.dot(n2[...], gu_s[1, :, cols], preferred_element_type=F32)
            kept = (lane >= (128 if n == 0 else 0)) | (x < 2)

            def gated(i, carry):
                block = pl.ds(pl.multiple_of(i * 64, 64), 64)
                gate, up = gate_v[block, :], up_v[block, :]
                sig = jax.nn.sigmoid(gate)
                act = gate * sig
                grad = jnp.where(kept, grad_hidden[block, cols].astype(F32), 0.0)
                hidden[block, cols] = jnp.where(kept, act * up, 0.0).astype(BF)
                gg[block, cols] = (grad * up * (sig * (1.0 + gate * (1.0 - sig)))).astype(BF)
                grad_up[block, cols] = (grad * act).astype(BF)
                return carry

            lax.fori_loop(0, 8, gated, 0)

        for n in range(3):
            chunk(n)
        to_sibling(
            "hidden",
            hidden.at[:, pl.ds(pl.multiple_of((1 - core) * 384, 128), 384)],
            hidden_sib,
            5,
        )
        to_sibling("gg", gg, gg_sib, 6)
        to_sibling("up", grad_up, gate_up_sib, 7)

        def product(xt):
            block = block_of(xt)
            value = lax.dot_general(
                gg[block, :], gu_s[0], ROWS_BY_COLS, preferred_element_type=F32
            ) + lax.dot_general(
                grad_up[block, :], gu_s[1], ROWS_BY_COLS, preferred_element_type=F32
            )
            part[block, :] = value.astype(BF)

        product(far)
        rs1.zero()
        product(right)
        product(left)
        rs1.sides()
        rs1.first()
        product(x)

    def down_product(down_s):
        load("down", down_h, down_s, 9)
        loads["down"]().wait()

        def product_two(i, carry):
            block = block_of(i)
            part2[block, :] = jnp.dot(
                hidden[block, :], down_s[...], preferred_element_type=F32
            ).astype(BF)
            return carry

        lax.fori_loop(0, 4, product_two, 0)

    load_cot_sib(0)
    load_cot_sib(1)
    pl.run_scoped(
        feed_forward,
        pltpu.VMEM((2, D, WIDE), BF),
        pltpu.VMEM((TOK, 256), F32),
        pltpu.VMEM((TOK, 256), F32),
    )
    exchanged("gg")
    exchanged("up")
    for xt in range(4):
        exchanged(("n2", xt))

    def gate_up_grad(xt, carry):
        own, sib = n2[:, columns(core, xt)], n2_sib[xt]
        gu_a[0, xt] = outer_sum(own, gg[...], sib, gg_sib[...]).astype(BF).reshape(8, 32, WIDE)
        gu_a[1, xt] = (
            outer_sum(own, grad_up[...], sib, gate_up_sib[...]).astype(BF).reshape(8, 32, WIDE)
        )
        return carry

    lax.fori_loop(0, 4, gate_up_grad, 0)
    s_gu.first()
    rs1.third()
    rs1.second()
    pl.run_scoped(down_product, pltpu.VMEM((WIDE, D), BF))
    load("nh", normed_h, n2, 4)
    load("nh_sib", norm_sib_h, n2_sib, 5)
    load("att_sib", att_sib_h, att_sib, 6)
    loads["cot"]().wait()
    exchanged("hidden")
    down_grad(0)
    scaled, inverse = norm(hidden_in[...])
    grad = rs1.fourth()
    value = cot[own_rows(at), :].astype(F32) + norm_back(grad, scaled, inverse, par[2:3, :])
    rows[0] = value.astype(BF)
    gb[own_rows(at), :] = value.astype(BF)
    g_branch.start(rows.at[0])
    grad_in[...] = value
    sums[...] = jnp.zeros_like(sums)
    sums[2:3, :] = jnp.sum(grad * scaled, axis=0, keepdims=True)
    sums[3:4, :] = jnp.sum(grad, axis=0, keepdims=True)
    s_gu.second(0)
    s_gu.second(1)
    down_grad(1)
    down_grad(2)
    down_grad(3)
    s_down.first()
    g_branch.forward_ring()
    g_branch.spread_pair()
    g_branch.spread_far()
    s_gu.third()
    g_branch.finish()
    to_sibling("gb", gb, gb_sib, 13)
    settle(inbox("gg"), sib_sems, exchange["gg"][1], at.sibling()).wait_send()
    gp = gg

    def qkv_grad(xt, carry):
        qkv_a[xt // 2, xt % 2] = (
            outer_sum(n2[:, columns(core, xt)], gp[...], n2_sib[xt], gp_sib[...])
            .astype(BF)
            .reshape(8, 32, WIDE)
        )
        return carry

    def out_grad():
        exchanged("gb")
        loads["att_sib"]().wait()
        mine = att[:, pl.ds(pl.multiple_of(core * 128, 128), 128)]
        for a in range(2):
            cols = pl.ds(a * 1024, 1024)
            out_a[a, 0] = (
                outer_sum(mine, gb[:, cols], att_sib[...], gb_sib[:, cols])
                .astype(BF)
                .reshape(8, 16, 1024)
            )
        s_out.first()

    def attention(tables, pieces, qkv_s):
        load("tab", tab_h, tables, 10)
        load("qkv_s", qkvs_h, qkv_s, 11)
        loads["out_s"]().wait()
        grad_att[...] = lax.dot_general(
            gb[...], out_s[...].reshape(256, D), ROWS_BY_COLS, preferred_element_type=F32
        ).astype(BF)
        rs2.zero()
        rs2.sides()
        s_down.second(0)
        s_down.second(1)
        loads["tab"]().wait()

        between = [
            lambda: (send_rows(0),),
            lambda: (out_grad(), rs2.first(), rs2.third()),
            lambda: (begin(0),),
            lambda: (s_down.third(),),
        ]
        bias_sums = attend_back(
            qkv, grad_att, tables, seg_col, seg_row, maxima, totals, gp, pieces, between
        )
        to_sibling("gp", gp, gp_sib, 14)
        loads["qkv_s"]().wait()
        rs1.drain()

        def product(xt):
            block = block_of(xt)
            weight = qkv_s[...].reshape(D, WIDE)
            part[block, :] = lax.dot_general(
                gp[block, :], weight, ROWS_BY_COLS, preferred_element_type=F32
            ).astype(BF)

        product(far)
        rs3.zero()
        product(right)
        product(left)
        rs3.sides()
        exchanged("gp")
        loads["nh"]().wait()
        loads["nh_sib"]().wait()
        lax.fori_loop(0, 4, qkv_grad, 0)
        s_qkv.first()
        product(x)
        sums[4:7, 0:256] = jnp.concatenate([bias_sums[:, j * 256 : (j + 1) * 256] for j in range(3)])

    pl.run_scoped(
        attention,
        pltpu.VMEM((3, TOK, 384), F32),
        pltpu.VMEM((HEADS, 3, TOK, HD), F32),
        pltpu.VMEM((4, 16, 32, WIDE), BF),
    )
    rs3.first()
    g_gu.forward_ring()
    g_gu.spread_pair()
    rs3.third()
    s_out.second(0)
    s_out.second(1)
    rs3.second()
    rs2.second()
    s_qkv.second(0)
    s_qkv.second(1)
    send_rows(2)
    scaled, inverse = norm(x_own[...].astype(F32))
    grad = rs3.fourth()
    value = grad_in[...] + norm_back(grad, scaled, inverse, par[0:1, :])
    rows[2] = value.astype(BF)
    start_columns(at, rows.at[2], input_out, act_sems, 16, local.at[17])
    sums[0:1, :] = jnp.sum(grad * scaled, axis=0, keepdims=True)
    sums[1:2, :] = jnp.sum(grad, axis=0, keepdims=True)
    own_columns = pl.ds(pl.multiple_of(at.g * 256, 256), 256)
    ln_copies = []
    for j in range(1, 8):
        g = (at.g + j) % 8
        ln_copies.append(
            push(
                sums.at[pl.ds(0, 4), pl.ds(pl.multiple_of(g * 256, 256), 256)],
                ln_t.at[j - 1],
                ln_sems,
                j - 1,
                at.group(g),
            )
        )
    s_qkv.third()
    s_out.third()
    begin(2)
    g_gu.forward_pair()
    total = rs2.fourth() + hidden_in[...]
    rows[1] = total.astype(BF)
    start_columns(at, rows.at[1], act_out, act_sems, 9, local.at[16])
    total = sums[0:4, own_columns]
    for j in range(7):
        ln_copies[j].wait_recv()
        total += ln_t[j]
    small_t[pl.ds(at.dp, 1), 0:4] = total[None]
    small_t[pl.ds(at.dp, 1), 4:8] = sums[4:8, 0:256][None]
    small_copies = [
        push(small_t.at[at.dp], small_t.at[at.dp], small_sems, j, device)
        for j, device in enumerate(others)
    ]
    send_rows(1)
    send_rows(3)
    g_down.forward_ring()
    begin(1)
    begin(3)
    g_gu.finish()
    g_down.spread_far()
    g_qkv.forward_ring()
    g_qkv.spread_pair()
    g_out.forward_ring()
    g_out.spread_pair()
    g_qkv.forward_pair()
    g_out.forward_pair()
    g_down.finish()
    for copy in small_copies:
        copy.wait_recv()
    result = small_t[0]
    for j in range(1, 16):
        result += small_t[j]
    small_f[...] = result
    g_out.finish()
    g_qkv.finish()
    for k in range(4):
        ref = whole(k)(at.y, at.zl)
        for index in range(8):
            settle(ref, core_sems, k * 8 + index, at.sibling()).wait_recv()
            settle(ref, core_sems, k * 8 + index, at.sibling()).wait_send()
        scatters[k].drain()
        gathers[k].drain()
        for j in range(3):
            settle(pack_for(k, x), row_sems, k * 3 + j, at.row(x)).wait_send()
    for copy in ln_copies + small_copies:
        copy.wait_send()
    for name in exchange:
        if name == "gg":
            continue
        settle(inbox(name), sib_sems, exchange[name][1], at.sibling()).wait_send()
    g_branch.drain()
    rs2.drain()
    rs3.drain()
    finish_columns(at, rows.at[1], act_out, act_sems, 9, local.at[16])
    finish_columns(at, rows.at[2], input_out, act_sems, 16, local.at[17])


def back(
    n2, gu_s, down_s, out_s, qkv_s, cot, normed, tables, norm_sib, cot_sib, att_sib,
    hidden_in, par, att, qkv, seg_col, seg_row, maxima, totals, x_own, grad_hidden,
):
    shape = jax.ShapeDtypeStruct
    vmem = pltpu.VMEM
    wide = vmem((TOK, D), BF)
    inner = vmem((TOK, WIDE), BF)
    quarters = vmem((4, TOK, 256), BF)
    box = scatter_scratch()[1:7]
    return pl.pallas_call(
        back_kernel,
        out_shape=(
            shape((TOK, 256), BF),
            shape((TOK, 256), BF),
            shape((4, 2, 16, 32, WIDE), BF),
            shape((16, 32, 4 * WIDE), BF),
            shape((4, 16, 48, 512), BF),
            shape((4, 16, 16, 512), BF),
            shape((8, 256), F32),
        ),
        in_specs=[IN_ANY] * 11 + [IN_VMEM] * 10,
        out_specs=(IN_ANY,) * 6 + (IN_VMEM,),
        scratch_shapes=[
            wide, quarters, wide, vmem((2, TOK, 512), BF), wide, wide, vmem((TOK, 128), BF),
            inner, vmem((TOK, 384), BF), inner, inner, inner, inner, inner,
            vmem((TOK, 256), BF), vmem((OWN, D), F32),
            vmem((16, 16, D), BF), vmem((3, OWN, D), BF), vmem((8, D), F32),
            vmem((7, 4, 256), F32), vmem((16, 8, 256), F32),
            wide, wide,
        ]
        + box * 2
        + piece_scratch(4, 32, WIDE)
        + piece_scratch(2, 32, WIDE)
        + piece_scratch(1, 48, 1024)
        + piece_scratch(1, 16, 1024)
        + dma_sems(27)
        + dma_sems(23)
        + dma_sems(15)
        + dma_sems(36)
        + dma_sems(12)
        + dma_sems(36)
        + dma_sems(32)
        + dma_sems(7)
        + dma_sems(15)
        + [pltpu.SemaphoreType.DMA((19,))],
        compiler_params=params(2),
        name="back",
    )(
        n2, gu_s, down_s, out_s, qkv_s, cot, normed, tables, norm_sib, cot_sib, att_sib,
        hidden_in, par, att, qkv, seg_col, seg_row, maxima, totals, x_own, grad_hidden,
    )


def widen_gate_up_kernel(low, out):
    for j in range(2):
        shares = [low[x, j] for x in range(4)]
        out[:, j, 0:768] = shares[0].astype(F32)
        out[:, j, 768:1536] = shares[1].astype(F32)
        out[:, j, 1536:2176] = shares[2][:, 128:].astype(F32)
        out[:, j, 2176:2816] = shares[3][:, 128:].astype(F32)


def widen_gate_up(low):
    return pl.pallas_call(
        widen_gate_up_kernel,
        out_shape=jax.ShapeDtypeStruct((512, 2, 2816), F32),
        grid=(8,),
        in_specs=[pl.BlockSpec((4, 2, 64, WIDE), lambda i: (0, 0, i, 0))],
        out_specs=pl.BlockSpec((64, 2, 2816), lambda i: (i, 0, 0)),
        compiler_params=pltpu.CompilerParams(vmem_limit_bytes=VMEM_LIMIT),
        name="widen_gate_up",
    )(low)


def on_device(
    block_in, segments, ln1_gain, ln1_bias, qkv_weight, qkv_bias, out_weight,
    ln2_gain, ln2_bias, gate_up_weight, down_weight, cotangent,
):
    (
        cot_full, par, normed, qkv, attended, maxima, totals, tables, x_own,
        seg_col, seg_row, grad_hidden,
        hidden_in, normed_two, qkv_s, out_s, gu_s, down_s, norm_sib, cot_sib, att_sib,
    ) = front(
        block_in, cotangent, ln1_gain, ln1_bias, ln2_gain, ln2_bias, qkv_bias, segments,
        qkv_weight, out_weight, gate_up_weight, down_weight,
    )
    activations, input_grad, gu_f, qkv_f, down_f, out_f, small = back(
        normed_two, gu_s.reshape(2, D, WIDE), down_s.reshape(WIDE, D), out_s, qkv_s, cot_full,
        normed, tables, norm_sib, cot_sib, att_sib, hidden_in, par, attended, qkv, seg_col, seg_row, maxima, totals, x_own, grad_hidden,
    )
    gu_grad = widen_gate_up(gu_f.reshape(4, 2, 512, WIDE))
    down_f = down_f.reshape(4, WIDE, 512)
    down_grad = jnp.concatenate(
        [down_f[0], down_f[1], down_f[2, 128:], down_f[3, 128:]], axis=0
    ).astype(F32)
    return (
        activations,
        input_grad,
        small[0],
        small[1],
        qkv_f.reshape(512, 4 * WIDE).astype(F32),
        small[4:7].reshape(WIDE),
        out_f.reshape(1024, 512).astype(F32),
        small[2],
        small[3],
        gu_grad,
        down_grad,
    )


def solution(mesh):
    wide = P("dp", ("row", "col"))
    vector = P(("row", "col"))
    return jax.shard_map(
        on_device,
        mesh=mesh,
        in_specs=(
            wide, P("dp"), vector, vector, P("row", "col"), P(("col", "row")), P("col", "row"),
            vector, vector, P("row", None, "col"), P("col", "row"), wide,
        ),
        out_specs=(
            wide, wide, vector, vector, P("row", "col"), P(("col", "row")), P("col", "row"),
            vector, vector, P("row", None, "col"), P("col", "row"),
        ),
        check_vma=False,
    )
```

```python
import math

import jax
import jax.numpy as jnp
from jax import lax
from jax.experimental import pallas as pl
from jax.experimental.pallas import tpu as pltpu
from jax.sharding import PartitionSpec as P

D = 2048
HD = 64
ROT = 16
HEADS = 4
TOK = 512
OWN = 64
WIDE = 768
EPSILON = 1e-05
BF = jnp.bfloat16
F32 = jnp.float32
MESH = pl.DeviceIdType.MESH
VMEM_LIMIT = 59 * 2**20
ROWS_BY_COLS = (((1,), (1,)), ((), ()))
OVER_ROWS = (((0,), (0,)), ((), ()))

IN_VMEM = pl.BlockSpec(memory_space=pltpu.VMEM)
IN_ANY = pl.BlockSpec(memory_space=pl.ANY)


class Place:
    def __init__(self):
        self.dp = lax.axis_index("dp")
        self.x = lax.axis_index("row")
        self.zh = lax.axis_index("col")
        self.y = self.dp // 4
        self.zl = (self.dp // 2) % 2
        self.core = self.dp % 2
        self.q = self.dp // 2
        self.g = self.x * 2 + self.zh

    def group(self, g):
        return (self.dp, g // 2, g % 2)

    def row(self, x):
        return (self.dp, x, self.zh)

    def chip(self, q):
        return (q * 2 + self.core, self.x, self.zh)

    def mate(self):
        return (self.dp, self.x, 1 - self.zh)

    def near_replicas(self):
        def chip(y, zl):
            return ((y * 2 + zl) * 2 + self.core, self.x, self.zh)

        return [
            chip((self.y + 1) % 4, self.zl),
            chip((self.y + 3) % 4, self.zl),
            chip(self.y, 1 - self.zl),
            self.sibling(),
        ]

    def sibling(self):
        return (self.q * 2 + 1 - self.core, self.x, self.zh)

    def replica(self, dp):
        return (dp, self.x, self.zh)


def greet(partners):
    barrier = pltpu.get_barrier_semaphore()
    for partner in partners:
        pl.semaphore_signal(barrier, inc=1, device_id=partner, device_id_type=MESH)
    pl.semaphore_wait(barrier, len(partners))


def push(src, dst, sems, index, device):
    send, recv = sems
    copy = pltpu.make_async_remote_copy(
        src_ref=src,
        dst_ref=dst,
        send_sem=send.at[index],
        recv_sem=recv.at[index],
        device_id=device,
        device_id_type=MESH,
    )
    copy.start()
    return copy


def group_others(at):
    return [at.group((at.g + k) % 8) for k in range(1, 8)]


def chip_others(at):
    return [at.chip(at.q ^ k) for k in range(1, 8)]


def dma_sems(amount):
    return [pltpu.SemaphoreType.DMA((amount,)), pltpu.SemaphoreType.DMA((amount,))]


def params(collective_id):
    return pltpu.CompilerParams(
        collective_id=collective_id, has_side_effects=True, vmem_limit_bytes=VMEM_LIMIT
    )


def tile_start(x):
    return 5 * x + jnp.minimum(x, 1)


def settle(ref, sems, index, device):
    send, recv = sems
    return pltpu.make_async_remote_copy(
        src_ref=ref,
        dst_ref=ref,
        send_sem=send.at[index],
        recv_sem=recv.at[index],
        device_id=device,
        device_id_type=MESH,
    )


class Gather:
    def __init__(self, pos, pair, device, whole, half, sems, base=0, on_piece=None):
        self.pos, self.pair, self.device = pos, pair, device
        self.whole, self.half, self.sems, self.base = whole, half, sems, base
        self.right, self.left, self.far = (pos + 1) % 4, (pos + 3) % 4, (pos + 2) % 4
        self.on_piece = on_piece or (lambda r, p, k: None)

    def push(self, index, ref, device, src=None):
        push(ref if src is None else src, ref, self.sems, self.base + index, device)

    def arrived(self, index, ref):
        settle(ref, self.sems, self.base + index, self.device(self.pos, self.pair)).wait_recv()

    def start(self, own=None):
        self.start_ring(own)
        self.start_pair(own)

    def start_ring(self, own=None):
        ref = self.whole(self.pos, self.pair)
        self.push(1, ref, self.device(self.right, self.pair), own)
        self.push(2, ref, self.device(self.left, self.pair), own)
        self.on_piece(self.pos, self.pair, 0)

    def start_pair(self, own=None):
        ref = self.whole(self.pos, self.pair)
        self.push(0, ref, self.device(self.pos, 1 - self.pair), own)

    def forward(self, first, pair, slot):
        self.arrived(first, self.whole(self.left, pair))
        self.push(first + 2, self.half(self.left, pair, 0), self.device(self.right, self.pair))
        self.on_piece(self.left, pair, slot)
        self.arrived(first + 1, self.whole(self.right, pair))
        self.push(first + 3, self.half(self.right, pair, 1), self.device(self.left, self.pair))
        self.on_piece(self.right, pair, slot + 1)

    def forward_ring(self):
        self.forward(1, self.pair, 1)

    def spread_pair(self):
        ref = self.whole(self.pos, 1 - self.pair)
        self.arrived(0, ref)
        self.push(5, ref, self.device(self.right, self.pair))
        self.push(6, ref, self.device(self.left, self.pair))
        self.on_piece(self.pos, 1 - self.pair, 3)

    def forward_pair(self):
        self.forward(5, 1 - self.pair, 4)

    def finish(self):
        for first, pair, slot in ((3, self.pair, 6), (7, 1 - self.pair, 7)):
            self.arrived(first, self.half(self.far, pair, 0))
            self.arrived(first + 1, self.half(self.far, pair, 1))
            self.on_piece(self.far, pair, slot)

    def drain(self):
        for index in range(9):
            ref = self.whole(self.pos, self.pair)
            if index in (3, 4, 7, 8):
                ref = self.half(self.pos, self.pair, 0)
            settle(ref, self.sems, self.base + index, self.device(self.pos, self.pair)).wait_send()


class RingGather(Gather):
    def start(self, own=None):
        ref = self.whole(self.pos, self.pair)
        self.push(1, ref, self.device(self.right, self.pair), own)
        self.push(2, ref, self.device(self.left, self.pair), own)
        self.push(0, ref, self.device(self.pos, 1 - self.pair), own)
        self.on_piece(self.pos, self.pair, 0)

    def forward_ring(self):
        mate = self.device(self.pos, 1 - self.pair)
        self.arrived(1, self.whole(self.left, self.pair))
        self.push(3, self.half(self.left, self.pair, 0), self.device(self.right, self.pair))
        self.push(5, self.whole(self.left, self.pair), mate)
        self.on_piece(self.left, self.pair, 1)
        self.arrived(2, self.whole(self.right, self.pair))
        self.push(4, self.half(self.right, self.pair, 1), self.device(self.left, self.pair))
        self.push(6, self.whole(self.right, self.pair), mate)
        self.on_piece(self.right, self.pair, 2)

    def spread_far(self):
        self.arrived(3, self.half(self.far, self.pair, 0))
        self.arrived(4, self.half(self.far, self.pair, 1))
        ref = self.whole(self.far, self.pair)
        self.push(7, ref, self.device(self.pos, 1 - self.pair))
        self.on_piece(self.far, self.pair, 3)

    def finish(self):
        pieces = ((0, self.pos), (5, self.left), (6, self.right), (7, self.far))
        for slot, (index, r) in enumerate(pieces):
            self.arrived(index, self.whole(r, 1 - self.pair))
            self.on_piece(r, 1 - self.pair, 4 + slot)

    def drain(self):
        for index in range(8):
            ref = self.whole(self.pos, self.pair)
            if index in (3, 4):
                ref = self.half(self.pos, self.pair, 0)
            settle(ref, self.sems, self.base + index, self.device(self.pos, self.pair)).wait_send()


class MixedGather(RingGather):
    def forward_ring(self):
        self.arrived(1, self.whole(self.left, self.pair))
        self.push(3, self.half(self.left, self.pair, 0), self.device(self.right, self.pair))
        self.arrived(2, self.whole(self.right, self.pair))
        self.push(4, self.half(self.right, self.pair, 1), self.device(self.left, self.pair))

    def spread_pair(self):
        ref = self.whole(self.pos, 1 - self.pair)
        self.arrived(0, ref)
        self.push(5, ref, self.device(self.right, self.pair))
        self.push(6, ref, self.device(self.left, self.pair))

    def finish(self):
        for index, r in ((5, self.left), (6, self.right), (7, self.far)):
            self.arrived(index, self.whole(r, 1 - self.pair))


class RowScatter:
    def __init__(self, at, part, far_in, other_in, half_in, full_in, pair_in, pair_out, sems, base=0):
        self.at, self.part, self.sems, self.base = at, part, sems, base
        self.far_in, self.other_in, self.half_in, self.full_in = far_in, other_in, half_in, full_in
        self.pair_in, self.pair_out = pair_in, pair_out
        self.right, self.left, self.far = (at.x + 1) % 4, (at.x + 3) % 4, (at.x + 2) % 4

    def rows(self, x, plane, half=None):
        start = (x * 2 + plane) * OWN
        if half is None:
            return pl.ds(pl.multiple_of(start, OWN), OWN)
        return pl.ds(pl.multiple_of(start + half * (OWN // 2), OWN // 2), OWN // 2)

    def push(self, index, src, dst, device):
        push(src, dst, self.sems, self.base + index, device)

    def arrived(self, index, ref):
        settle(ref, self.sems, self.base + index, self.at.row(self.at.x)).wait_recv()

    def add(self, rows, box):
        self.part[rows, :] = (self.part[rows, :].astype(F32) + box[...].astype(F32)).astype(BF)

    def zero(self):
        other = 1 - self.at.zh
        self.push(0, self.part.at[self.rows(self.far, other)], self.far_in, self.at.mate())

    def sides(self):
        other = 1 - self.at.zh
        for side, x in enumerate((self.right, self.left)):
            src = self.part.at[self.rows(x, other)]
            self.push(1 + side, src, self.other_in.at[side], self.at.row(x))

    def first(self):
        plane = self.at.zh
        self.arrived(0, self.far_in)
        self.add(self.rows(self.far, plane), self.far_in)
        for side, x in enumerate((self.right, self.left)):
            src = self.part.at[self.rows(self.far, plane, side)]
            self.push(3 + side, src, self.half_in.at[side], self.at.row(x))

    def second(self):
        plane = self.at.zh
        for side, x in enumerate((self.right, self.left)):
            box = self.half_in.at[side]
            self.arrived(3 + side, box)
            self.add(self.rows(x, plane, side), box)
            src = self.part.at[self.rows(x, plane)]
            self.push(5 + side, src, self.full_in.at[side], self.at.row(x))

    def own(self, plane, boxes, index):
        for side in range(2):
            self.arrived(index + side, boxes.at[side])
        total = self.part[self.rows(self.at.x, plane), :].astype(F32)
        return total + boxes[0].astype(F32) + boxes[1].astype(F32)

    def third(self):
        self.pair_out[...] = self.own(1 - self.at.zh, self.other_in, 1).astype(BF)
        self.push(7, self.pair_out, self.pair_in, self.at.mate())

    def fourth(self):
        total = self.own(self.at.zh, self.full_in, 5)
        self.arrived(7, self.pair_in)
        return total + self.pair_in[...].astype(F32)

    def drain(self):
        for index in range(8):
            box = self.half_in.at[0] if index in (3, 4) else self.pair_in
            settle(box, self.sems, self.base + index, self.at.row(self.at.x)).wait_send()


def scatter_scratch():
    vmem = pltpu.VMEM
    return [
        vmem((TOK, D), BF),
        vmem((OWN, D), BF),
        vmem((2, OWN, D), BF),
        vmem((2, OWN // 2, D), BF),
        vmem((2, OWN, D), BF),
        vmem((OWN, D), BF),
        vmem((OWN, D), BF),
    ] + dma_sems(9)


class PieceScatter:
    def __init__(self, at, acc, boxes, sems, base):
        self.at, self.acc, self.sems, self.base = at, acc, sems, base
        self.half_in, self.full_in, self.pair_in, self.pair_out, self.pack = boxes
        self.right, self.left = (at.y + 1) % 4, (at.y + 3) % 4
        self.planes = (1 - at.zl, at.zl)

    def push(self, index, src, dst, y, zl):
        device = ((y * 2 + zl) * 2 + self.at.core, self.at.x, self.at.zh)
        push(src, dst, self.sems, self.base + index, device)

    def arrived(self, index, ref):
        settle(ref, self.sems, self.base + index, self.at.row(self.at.x)).wait_recv()

    def first(self):
        far = (self.at.y + 2) % 4
        for role, plane in enumerate(self.planes):
            for side, y in enumerate((self.right, self.left)):
                self.push(
                    role * 4 + side,
                    self.acc.at[side, :, far * 2 + plane],
                    self.half_in.at[role, side],
                    y,
                    self.at.zl,
                )

    def second(self, role):
        plane = self.planes[role]
        for side, y in enumerate((self.right, self.left)):
            self.arrived(role * 4 + side, self.half_in.at[role, side])
            q = y * 2 + plane
            for b in range(self.acc.shape[1]):
                self.acc[side, b, q] = (
                    self.acc[side, b, q].astype(F32) + self.half_in[role, side, b].astype(F32)
                ).astype(BF)
            self.push(
                role * 4 + 2 + side,
                self.acc.at[:, :, q],
                self.full_in.at[role, side],
                y,
                self.at.zl,
            )

    def total(self, role, out, extra=None):
        for side in range(2):
            self.arrived(role * 4 + 2 + side, self.full_in.at[role, side])
        q = self.at.y * 2 + self.planes[role]
        for a in range(2):
            for b in range(self.acc.shape[1]):
                value = self.acc[a, b, q].astype(F32)
                value += self.full_in[role, 0, a, b].astype(F32)
                value += self.full_in[role, 1, a, b].astype(F32)
                if extra is not None:
                    value += extra[a, b].astype(F32)
                out[a, b] = value.astype(BF)

    def third(self):
        self.total(0, self.pair_out)
        self.push(8, self.pair_out, self.pair_in, self.at.y, 1 - self.at.zl)

    def fourth(self):
        self.arrived(8, self.pair_in)
        self.total(1, self.pack, self.pair_in)

    def drain(self):
        for index in range(9):
            box = self.full_in.at[0, 0] if index % 4 > 1 else self.half_in.at[0, 0]
            if index == 8:
                box = self.pair_in
            settle(box, self.sems, self.base + index, self.at.row(self.at.x)).wait_send()


def piece_scratch(blocks, rows, width):
    vmem = pltpu.VMEM
    return [
        vmem((2, blocks, 8, rows, width), BF),
        vmem((2, 2, blocks, rows, width), BF),
        vmem((2, 2, 2, blocks, rows, width), BF),
        vmem((2, blocks, rows, width), BF),
        vmem((2, blocks, rows, width), BF),
        vmem((2, blocks, rows, width), BF),
    ]


def row_gather(at, ref, sems, base=0, kind=MixedGather):
    def whole(x, plane):
        return ref.at[pl.ds(pl.multiple_of((x * 2 + plane) * OWN, OWN), OWN)]

    def half(x, plane, side):
        start = (x * 2 + plane) * OWN + side * (OWN // 2)
        return ref.at[pl.ds(pl.multiple_of(start, OWN // 2), OWN // 2)]

    return kind(at.x, at.zh, lambda x, plane: (at.dp, x, plane), whole, half, sems, base)


def column_gather(at, ref, sems, base=0, kind=MixedGather):
    def columns(x, plane):
        return pl.ds(pl.multiple_of((x * 2 + plane) * 256, 256), 256)

    def whole(x, plane):
        return ref.at[:, columns(x, plane)]

    def half(x, plane, side):
        return ref.at[pl.ds(side * 256, 256), columns(x, plane)]

    return kind(at.x, at.zh, lambda x, plane: (at.dp, x, plane), whole, half, sems, base)


def front_kernel(
    x_in, cot_in, gain1, shift1, gain2, shift2, bias, seg, qkv_w, out_w, gu_w, down_w,
    cot_out, par_out, normed_out, qkv_out, att_out, max_out, sum_out, tab_out, own_out,
    seg_col, seg_row, grad_hidden,
    hidden_out, normed2_out, qkv_s_out, out_s_out, gu_s, down_s_out, norm_sib, cot_sib, att_sib,
    x_v, normed, par, par_in, proj, tables, qkv_s, out_s, down_s, cot, normed2, rows, raw, split,
    part, far_in, other_in, half_in, full_in, pair_in, pair_out, rs_send, rs_recv,
    par_send, par_recv, act_send, act_recv, a_send, a_recv, dp_send, dp_recv, core_send, core_recv,
    sib_send, sib_recv, local,
):
    at = Place()
    dp, x, core = at.dp, at.x, at.core
    raw_copy = pltpu.make_async_copy(gu_w.at[pl.ds(dp * 32, 32)], raw, local.at[13])
    raw_copy.start()
    par_in[...] = jnp.zeros_like(par_in)
    for j, vector in enumerate((gain1, shift1, gain2, shift2)):
        par_in[j : j + 1, :] = vector[...].reshape(1, 256)
    greet(group_others(at) + at.near_replicas())
    act, step_a, step_dp = (act_send, act_recv), (a_send, a_recv), (dp_send, dp_recv)
    step_core, step_par = (core_send, core_recv), (par_send, par_recv)
    slabs = (qkv_s, out_s, gu_s, down_s)

    def source(k, xt):
        if k == 0:
            return qkv_w.at[pl.ds(dp * 32, 32), pl.ds(pl.multiple_of(xt * WIDE, WIDE), WIDE)]
        if k == 1:
            return out_w.at[pl.ds(xt * 256 + dp * 16, 16), :]
        start = pl.multiple_of(tile_start(xt) * 128, 128)
        if k == 2:
            return split.at[:, :, pl.ds(start, WIDE)]
        return down_w.at[pl.ds(start + dp * 48, 48), :]

    def landing(k, xs, p):
        if k == 0:
            return qkv_s.at[xs, p]
        if k == 2:
            return gu_s.at[:, xs, p]
        return slabs[k].at[p, :, pl.ds(pl.multiple_of(xs * 512, 512), 512)]

    def replica(y, zl):
        return (y * 2 + zl) * 2 + core

    def whole(k):
        def of(y, zl):
            p = replica(y, zl)
            if k == 0:
                return qkv_s.at[:, p]
            if k == 2:
                return gu_s.at[:, :, p]
            return slabs[k].at[p]

        return of

    def half(k):
        def of(y, zl, side):
            p = replica(y, zl)
            if k == 0:
                return qkv_s.at[pl.ds(side * 2, 2), p]
            if k == 2:
                return gu_s.at[side, :, p]
            return slabs[k].at[p, :, pl.ds(side * 1024, 1024)]

        return of

    core_copies = []

    def to_sibling(k):
        def on_piece(y, zl, slot):
            ref = whole(k)(y, zl)
            core_copies.append(push(ref, ref, step_core, k * 8 + slot, at.sibling()))

        return on_piece

    first = {}

    def send_rows(k):
        for j in (2, 1, 3):
            xt = (x + j) % 4
            first[k, j] = push(
                source(k, xt), landing(k, x, dp), step_a, k * 3 + j - 1, at.row(xt)
            )
        first[k, 0] = pltpu.make_async_copy(source(k, x), landing(k, x, dp), local.at[k])
        first[k, 0].start()

    weights = [
        Gather(
            at.y, at.zl, lambda y, zl: (replica(y, zl), x, at.zh), whole(k), half(k), step_dp, k * 9,
            to_sibling(k),
        )
        for k in range(4)
    ]
    w_qkv, w_out, w_gu, w_down = weights

    def begin(k):
        first[k, 0].wait()
        for j in range(1, 4):
            first[k, j].wait_recv()
        weights[k].start()

    def from_sibling(k):
        ref = whole(k)(at.y, at.zl)
        for slot in range(8):
            settle(ref, step_core, k * 8 + slot, at.sibling()).wait_recv()

    slot = pl.ds(pl.multiple_of(at.g * 256, 256), 256)
    send_rows(0)
    gx = column_gather(at, x_v, act, 0)
    gx.start(x_in)
    par_copies = []
    for j, device in enumerate(group_others(at)):
        par_copies.append(push(par_in, par.at[:, slot], step_par, j, device))
    own = [
        pltpu.make_async_copy(x_in, x_v.at[:, slot], local.at[4]),
        pltpu.make_async_copy(par_in, par.at[:, slot], local.at[5]),
        pltpu.make_async_copy(cot_in, cot.at[:, slot], local.at[6]),
    ]
    for copy in own:
        copy.start()
    line = seg[...].reshape(1, TOK).astype(F32)
    seg_row[...] = jnp.broadcast_to(line, (8, TOK))
    seg_col[...] = jnp.transpose(jnp.broadcast_to(line, (128, TOK)))
    begin(0)
    make_tables(seg_col, seg_row, tables)
    raw_copy.wait()
    both = raw[...]
    split[0] = both[:, 0, :]
    split[1] = both[:, 1, :]
    gx.forward_ring()
    gx.spread_pair()
    w_qkv.forward_ring()
    w_qkv.spread_pair()
    send_rows(1)
    gx.spread_far()
    w_qkv.forward_pair()
    begin(1)
    gx.finish()
    gcot = column_gather(at, cot, act, 9)
    gcot.start(cot_in)
    send_rows(3)
    send_rows(2)
    for copy in own:
        copy.wait()
    for copy in par_copies:
        copy.wait_recv()

    def norm_rows(i, carry):
        block = pl.ds(pl.multiple_of(i * 32, 32), 32)
        scaled, _ = norm(x_v[block, :].astype(F32))
        normed[block, :] = (scaled * par[0:1, :] + par[1:2, :]).astype(BF)
        return carry

    lax.fori_loop(0, TOK // 32, norm_rows, 0)
    w_qkv.finish()
    w_out.forward_ring()
    w_out.spread_pair()
    from_sibling(0)
    outgoing = []

    def put(src, dst, index):
        copy = pltpu.make_async_copy(src, dst, local.at[index])
        copy.start()
        outgoing.append(copy)

    for n in range(3):
        cols = pl.ds(n * 256, 256)
        weight = qkv_s[:, :, :, cols].reshape(D, 256)
        proj[:, cols] = jnp.dot(normed[...], weight, preferred_element_type=F32) + bias[
            cols
        ].reshape(1, 256)
    put(normed, normed_out, 7)
    put(qkv_s, qkv_s_out, 8)
    put(x_v.at[own_rows(at)], own_out, 9)
    put(par, par_out, 10)
    sib = (sib_send, sib_recv)
    sib_copies = []
    for xt in range(4):
        cols = pl.ds(xt * 512 + pl.multiple_of((1 - core) * 256, 256), 256)
        sib_copies.append(push(normed.at[:, cols], norm_sib.at[xt], sib, xt, at.sibling()))
    between = [
        lambda: (w_out.forward_pair(), gcot.forward_ring(), gcot.spread_pair()),
        lambda: (begin(3),),
        lambda: (w_out.finish(),),
        lambda: None,
    ]
    attend(proj, tables, seg_col, seg_row, qkv_out, att_out, max_out, sum_out, between)
    from_sibling(1)
    put(out_s, out_s_out, 11)
    put(tables, tab_out, 12)
    rs = RowScatter(
        at, part, far_in, other_in, half_in, full_in, pair_in, pair_out, (rs_send, rs_recv)
    )

    def product(xt):
        weight = out_s[...].reshape(256, D)
        block = pl.ds(pl.multiple_of(xt * 128, 128), 128)
        part[block, :] = jnp.dot(att_out[block, :], weight, preferred_element_type=F32).astype(BF)

    product((x + 2) % 4)
    rs.zero()
    product((x + 1) % 4)
    product((x + 3) % 4)
    rs.sides()
    product(x)
    begin(2)
    w_down.forward_ring()
    rs.first()
    w_down.spread_pair()
    rs.third()
    gcot.spread_far()
    rs.second()
    w_gu.forward_ring()
    w_gu.spread_pair()
    hidden_in = rs.fourth() + x_v[own_rows(at), :].astype(F32)
    hidden_out[...] = hidden_in
    scaled, _ = norm(hidden_in)
    rows[...] = (scaled * par[2:3, :] + par[3:4, :]).astype(BF)
    normed2[own_rows(at), :] = rows[...]
    gn = row_gather(at, normed2, act, 18)
    gn.start(rows)
    gcot.finish()
    put(cot, cot_out, 14)
    sib_copies.append(push(cot, cot_sib, sib, 4, at.sibling()))
    cols = pl.ds(pl.multiple_of((1 - core) * 128, 128), 128)
    sib_copies.append(push(att_out.at[:, cols], att_sib, sib, 5, at.sibling()))
    w_down.forward_pair()
    gn.forward_ring()
    gn.spread_pair()
    w_gu.forward_pair()
    w_down.finish()
    from_sibling(3)
    put(down_s, down_s_out, 15)
    for n in range(3):
        weight = down_s[...].reshape(WIDE, D)[n * 256 : (n + 1) * 256]
        grad_hidden[:, pl.ds(n * 256, 256)] = lax.dot_general(
            cot[...], weight, ROWS_BY_COLS, preferred_element_type=F32
        ).astype(BF)
    gn.spread_far()
    w_gu.finish()
    from_sibling(2)
    gn.finish()
    put(normed2, normed2_out, 16)
    for k in range(4):
        for j in range(1, 4):
            first[k, j].wait_send()
        weights[k].drain()
    for copy in core_copies + par_copies:
        copy.wait_send()
    for copy in sib_copies:
        copy.wait()
    for program in (gx, gcot, gn, rs):
        program.drain()
    for copy in outgoing:
        copy.wait()


def front(*operands):
    shape = jax.ShapeDtypeStruct
    vmem = pltpu.VMEM
    return pl.pallas_call(
        front_kernel,
        out_shape=(
            shape((TOK, D), BF),
            shape((8, D), F32),
            shape((TOK, D), BF),
            shape((TOK, WIDE), BF),
            shape((TOK, 256), BF),
            shape((TOK, 128), F32),
            shape((TOK, 128), F32),
            shape((3, TOK, 384), F32),
            shape((OWN, D), BF),
            shape((TOK, 128), F32),
            shape((8, TOK), F32),
            shape((TOK, WIDE), BF),
            shape((OWN, D), F32),
            shape((TOK, D), BF),
            shape((4, 16, 32, WIDE), BF),
            shape((16, 16, D), BF),
            shape((2, 4, 16, 32, WIDE), BF),
            shape((16, 48, D), BF),
            shape((4, TOK, 256), BF),
            shape((TOK, D), BF),
            shape((TOK, 128), BF),
        ),
        in_specs=[IN_ANY] * 2 + [IN_VMEM] * 6 + [IN_ANY] * 4,
        out_specs=(IN_ANY,) * 3
        + (IN_VMEM,) * 4
        + (IN_ANY,) * 2
        + (IN_VMEM,) * 4
        + (IN_ANY,) * 8,
        scratch_shapes=[
            vmem((TOK, D), BF),
            vmem((TOK, D), BF),
            vmem((8, D), F32),
            vmem((8, 256), F32),
            vmem((TOK, WIDE), F32),
            vmem((3, TOK, 384), F32),
            vmem((4, 16, 32, WIDE), BF),
            vmem((16, 16, D), BF),
            vmem((16, 48, D), BF),
            vmem((TOK, D), BF),
            vmem((TOK, D), BF),
            vmem((OWN, D), BF),
            vmem((32, 2, 2816), BF),
            vmem((2, 32, 2816), BF),
        ]
        + scatter_scratch()
        + dma_sems(7)
        + dma_sems(27)
        + dma_sems(12)
        + dma_sems(36)
        + dma_sems(32)
        + dma_sems(6)
        + [pltpu.SemaphoreType.DMA((17,))],
        compiler_params=params(1),
        name="front",
    )(*operands)


def own_rows(at):
    return pl.ds(pl.multiple_of(at.g * OWN, OWN), OWN)


def columns_of(rows, g):
    return rows.at[:, pl.ds(pl.multiple_of(g * 256, 256), 256)]


def start_columns(at, rows, full, sems, base, local):
    pltpu.make_async_copy(columns_of(rows, at.g), full.at[own_rows(at)], local).start()
    for k in range(1, 8):
        g = (at.g + k) % 8
        push(columns_of(rows, g), full.at[own_rows(at)], sems, base + k - 1, at.group(g))


def finish_columns(at, rows, full, sems, base, local):
    pltpu.make_async_copy(columns_of(rows, at.g), full.at[own_rows(at)], local).wait()
    for k in range(7):
        copy = settle(columns_of(rows, at.g), sems, base + k, at.group(at.g))
        copy.wait_send()
        copy.wait_recv()


def norm(value):
    mean = jnp.mean(value, axis=1, keepdims=True)
    square = jnp.mean(value * value, axis=1, keepdims=True)
    inverse = lax.rsqrt(square - mean * mean + EPSILON)
    return (value - mean) * inverse, inverse


def norm_back(grad, scaled, inverse, gain):
    inner = grad * gain
    mean = jnp.mean(inner, axis=1, keepdims=True)
    along = jnp.mean(inner * scaled, axis=1, keepdims=True)
    return inverse * (inner - mean - scaled * along)


def rotary(value, tables, sign):
    width = value.shape[1]
    return (
        value * tables[0]
        + pltpu.roll(value, width - 8, 1) * (sign * tables[1])
        + pltpu.roll(value, 8, 1) * (sign * tables[2])
    )


def make_tables(seg_col, seg_row, tables):
    half = ROT // 2
    for block in range(4):
        rows = pl.ds(block * 128, 128)
        places = lax.broadcasted_iota(jnp.int32, (128, 128), 0) + block * 128
        before = jnp.where(seg_row[0:1, :] < seg_col[rows, 0:1], 1.0, 0.0)
        starts = jnp.sum(before, axis=1, keepdims=True)
        offsets = places.astype(F32) - starts
        lane = lax.broadcasted_iota(jnp.int32, (128, 128), 1)
        entry = lane % HD
        power = (entry % half).astype(F32) * (-2.0 * math.log(10000.0) / ROT)
        angles = offsets * jnp.exp(power)
        cosine, sine = jnp.cos(angles), jnp.sin(angles)
        keep = jnp.where(entry < ROT, cosine, 1.0)
        fore = jnp.where(entry < half, -sine, 0.0)
        back = jnp.where((entry >= half) & (entry < ROT), sine, 0.0)
        for j, (table, rest) in enumerate(((keep, 1.0), (fore, 0.0), (back, 0.0))):
            low = lane < HD
            tables[j, rows, 0:128] = table
            tables[j, rows, 128:256] = jnp.where(low, rest, table)
            tables[j, rows, 256:384] = jnp.where(low, table, rest)


def head_part(value, head, kind):
    start = head * 3 * HD + kind * HD
    return value[:, start : start + HD]


def allowed(seg_col, seg_row, block, keys):
    start = block * 128
    rows = lax.broadcasted_iota(jnp.int32, (128, keys), 0) + start
    cols = lax.broadcasted_iota(jnp.int32, (128, keys), 1)
    same = seg_col[start : start + 128, 0:1] == seg_row[0:1, :keys]
    return (cols <= rows) & same


def attend(proj, tables, seg_col, seg_row, qkv_out, att_out, max_out, sum_out, between):
    scale = 1.0 / math.sqrt(HD)
    for half in range(2):
        cols = pl.ds(half * 384, 384)
        tab = (tables[0], tables[1], tables[2])
        qkv_out[:, cols] = rotary(proj[:, cols], tab, 1.0).astype(BF)
    for block in range(4):
        keys = (block + 1) * 128
        rows = pl.ds(block * 128, 128)
        mask = allowed(seg_col, seg_row, block, keys)
        outs, maxima, totals = [], [], []
        for head in range(HEADS):
            q = head_part(qkv_out[rows, :], head, 0)
            k = head_part(qkv_out[pl.ds(0, keys), :], head, 1)
            v = head_part(qkv_out[pl.ds(0, keys), :], head, 2)
            score = lax.dot_general(q, k, ROWS_BY_COLS, preferred_element_type=F32) * scale
            score = jnp.where(mask, score, -1e30)
            top = jnp.max(score, axis=1, keepdims=True)
            raised = jnp.exp(score - top)
            total = jnp.sum(raised, axis=1, keepdims=True)
            low = (raised / total).astype(BF)
            outs.append(jnp.dot(low, v, preferred_element_type=F32))
            maxima.append(top)
            totals.append(total)
        att_out[rows, :] = jnp.concatenate(outs, axis=1).astype(BF)
        for head in range(HEADS):
            max_out[rows, head : head + 1] = maxima[head]
            sum_out[rows, head : head + 1] = totals[head]
        if block < len(between):
            between[block]()


def attend_back(
    qkv, grad_att, tables, seg_col, seg_row, maxima, totals, grad_out, pieces, between
):
    scale = 1.0 / math.sqrt(HD)
    pieces[...] = jnp.zeros_like(pieces)
    for block in range(4):
        keys = (block + 1) * 128
        rows = pl.ds(block * 128, 128)
        upto = pl.ds(0, keys)
        mask = allowed(seg_col, seg_row, block, keys)
        for head in range(HEADS):
            q = head_part(qkv[rows, :], head, 0)
            k = head_part(qkv[upto, :], head, 1)
            v = head_part(qkv[upto, :], head, 2)
            grad = grad_att[rows, :][:, head * HD : (head + 1) * HD]
            score = lax.dot_general(q, k, ROWS_BY_COLS, preferred_element_type=F32) * scale
            score = jnp.where(mask, score, -1e30)
            probs = jnp.exp(score - maxima[rows, head : head + 1]) / totals[rows, head : head + 1]
            grad_probs = lax.dot_general(grad, v, ROWS_BY_COLS, preferred_element_type=F32)
            delta = jnp.sum(probs * grad_probs, axis=1, keepdims=True)
            grad_score = (probs * (grad_probs - delta)).astype(BF)
            pieces[head, 0, rows, :] = (
                jnp.dot(grad_score, k, preferred_element_type=F32) * scale
            )
            pieces[head, 1, upto, :] += (
                lax.dot_general(grad_score, q, OVER_ROWS, preferred_element_type=F32) * scale
            )
            pieces[head, 2, upto, :] += lax.dot_general(
                probs.astype(BF), grad, OVER_ROWS, preferred_element_type=F32
            )
        between[block]()
    tab = (tables[0], tables[1], tables[2])
    sums = []
    for half in range(2):
        parts = [pieces[half * 2 + j // 3, j % 3] for j in range(6)]
        cols = pl.ds(half * 384, 384)
        low = rotary(jnp.concatenate(parts, axis=1), tab, -1.0).astype(BF)
        grad_out[:, cols] = low
        sums.append(jnp.sum(low.astype(F32), axis=0, keepdims=True))
    return jnp.concatenate(sums, axis=1)


def back_kernel(
    n2_h, gu_h, down_h, out_h, qkvs_h, cot_h, normed_h, tab_h, norm_sib_h, cot_sib_h, att_sib_h,
    hidden_in, par, att, qkv, seg_col, seg_row, maxima, totals, x_own, grad_hidden,
    act_out, input_out, gu_f, qkv_f, down_f, out_f, small_f,
    n2, n2_sib, cot, cot_sib, gb, gb_sib, att_sib,
    hidden, hidden_sib, gg, gg_sib, gate_up_sib, grad_up, gp_sib, grad_att, grad_in,
    out_s, rows, sums, ln_t, small_t,
    part, part2,
    *rest,
):
    at = Place()
    others = [at.replica((at.dp + k) % 16) for k in range(1, 16)]
    core, q, x = at.core, at.q, at.x
    cq = core * 8 + q
    rest = list(rest)

    def take(amount):
        head, rest[:] = rest[:amount], rest[amount:]
        return head

    boxes = [take(6) for _ in range(2)]
    boxes.append(boxes[0])
    arrays = [take(6) for _ in range(4)]
    (gu_a, qkv_a, down_a, out_a) = [a[0] for a in arrays]
    packs = [a[-1] for a in arrays]
    rs_sems, act_sems, sib_sems = take(2), take(2), take(2)
    dps_sems, row_sems, dpg_sems, core_sems = take(2), take(2), take(2), take(2)
    ln_sems, small_sems = take(2), take(2)
    (local,) = take(1)
    finals = (gu_f, qkv_f, down_f, out_f)

    loads = {}

    def load(name, src, dst, index):
        loads[name] = lambda: pltpu.make_async_copy(src, dst, local.at[index])
        loads[name]().start()

    def columns(c, xt):
        return pl.ds(pl.multiple_of(xt * 512 + c * 256, 256), 256)

    exchange = {}

    def to_sibling(name, src, dst, index):
        exchange[name] = (dst, index)
        push(src, inbox(name), sib_sems, index, at.sibling())

    def inbox(name):
        ref = exchange[name][0]
        return ref.at[name[1]] if isinstance(name, tuple) else ref

    def exchanged(name):
        settle(inbox(name), sib_sems, exchange[name][1], at.sibling()).wait_recv()

    def load_cot_sib(a):
        cols = pl.ds(a * 512, 512)
        load(("cot_sib", a), cot_sib_h.at[:, cols], cot_sib.at[a % 2], 3 if a % 2 else 18)

    load("n2", n2_h, n2, 0)
    def pack_for(k, xt):
        if k == 0:
            return packs[0].at[:, xt]
        if k == 1:
            return packs[1].at[xt // 2, xt % 2]
        return packs[k].at[xt // 2, 0, :, pl.ds(pl.multiple_of((xt % 2) * 512, 512), 512)]

    def landing(k, xs, p):
        if k == 0:
            return gu_f.at[xs, :, p]
        if k == 1:
            return qkv_f.at[p, :, pl.ds(pl.multiple_of(xs * WIDE, WIDE), WIDE)]
        return finals[k].at[xs, p]

    def slot(y, zl):
        return core * 8 + y * 2 + zl

    def whole(k):
        def of(y, zl):
            p = slot(y, zl)
            if k == 0:
                return gu_f.at[:, :, p]
            if k == 1:
                return qkv_f.at[p]
            return finals[k].at[:, p]

        return of

    def half(k):
        def of(y, zl, side):
            p = slot(y, zl)
            if k == 0:
                return gu_f.at[pl.ds(side * 2, 2), :, p]
            if k == 1:
                return qkv_f.at[p, :, pl.ds(side * 2 * WIDE, 2 * WIDE)]
            return finals[k].at[pl.ds(side * 2, 2), p]

        return of

    def share(k):
        def on_piece(y, zl, index):
            ref = whole(k)(y, zl)
            push(ref, ref, core_sems, k * 8 + index, at.sibling())

        return on_piece

    scatters = [
        PieceScatter(at, arrays[k][0], arrays[k][1:], dps_sems, k * 9) for k in range(4)
    ]
    s_gu, s_qkv, s_down, s_out = scatters
    gathers = [
        Gather(
            at.y, at.zl, lambda y, zl: ((y * 2 + zl) * 2 + core, x, at.zh), whole(k), half(k),
            dpg_sems, k * 9, share(k),
        )
        for k in range(4)
    ]
    g_gu, g_qkv, g_down, g_out = gathers
    def send_rows(k):
        scatters[k].fourth()
        for j in (2, 1, 3):
            xt = (x + j) % 4
            push(pack_for(k, xt), landing(k, x, cq), row_sems, k * 3 + j - 1, at.row(xt))
        pltpu.make_async_copy(pack_for(k, x), landing(k, x, cq), local.at[12 + k]).start()

    def begin(k, pair=True):
        pltpu.make_async_copy(pack_for(k, x), landing(k, x, cq), local.at[12 + k]).wait()
        for j in range(3):
            settle(pack_for(k, x), row_sems, k * 3 + j, at.row(x)).wait_recv()
        if pair:
            gathers[k].start()
        else:
            gathers[k].start_ring()

    rs1, rs2, rs3 = [
        RowScatter(at, p, *boxes[j], rs_sems, j * 9) for j, p in enumerate((part, part2, part))
    ]
    block_of = lambda xt: pl.ds(pl.multiple_of(xt * 128, 128), 128)
    far, right, left = (x + 2) % 4, (x + 1) % 4, (x + 3) % 4
    g_branch = row_gather(at, gb, act_sems, 0)

    def outer_sum(a, b, a_sib, b_sib):
        return lax.dot_general(
            a, b, OVER_ROWS, preferred_element_type=F32
        ) + lax.dot_general(a_sib, b_sib, OVER_ROWS, preferred_element_type=F32)

    def down_grad(a):
        cols = pl.ds(a * 512, 512)
        mine = hidden[:, pl.ds(pl.multiple_of(core * 384, 128), 384)]
        loads["cot_sib", a]().wait()
        down_a[a // 2, 0, :, :, pl.ds((a % 2) * 512, 512)] = (
            outer_sum(mine, cot[:, cols], hidden_sib[...], cot_sib[a % 2])
            .astype(BF)
            .reshape(8, 48, 512)
        )
        if a < 2:
            load_cot_sib(a + 2)

    def gate_up_grad(xt, carry):
        own, sib = n2[:, columns(core, xt)], n2_sib[xt]
        gu_a[0, xt] = outer_sum(own, gg[...], sib, gg_sib[...]).astype(BF).reshape(8, 32, WIDE)
        gu_a[1, xt] = (
            outer_sum(own, grad_up[...], sib, gate_up_sib[...]).astype(BF).reshape(8, 32, WIDE)
        )
        return carry

    def feed_forward(gu_s, gate_v, up_v):
        load("gate", gu_h.at[0], gu_s.at[0], 7)
        load("up", gu_h.at[1], gu_s.at[1], 8)
        load("cot", cot_h, cot, 1)
        load("out_s", out_h, out_s, 2)
        greet(group_others(at) + others)
        for xt in range(4):
            to_sibling(("n2", xt), n2_h.at[:, columns(1 - core, xt)], n2_sib, xt)
        for name in ("n2", "gate", "up"):
            loads[name]().wait()
        lane = lax.broadcasted_iota(jnp.int32, (1, 256), 1)

        def chunk(n):
            cols = pl.ds(n * 256, 256)
            gate_v[...] = jnp.dot(n2[...], gu_s[0, :, cols], preferred_element_type=F32)
            up_v[...] = jnp.dot(n2[...], gu_s[1, :, cols], preferred_element_type=F32)
            kept = (lane >= (128 if n == 0 else 0)) | (x < 2)

            def gated(i, carry):
                block = pl.ds(pl.multiple_of(i * 64, 64), 64)
                gate, up = gate_v[block, :], up_v[block, :]
                sig = jax.nn.sigmoid(gate)
                act = gate * sig
                grad = jnp.where(kept, grad_hidden[block, cols].astype(F32), 0.0)
                hidden[block, cols] = jnp.where(kept, act * up, 0.0).astype(BF)
                gg[block, cols] = (grad * up * (sig * (1.0 + gate * (1.0 - sig)))).astype(BF)
                grad_up[block, cols] = (grad * act).astype(BF)
                return carry

            lax.fori_loop(0, 8, gated, 0)

        for n in range(3):
            chunk(n)
        to_sibling(
            "hidden",
            hidden.at[:, pl.ds(pl.multiple_of((1 - core) * 384, 128), 384)],
            hidden_sib,
            5,
        )
        to_sibling("gg", gg, gg_sib, 6)
        to_sibling("up", grad_up, gate_up_sib, 7)

        def product(xt):
            block = block_of(xt)
            value = lax.dot_general(
                gg[block, :], gu_s[0], ROWS_BY_COLS, preferred_element_type=F32
            ) + lax.dot_general(
                grad_up[block, :], gu_s[1], ROWS_BY_COLS, preferred_element_type=F32
            )
            part[block, :] = value.astype(BF)

        product(far)
        rs1.zero()
        exchanged("gg")
        exchanged("up")
        for xt in range(4):
            exchanged(("n2", xt))
        lax.fori_loop(0, 4, gate_up_grad, 0)
        s_gu.first()
        product(right)
        product(left)
        rs1.sides()
        rs1.first()
        product(x)

    def down_product(down_s):
        load("down", down_h, down_s, 9)
        loads["down"]().wait()

        def product_two(i, carry):
            block = block_of(i)
            part2[block, :] = jnp.dot(
                hidden[block, :], down_s[...], preferred_element_type=F32
            ).astype(BF)
            return carry

        lax.fori_loop(0, 4, product_two, 0)

    load_cot_sib(0)
    load_cot_sib(1)
    pl.run_scoped(
        feed_forward,
        pltpu.VMEM((2, D, WIDE), BF),
        pltpu.VMEM((TOK, 256), F32),
        pltpu.VMEM((TOK, 256), F32),
    )
    s_gu.second(0)
    s_gu.second(1)
    rs1.third()
    rs1.second()
    load("nh", normed_h, n2, 4)
    load("nh_sib", norm_sib_h, n2_sib, 5)
    load("att_sib", att_sib_h, att_sib, 6)
    loads["cot"]().wait()
    exchanged("hidden")
    down_grad(0)
    down_grad(1)
    down_grad(2)
    down_grad(3)
    s_down.first()
    scaled, inverse = norm(hidden_in[...])
    grad = rs1.fourth()
    value = cot[own_rows(at), :].astype(F32) + norm_back(grad, scaled, inverse, par[2:3, :])
    rows[0] = value.astype(BF)
    gb[own_rows(at), :] = value.astype(BF)
    g_branch.start(rows.at[0])
    grad_in[...] = value
    sums[...] = jnp.zeros_like(sums)
    sums[2:3, :] = jnp.sum(grad * scaled, axis=0, keepdims=True)
    sums[3:4, :] = jnp.sum(grad, axis=0, keepdims=True)
    s_gu.third()
    pl.run_scoped(down_product, pltpu.VMEM((WIDE, D), BF))
    g_branch.forward_ring()
    g_branch.spread_pair()
    s_down.second(0)
    s_down.second(1)
    g_branch.spread_far()
    send_rows(0)
    g_branch.finish()
    to_sibling("gb", gb, gb_sib, 13)
    settle(inbox("gg"), sib_sems, exchange["gg"][1], at.sibling()).wait_send()
    gp = gg

    def qkv_grad(xt, carry):
        qkv_a[xt // 2, xt % 2] = (
            outer_sum(n2[:, columns(core, xt)], gp[...], n2_sib[xt], gp_sib[...])
            .astype(BF)
            .reshape(8, 32, WIDE)
        )
        return carry

    def out_grad():
        exchanged("gb")
        loads["att_sib"]().wait()
        mine = att[:, pl.ds(pl.multiple_of(core * 128, 128), 128)]
        for a in range(2):
            cols = pl.ds(a * 1024, 1024)
            out_a[a, 0] = (
                outer_sum(mine, gb[:, cols], att_sib[...], gb_sib[:, cols])
                .astype(BF)
                .reshape(8, 16, 1024)
            )
        s_out.first()

    def attention(tables, pieces, qkv_s):
        load("tab", tab_h, tables, 10)
        load("qkv_s", qkvs_h, qkv_s, 11)
        loads["out_s"]().wait()
        grad_att[...] = lax.dot_general(
            gb[...], out_s[...].reshape(256, D), ROWS_BY_COLS, preferred_element_type=F32
        ).astype(BF)
        rs2.zero()
        rs2.sides()
        loads["tab"]().wait()

        between = [
            lambda: (begin(0),),
            lambda: (out_grad(),),
            lambda: (rs2.first(), s_down.third()),
            lambda: (g_gu.forward_ring(),),
        ]
        bias_sums = attend_back(
            qkv, grad_att, tables, seg_col, seg_row, maxima, totals, gp, pieces, between
        )
        to_sibling("gp", gp, gp_sib, 14)
        loads["qkv_s"]().wait()
        rs1.drain()

        def product(xt):
            block = block_of(xt)
            weight = qkv_s[...].reshape(D, WIDE)
            part[block, :] = lax.dot_general(
                gp[block, :], weight, ROWS_BY_COLS, preferred_element_type=F32
            ).astype(BF)

        product(far)
        rs3.zero()
        product(right)
        product(left)
        rs3.sides()
        s_out.second(0)
        s_out.second(1)
        exchanged("gp")
        loads["nh"]().wait()
        loads["nh_sib"]().wait()
        lax.fori_loop(0, 4, qkv_grad, 0)
        s_qkv.first()
        product(x)
        g_gu.spread_pair()
        sums[4:7, 0:256] = jnp.concatenate([bias_sums[:, j * 256 : (j + 1) * 256] for j in range(3)])

    pl.run_scoped(
        attention,
        pltpu.VMEM((3, TOK, 384), F32),
        pltpu.VMEM((HEADS, 3, TOK, HD), F32),
        pltpu.VMEM((4, 16, 32, WIDE), BF),
    )
    rs3.first()
    rs3.third()
    s_qkv.second(0)
    s_qkv.second(1)
    rs3.second()
    send_rows(2)
    rs2.third()
    rs2.second()
    scaled, inverse = norm(x_own[...].astype(F32))
    grad = rs3.fourth()
    value = grad_in[...] + norm_back(grad, scaled, inverse, par[0:1, :])
    rows[2] = value.astype(BF)
    start_columns(at, rows.at[2], input_out, act_sems, 16, local.at[17])
    sums[0:1, :] = jnp.sum(grad * scaled, axis=0, keepdims=True)
    sums[1:2, :] = jnp.sum(grad, axis=0, keepdims=True)
    own_columns = pl.ds(pl.multiple_of(at.g * 256, 256), 256)
    ln_copies = []
    for j in range(1, 8):
        g = (at.g + j) % 8
        ln_copies.append(
            push(
                sums.at[pl.ds(0, 4), pl.ds(pl.multiple_of(g * 256, 256), 256)],
                ln_t.at[j - 1],
                ln_sems,
                j - 1,
                at.group(g),
            )
        )
    begin(2)
    s_qkv.third()
    s_out.third()
    g_gu.forward_pair()
    total = sums[0:4, own_columns]
    for j in range(7):
        ln_copies[j].wait_recv()
        total += ln_t[j]
    small_t[pl.ds(at.dp, 1), 0:4] = total[None]
    small_t[pl.ds(at.dp, 1), 4:8] = sums[4:8, 0:256][None]
    small_copies = [
        push(small_t.at[at.dp], small_t.at[at.dp], small_sems, j, device)
        for j, device in enumerate(others)
    ]
    send_rows(1)
    send_rows(3)
    g_down.forward_ring()
    g_down.spread_pair()
    begin(1)
    begin(3)
    total = rs2.fourth() + hidden_in[...]
    rows[1] = total.astype(BF)
    start_columns(at, rows.at[1], act_out, act_sems, 9, local.at[16])
    g_qkv.forward_ring()
    g_qkv.spread_pair()
    g_out.forward_ring()
    g_out.spread_pair()
    g_gu.finish()
    g_down.forward_pair()
    g_qkv.forward_pair()
    g_out.forward_pair()
    g_down.finish()
    for copy in small_copies:
        copy.wait_recv()
    result = small_t[0]
    for j in range(1, 16):
        result += small_t[j]
    small_f[...] = result
    g_out.finish()
    g_qkv.finish()
    for k in range(4):
        ref = whole(k)(at.y, at.zl)
        for index in range(8):
            settle(ref, core_sems, k * 8 + index, at.sibling()).wait_recv()
            settle(ref, core_sems, k * 8 + index, at.sibling()).wait_send()
        scatters[k].drain()
        gathers[k].drain()
        for j in range(3):
            settle(pack_for(k, x), row_sems, k * 3 + j, at.row(x)).wait_send()
    for copy in ln_copies + small_copies:
        copy.wait_send()
    for name in exchange:
        if name == "gg":
            continue
        settle(inbox(name), sib_sems, exchange[name][1], at.sibling()).wait_send()
    g_branch.drain()
    rs2.drain()
    rs3.drain()
    finish_columns(at, rows.at[1], act_out, act_sems, 9, local.at[16])
    finish_columns(at, rows.at[2], input_out, act_sems, 16, local.at[17])


def back(
    n2, gu_s, down_s, out_s, qkv_s, cot, normed, tables, norm_sib, cot_sib, att_sib,
    hidden_in, par, att, qkv, seg_col, seg_row, maxima, totals, x_own, grad_hidden,
):
    shape = jax.ShapeDtypeStruct
    vmem = pltpu.VMEM
    wide = vmem((TOK, D), BF)
    inner = vmem((TOK, WIDE), BF)
    quarters = vmem((4, TOK, 256), BF)
    box = scatter_scratch()[1:7]
    return pl.pallas_call(
        back_kernel,
        out_shape=(
            shape((TOK, 256), BF),
            shape((TOK, 256), BF),
            shape((4, 2, 16, 32, WIDE), BF),
            shape((16, 32, 4 * WIDE), BF),
            shape((4, 16, 48, 512), BF),
            shape((4, 16, 16, 512), BF),
            shape((8, 256), F32),
        ),
        in_specs=[IN_ANY] * 11 + [IN_VMEM] * 10,
        out_specs=(IN_ANY,) * 6 + (IN_VMEM,),
        scratch_shapes=[
            wide, quarters, wide, vmem((2, TOK, 512), BF), wide, wide, vmem((TOK, 128), BF),
            inner, vmem((TOK, 384), BF), inner, inner, inner, inner, inner,
            vmem((TOK, 256), BF), vmem((OWN, D), F32),
            vmem((16, 16, D), BF), vmem((3, OWN, D), BF), vmem((8, D), F32),
            vmem((7, 4, 256), F32), vmem((16, 8, 256), F32),
            wide, wide,
        ]
        + box * 2
        + piece_scratch(4, 32, WIDE)
        + piece_scratch(2, 32, WIDE)
        + piece_scratch(1, 48, 1024)
        + piece_scratch(1, 16, 1024)
        + dma_sems(27)
        + dma_sems(23)
        + dma_sems(15)
        + dma_sems(36)
        + dma_sems(12)
        + dma_sems(36)
        + dma_sems(32)
        + dma_sems(7)
        + dma_sems(15)
        + [pltpu.SemaphoreType.DMA((19,))],
        compiler_params=params(2),
        name="back",
    )(
        n2, gu_s, down_s, out_s, qkv_s, cot, normed, tables, norm_sib, cot_sib, att_sib,
        hidden_in, par, att, qkv, seg_col, seg_row, maxima, totals, x_own, grad_hidden,
    )


def widen_gate_up_kernel(low, out):
    for j in range(2):
        shares = [low[x, j] for x in range(4)]
        out[:, j, 0:768] = shares[0].astype(F32)
        out[:, j, 768:1536] = shares[1].astype(F32)
        out[:, j, 1536:2176] = shares[2][:, 128:].astype(F32)
        out[:, j, 2176:2816] = shares[3][:, 128:].astype(F32)


def widen_gate_up(low):
    return pl.pallas_call(
        widen_gate_up_kernel,
        out_shape=jax.ShapeDtypeStruct((512, 2, 2816), F32),
        grid=(8,),
        in_specs=[pl.BlockSpec((4, 2, 64, WIDE), lambda i: (0, 0, i, 0))],
        out_specs=pl.BlockSpec((64, 2, 2816), lambda i: (i, 0, 0)),
        compiler_params=pltpu.CompilerParams(vmem_limit_bytes=VMEM_LIMIT),
        name="widen_gate_up",
    )(low)


def on_device(
    block_in, segments, ln1_gain, ln1_bias, qkv_weight, qkv_bias, out_weight,
    ln2_gain, ln2_bias, gate_up_weight, down_weight, cotangent,
):
    (
        cot_full, par, normed, qkv, attended, maxima, totals, tables, x_own,
        seg_col, seg_row, grad_hidden,
        hidden_in, normed_two, qkv_s, out_s, gu_s, down_s, norm_sib, cot_sib, att_sib,
    ) = front(
        block_in, cotangent, ln1_gain, ln1_bias, ln2_gain, ln2_bias, qkv_bias, segments,
        qkv_weight, out_weight, gate_up_weight, down_weight,
    )
    activations, input_grad, gu_f, qkv_f, down_f, out_f, small = back(
        normed_two, gu_s.reshape(2, D, WIDE), down_s.reshape(WIDE, D), out_s, qkv_s, cot_full,
        normed, tables, norm_sib, cot_sib, att_sib, hidden_in, par, attended, qkv, seg_col, seg_row, maxima, totals, x_own, grad_hidden,
    )
    gu_grad = widen_gate_up(gu_f.reshape(4, 2, 512, WIDE))
    down_f = down_f.reshape(4, WIDE, 512)
    down_grad = jnp.concatenate(
        [down_f[0], down_f[1], down_f[2, 128:], down_f[3, 128:]], axis=0
    ).astype(F32)
    return (
        activations,
        input_grad,
        small[0],
        small[1],
        qkv_f.reshape(512, 4 * WIDE).astype(F32),
        small[4:7].reshape(WIDE),
        out_f.reshape(1024, 512).astype(F32),
        small[2],
        small[3],
        gu_grad,
        down_grad,
    )


def solution(mesh):
    wide = P("dp", ("row", "col"))
    vector = P(("row", "col"))
    return jax.shard_map(
        on_device,
        mesh=mesh,
        in_specs=(
            wide, P("dp"), vector, vector, P("row", "col"), P(("col", "row")), P("col", "row"),
            vector, vector, P("row", None, "col"), P("col", "row"), wide,
        ),
        out_specs=(
            wide, wide, vector, vector, P("row", "col"), P(("col", "row")), P("col", "row"),
            vector, vector, P("row", None, "col"), P("col", "row"),
        ),
        check_vma=False,
    )
```

```python
import math

import jax
import jax.numpy as jnp
from jax import lax
from jax.experimental import pallas as pl
from jax.experimental.pallas import tpu as pltpu
from jax.sharding import PartitionSpec as P

D = 2048
HD = 64
ROT = 16
HEADS = 4
TOK = 512
OWN = 64
WIDE = 768
EPSILON = 1e-05
BF = jnp.bfloat16
F32 = jnp.float32
MESH = pl.DeviceIdType.MESH
VMEM_LIMIT = 59 * 2**20
ROWS_BY_COLS = (((1,), (1,)), ((), ()))
OVER_ROWS = (((0,), (0,)), ((), ()))

IN_VMEM = pl.BlockSpec(memory_space=pltpu.VMEM)
IN_ANY = pl.BlockSpec(memory_space=pl.ANY)


class Place:
    def __init__(self):
        self.dp = lax.axis_index("dp")
        self.x = lax.axis_index("row")
        self.zh = lax.axis_index("col")
        self.y = self.dp // 4
        self.zl = (self.dp // 2) % 2
        self.core = self.dp % 2
        self.q = self.dp // 2
        self.g = self.x * 2 + self.zh

    def group(self, g):
        return (self.dp, g // 2, g % 2)

    def row(self, x):
        return (self.dp, x, self.zh)

    def chip(self, q):
        return (q * 2 + self.core, self.x, self.zh)

    def mate(self):
        return (self.dp, self.x, 1 - self.zh)

    def near_replicas(self):
        def chip(y, zl):
            return ((y * 2 + zl) * 2 + self.core, self.x, self.zh)

        return [
            chip((self.y + 1) % 4, self.zl),
            chip((self.y + 3) % 4, self.zl),
            chip(self.y, 1 - self.zl),
            self.sibling(),
        ]

    def sibling(self):
        return (self.q * 2 + 1 - self.core, self.x, self.zh)

    def replica(self, dp):
        return (dp, self.x, self.zh)


def greet(partners):
    barrier = pltpu.get_barrier_semaphore()
    for partner in partners:
        pl.semaphore_signal(barrier, inc=1, device_id=partner, device_id_type=MESH)
    pl.semaphore_wait(barrier, len(partners))


def push(src, dst, sems, index, device):
    send, recv = sems
    copy = pltpu.make_async_remote_copy(
        src_ref=src,
        dst_ref=dst,
        send_sem=send.at[index],
        recv_sem=recv.at[index],
        device_id=device,
        device_id_type=MESH,
    )
    copy.start()
    return copy


def group_others(at):
    return [at.group((at.g + k) % 8) for k in range(1, 8)]


def chip_others(at):
    return [at.chip(at.q ^ k) for k in range(1, 8)]


def dma_sems(amount):
    return [pltpu.SemaphoreType.DMA((amount,)), pltpu.SemaphoreType.DMA((amount,))]


def params(collective_id):
    return pltpu.CompilerParams(
        collective_id=collective_id, has_side_effects=True, vmem_limit_bytes=VMEM_LIMIT
    )


def tile_start(x):
    return 5 * x + jnp.minimum(x, 1)


def settle(ref, sems, index, device):
    send, recv = sems
    return pltpu.make_async_remote_copy(
        src_ref=ref,
        dst_ref=ref,
        send_sem=send.at[index],
        recv_sem=recv.at[index],
        device_id=device,
        device_id_type=MESH,
    )


class Gather:
    def __init__(self, pos, pair, device, whole, half, sems, base=0, on_piece=None):
        self.pos, self.pair, self.device = pos, pair, device
        self.whole, self.half, self.sems, self.base = whole, half, sems, base
        self.right, self.left, self.far = (pos + 1) % 4, (pos + 3) % 4, (pos + 2) % 4
        self.on_piece = on_piece or (lambda r, p, k: None)

    def push(self, index, ref, device, src=None):
        push(ref if src is None else src, ref, self.sems, self.base + index, device)

    def arrived(self, index, ref):
        settle(ref, self.sems, self.base + index, self.device(self.pos, self.pair)).wait_recv()

    def start(self, own=None):
        self.start_ring(own)
        self.start_pair(own)

    def start_ring(self, own=None):
        ref = self.whole(self.pos, self.pair)
        self.push(1, ref, self.device(self.right, self.pair), own)
        self.push(2, ref, self.device(self.left, self.pair), own)
        self.on_piece(self.pos, self.pair, 0)

    def start_pair(self, own=None):
        ref = self.whole(self.pos, self.pair)
        self.push(0, ref, self.device(self.pos, 1 - self.pair), own)

    def forward(self, first, pair, slot):
        self.arrived(first, self.whole(self.left, pair))
        self.push(first + 2, self.half(self.left, pair, 0), self.device(self.right, self.pair))
        self.on_piece(self.left, pair, slot)
        self.arrived(first + 1, self.whole(self.right, pair))
        self.push(first + 3, self.half(self.right, pair, 1), self.device(self.left, self.pair))
        self.on_piece(self.right, pair, slot + 1)

    def forward_ring(self):
        self.forward(1, self.pair, 1)

    def spread_pair(self):
        ref = self.whole(self.pos, 1 - self.pair)
        self.arrived(0, ref)
        self.push(5, ref, self.device(self.right, self.pair))
        self.push(6, ref, self.device(self.left, self.pair))
        self.on_piece(self.pos, 1 - self.pair, 3)

    def forward_pair(self):
        self.forward(5, 1 - self.pair, 4)

    def finish(self):
        for first, pair, slot in ((3, self.pair, 6), (7, 1 - self.pair, 7)):
            self.arrived(first, self.half(self.far, pair, 0))
            self.arrived(first + 1, self.half(self.far, pair, 1))
            self.on_piece(self.far, pair, slot)

    def drain(self):
        for index in range(9):
            ref = self.whole(self.pos, self.pair)
            if index in (3, 4, 7, 8):
                ref = self.half(self.pos, self.pair, 0)
            settle(ref, self.sems, self.base + index, self.device(self.pos, self.pair)).wait_send()


class RingGather(Gather):
    def start(self, own=None):
        ref = self.whole(self.pos, self.pair)
        self.push(1, ref, self.device(self.right, self.pair), own)
        self.push(2, ref, self.device(self.left, self.pair), own)
        self.push(0, ref, self.device(self.pos, 1 - self.pair), own)
        self.on_piece(self.pos, self.pair, 0)

    def forward_ring(self):
        mate = self.device(self.pos, 1 - self.pair)
        self.arrived(1, self.whole(self.left, self.pair))
        self.push(3, self.half(self.left, self.pair, 0), self.device(self.right, self.pair))
        self.push(5, self.whole(self.left, self.pair), mate)
        self.on_piece(self.left, self.pair, 1)
        self.arrived(2, self.whole(self.right, self.pair))
        self.push(4, self.half(self.right, self.pair, 1), self.device(self.left, self.pair))
        self.push(6, self.whole(self.right, self.pair), mate)
        self.on_piece(self.right, self.pair, 2)

    def spread_far(self):
        self.arrived(3, self.half(self.far, self.pair, 0))
        self.arrived(4, self.half(self.far, self.pair, 1))
        ref = self.whole(self.far, self.pair)
        self.push(7, ref, self.device(self.pos, 1 - self.pair))
        self.on_piece(self.far, self.pair, 3)

    def finish(self):
        pieces = ((0, self.pos), (5, self.left), (6, self.right), (7, self.far))
        for slot, (index, r) in enumerate(pieces):
            self.arrived(index, self.whole(r, 1 - self.pair))
            self.on_piece(r, 1 - self.pair, 4 + slot)

    def drain(self):
        for index in range(8):
            ref = self.whole(self.pos, self.pair)
            if index in (3, 4):
                ref = self.half(self.pos, self.pair, 0)
            settle(ref, self.sems, self.base + index, self.device(self.pos, self.pair)).wait_send()


class MixedGather(RingGather):
    def forward_ring(self):
        self.arrived(1, self.whole(self.left, self.pair))
        self.push(3, self.half(self.left, self.pair, 0), self.device(self.right, self.pair))
        self.arrived(2, self.whole(self.right, self.pair))
        self.push(4, self.half(self.right, self.pair, 1), self.device(self.left, self.pair))

    def spread_pair(self):
        ref = self.whole(self.pos, 1 - self.pair)
        self.arrived(0, ref)
        self.push(5, ref, self.device(self.right, self.pair))
        self.push(6, ref, self.device(self.left, self.pair))

    def finish(self):
        for index, r in ((5, self.left), (6, self.right), (7, self.far)):
            self.arrived(index, self.whole(r, 1 - self.pair))


class RowScatter:
    def __init__(self, at, part, far_in, other_in, half_in, full_in, pair_in, pair_out, sems, base=0):
        self.at, self.part, self.sems, self.base = at, part, sems, base
        self.far_in, self.other_in, self.half_in, self.full_in = far_in, other_in, half_in, full_in
        self.pair_in, self.pair_out = pair_in, pair_out
        self.right, self.left, self.far = (at.x + 1) % 4, (at.x + 3) % 4, (at.x + 2) % 4

    def rows(self, x, plane, half=None):
        start = (x * 2 + plane) * OWN
        if half is None:
            return pl.ds(pl.multiple_of(start, OWN), OWN)
        return pl.ds(pl.multiple_of(start + half * (OWN // 2), OWN // 2), OWN // 2)

    def push(self, index, src, dst, device):
        push(src, dst, self.sems, self.base + index, device)

    def arrived(self, index, ref):
        settle(ref, self.sems, self.base + index, self.at.row(self.at.x)).wait_recv()

    def add(self, rows, box):
        self.part[rows, :] = (self.part[rows, :].astype(F32) + box[...].astype(F32)).astype(BF)

    def zero(self):
        other = 1 - self.at.zh
        self.push(0, self.part.at[self.rows(self.far, other)], self.far_in, self.at.mate())

    def sides(self):
        other = 1 - self.at.zh
        for side, x in enumerate((self.right, self.left)):
            src = self.part.at[self.rows(x, other)]
            self.push(1 + side, src, self.other_in.at[side], self.at.row(x))

    def first(self):
        plane = self.at.zh
        self.arrived(0, self.far_in)
        self.add(self.rows(self.far, plane), self.far_in)
        for side, x in enumerate((self.right, self.left)):
            src = self.part.at[self.rows(self.far, plane, side)]
            self.push(3 + side, src, self.half_in.at[side], self.at.row(x))

    def second(self):
        plane = self.at.zh
        for side, x in enumerate((self.right, self.left)):
            box = self.half_in.at[side]
            self.arrived(3 + side, box)
            self.add(self.rows(x, plane, side), box)
            src = self.part.at[self.rows(x, plane)]
            self.push(5 + side, src, self.full_in.at[side], self.at.row(x))

    def own(self, plane, boxes, index):
        for side in range(2):
            self.arrived(index + side, boxes.at[side])
        total = self.part[self.rows(self.at.x, plane), :].astype(F32)
        return total + boxes[0].astype(F32) + boxes[1].astype(F32)

    def third(self):
        self.pair_out[...] = self.own(1 - self.at.zh, self.other_in, 1).astype(BF)
        self.push(7, self.pair_out, self.pair_in, self.at.mate())

    def fourth(self):
        total = self.own(self.at.zh, self.full_in, 5)
        self.arrived(7, self.pair_in)
        return total + self.pair_in[...].astype(F32)

    def drain(self):
        for index in range(8):
            box = self.half_in.at[0] if index in (3, 4) else self.pair_in
            settle(box, self.sems, self.base + index, self.at.row(self.at.x)).wait_send()


def scatter_scratch():
    vmem = pltpu.VMEM
    return [
        vmem((TOK, D), BF),
        vmem((OWN, D), BF),
        vmem((2, OWN, D), BF),
        vmem((2, OWN // 2, D), BF),
        vmem((2, OWN, D), BF),
        vmem((OWN, D), BF),
        vmem((OWN, D), BF),
    ] + dma_sems(9)


class PieceScatter:
    def __init__(self, at, acc, boxes, sems, base):
        self.at, self.acc, self.sems, self.base = at, acc, sems, base
        self.half_in, self.full_in, self.pair_in, self.pair_out, self.pack = boxes
        self.right, self.left = (at.y + 1) % 4, (at.y + 3) % 4
        self.planes = (1 - at.zl, at.zl)

    def push(self, index, src, dst, y, zl):
        device = ((y * 2 + zl) * 2 + self.at.core, self.at.x, self.at.zh)
        push(src, dst, self.sems, self.base + index, device)

    def arrived(self, index, ref):
        settle(ref, self.sems, self.base + index, self.at.row(self.at.x)).wait_recv()

    def first(self):
        far = (self.at.y + 2) % 4
        for role, plane in enumerate(self.planes):
            for side, y in enumerate((self.right, self.left)):
                self.push(
                    role * 4 + side,
                    self.acc.at[side, :, far * 2 + plane],
                    self.half_in.at[role, side],
                    y,
                    self.at.zl,
                )

    def second(self, role):
        plane = self.planes[role]
        for side, y in enumerate((self.right, self.left)):
            self.arrived(role * 4 + side, self.half_in.at[role, side])
            q = y * 2 + plane
            for b in range(self.acc.shape[1]):
                self.acc[side, b, q] = (
                    self.acc[side, b, q].astype(F32) + self.half_in[role, side, b].astype(F32)
                ).astype(BF)
            self.push(
                role * 4 + 2 + side,
                self.acc.at[:, :, q],
                self.full_in.at[role, side],
                y,
                self.at.zl,
            )

    def total(self, role, out, extra=None):
        for side in range(2):
            self.arrived(role * 4 + 2 + side, self.full_in.at[role, side])
        q = self.at.y * 2 + self.planes[role]
        for a in range(2):
            for b in range(self.acc.shape[1]):
                value = self.acc[a, b, q].astype(F32)
                value += self.full_in[role, 0, a, b].astype(F32)
                value += self.full_in[role, 1, a, b].astype(F32)
                if extra is not None:
                    value += extra[a, b].astype(F32)
                out[a, b] = value.astype(BF)

    def third(self):
        self.total(0, self.pair_out)
        self.push(8, self.pair_out, self.pair_in, self.at.y, 1 - self.at.zl)

    def fourth(self):
        self.arrived(8, self.pair_in)
        self.total(1, self.pack, self.pair_in)

    def drain(self):
        for index in range(9):
            box = self.full_in.at[0, 0] if index % 4 > 1 else self.half_in.at[0, 0]
            if index == 8:
                box = self.pair_in
            settle(box, self.sems, self.base + index, self.at.row(self.at.x)).wait_send()


def piece_scratch(blocks, rows, width):
    vmem = pltpu.VMEM
    return [
        vmem((2, blocks, 8, rows, width), BF),
        vmem((2, 2, blocks, rows, width), BF),
        vmem((2, 2, 2, blocks, rows, width), BF),
        vmem((2, blocks, rows, width), BF),
        vmem((2, blocks, rows, width), BF),
        vmem((2, blocks, rows, width), BF),
    ]


def row_gather(at, ref, sems, base=0, kind=MixedGather):
    def whole(x, plane):
        return ref.at[pl.ds(pl.multiple_of((x * 2 + plane) * OWN, OWN), OWN)]

    def half(x, plane, side):
        start = (x * 2 + plane) * OWN + side * (OWN // 2)
        return ref.at[pl.ds(pl.multiple_of(start, OWN // 2), OWN // 2)]

    return kind(at.x, at.zh, lambda x, plane: (at.dp, x, plane), whole, half, sems, base)


def column_gather(at, ref, sems, base=0, kind=MixedGather):
    def columns(x, plane):
        return pl.ds(pl.multiple_of((x * 2 + plane) * 256, 256), 256)

    def whole(x, plane):
        return ref.at[:, columns(x, plane)]

    def half(x, plane, side):
        return ref.at[pl.ds(side * 256, 256), columns(x, plane)]

    return kind(at.x, at.zh, lambda x, plane: (at.dp, x, plane), whole, half, sems, base)


def front_kernel(
    x_in, cot_in, gain1, shift1, gain2, shift2, bias, seg, qkv_w, out_w, gu_w, down_w,
    cot_out, par_out, normed_out, qkv_out, att_out, max_out, sum_out, tab_out, own_out,
    seg_col, seg_row, grad_hidden,
    hidden_out, normed2_out, qkv_s_out, out_s_out, gu_s, down_s_out, norm_sib, cot_sib, att_sib,
    x_v, normed, par, par_in, proj, tables, qkv_s, out_s, down_s, cot, normed2, rows, raw, split,
    part, far_in, other_in, half_in, full_in, pair_in, pair_out, rs_send, rs_recv,
    par_send, par_recv, act_send, act_recv, a_send, a_recv, dp_send, dp_recv, core_send, core_recv,
    sib_send, sib_recv, local,
):
    at = Place()
    dp, x, core = at.dp, at.x, at.core
    raw_copy = pltpu.make_async_copy(gu_w.at[pl.ds(dp * 32, 32)], raw, local.at[13])
    raw_copy.start()
    par_in[...] = jnp.zeros_like(par_in)
    for j, vector in enumerate((gain1, shift1, gain2, shift2)):
        par_in[j : j + 1, :] = vector[...].reshape(1, 256)
    greet(group_others(at) + at.near_replicas())
    act, step_a, step_dp = (act_send, act_recv), (a_send, a_recv), (dp_send, dp_recv)
    step_core, step_par = (core_send, core_recv), (par_send, par_recv)
    slabs = (qkv_s, out_s, gu_s, down_s)

    def source(k, xt):
        if k == 0:
            return qkv_w.at[pl.ds(dp * 32, 32), pl.ds(pl.multiple_of(xt * WIDE, WIDE), WIDE)]
        if k == 1:
            return out_w.at[pl.ds(xt * 256 + dp * 16, 16), :]
        start = pl.multiple_of(tile_start(xt) * 128, 128)
        if k == 2:
            return split.at[:, :, pl.ds(start, WIDE)]
        return down_w.at[pl.ds(start + dp * 48, 48), :]

    def landing(k, xs, p):
        if k == 0:
            return qkv_s.at[xs, p]
        if k == 2:
            return gu_s.at[:, xs, p]
        return slabs[k].at[p, :, pl.ds(pl.multiple_of(xs * 512, 512), 512)]

    def replica(y, zl):
        return (y * 2 + zl) * 2 + core

    def whole(k):
        def of(y, zl):
            p = replica(y, zl)
            if k == 0:
                return qkv_s.at[:, p]
            if k == 2:
                return gu_s.at[:, :, p]
            return slabs[k].at[p]

        return of

    def half(k):
        def of(y, zl, side):
            p = replica(y, zl)
            if k == 0:
                return qkv_s.at[pl.ds(side * 2, 2), p]
            if k == 2:
                return gu_s.at[side, :, p]
            return slabs[k].at[p, :, pl.ds(side * 1024, 1024)]

        return of

    core_copies = []

    def to_sibling(k):
        def on_piece(y, zl, slot):
            ref = whole(k)(y, zl)
            core_copies.append(push(ref, ref, step_core, k * 8 + slot, at.sibling()))

        return on_piece

    first = {}

    def send_rows(k):
        for j in (2, 1, 3):
            xt = (x + j) % 4
            first[k, j] = push(
                source(k, xt), landing(k, x, dp), step_a, k * 3 + j - 1, at.row(xt)
            )
        first[k, 0] = pltpu.make_async_copy(source(k, x), landing(k, x, dp), local.at[k])
        first[k, 0].start()

    weights = [
        Gather(
            at.y, at.zl, lambda y, zl: (replica(y, zl), x, at.zh), whole(k), half(k), step_dp, k * 9,
            to_sibling(k),
        )
        for k in range(4)
    ]
    w_qkv, w_out, w_gu, w_down = weights

    def begin(k):
        first[k, 0].wait()
        for j in range(1, 4):
            first[k, j].wait_recv()
        weights[k].start()

    def from_sibling(k):
        ref = whole(k)(at.y, at.zl)
        for slot in range(8):
            settle(ref, step_core, k * 8 + slot, at.sibling()).wait_recv()

    slot = pl.ds(pl.multiple_of(at.g * 256, 256), 256)
    send_rows(0)
    gx = column_gather(at, x_v, act, 0)
    gx.start(x_in)
    par_copies = []
    for j, device in enumerate(group_others(at)):
        par_copies.append(push(par_in, par.at[:, slot], step_par, j, device))
    own = [
        pltpu.make_async_copy(x_in, x_v.at[:, slot], local.at[4]),
        pltpu.make_async_copy(par_in, par.at[:, slot], local.at[5]),
        pltpu.make_async_copy(cot_in, cot.at[:, slot], local.at[6]),
    ]
    for copy in own:
        copy.start()
    line = seg[...].reshape(1, TOK).astype(F32)
    seg_row[...] = jnp.broadcast_to(line, (8, TOK))
    seg_col[...] = jnp.transpose(jnp.broadcast_to(line, (128, TOK)))
    begin(0)
    make_tables(seg_col, seg_row, tables)
    raw_copy.wait()
    both = raw[...]
    split[0] = both[:, 0, :]
    split[1] = both[:, 1, :]
    gx.forward_ring()
    gx.spread_pair()
    w_qkv.forward_ring()
    w_qkv.spread_pair()
    send_rows(1)
    gx.spread_far()
    w_qkv.forward_pair()
    begin(1)
    gx.finish()
    gcot = column_gather(at, cot, act, 9)
    gcot.start(cot_in)
    send_rows(3)
    send_rows(2)
    for copy in own:
        copy.wait()
    for copy in par_copies:
        copy.wait_recv()

    def norm_rows(i, carry):
        block = pl.ds(pl.multiple_of(i * 32, 32), 32)
        scaled, _ = norm(x_v[block, :].astype(F32))
        normed[block, :] = (scaled * par[0:1, :] + par[1:2, :]).astype(BF)
        return carry

    lax.fori_loop(0, TOK // 32, norm_rows, 0)
    w_qkv.finish()
    w_out.forward_ring()
    w_out.spread_pair()
    from_sibling(0)
    outgoing = []

    def put(src, dst, index):
        copy = pltpu.make_async_copy(src, dst, local.at[index])
        copy.start()
        outgoing.append(copy)

    for n in range(3):
        cols = pl.ds(n * 256, 256)
        weight = qkv_s[:, :, :, cols].reshape(D, 256)
        proj[:, cols] = jnp.dot(normed[...], weight, preferred_element_type=F32) + bias[
            cols
        ].reshape(1, 256)
    put(normed, normed_out, 7)
    put(qkv_s, qkv_s_out, 8)
    put(x_v.at[own_rows(at)], own_out, 9)
    put(par, par_out, 10)
    sib = (sib_send, sib_recv)
    sib_copies = []
    for xt in range(4):
        cols = pl.ds(xt * 512 + pl.multiple_of((1 - core) * 256, 256), 256)
        sib_copies.append(push(normed.at[:, cols], norm_sib.at[xt], sib, xt, at.sibling()))
    between = [
        lambda: (w_out.forward_pair(), gcot.forward_ring(), gcot.spread_pair()),
        lambda: (begin(3),),
        lambda: (w_out.finish(),),
        lambda: None,
    ]
    attend(proj, tables, seg_col, seg_row, qkv_out, att_out, max_out, sum_out, between)
    from_sibling(1)
    put(out_s, out_s_out, 11)
    put(tables, tab_out, 12)
    rs = RowScatter(
        at, part, far_in, other_in, half_in, full_in, pair_in, pair_out, (rs_send, rs_recv)
    )

    def product(xt):
        weight = out_s[...].reshape(256, D)
        block = pl.ds(pl.multiple_of(xt * 128, 128), 128)
        part[block, :] = jnp.dot(att_out[block, :], weight, preferred_element_type=F32).astype(BF)

    product((x + 2) % 4)
    rs.zero()
    product((x + 1) % 4)
    product((x + 3) % 4)
    rs.sides()
    product(x)
    begin(2)
    w_down.forward_ring()
    rs.first()
    w_down.spread_pair()
    rs.third()
    gcot.spread_far()
    rs.second()
    w_gu.forward_ring()
    w_gu.spread_pair()
    hidden_in = rs.fourth() + x_v[own_rows(at), :].astype(F32)
    hidden_out[...] = hidden_in
    scaled, _ = norm(hidden_in)
    rows[...] = (scaled * par[2:3, :] + par[3:4, :]).astype(BF)
    normed2[own_rows(at), :] = rows[...]
    gn = row_gather(at, normed2, act, 18)
    gn.start(rows)
    gcot.finish()
    put(cot, cot_out, 14)
    sib_copies.append(push(cot, cot_sib, sib, 4, at.sibling()))
    cols = pl.ds(pl.multiple_of((1 - core) * 128, 128), 128)
    sib_copies.append(push(att_out.at[:, cols], att_sib, sib, 5, at.sibling()))
    w_down.forward_pair()
    gn.forward_ring()
    gn.spread_pair()
    w_gu.forward_pair()
    w_down.finish()
    from_sibling(3)
    put(down_s, down_s_out, 15)
    for n in range(3):
        weight = down_s[...].reshape(WIDE, D)[n * 256 : (n + 1) * 256]
        grad_hidden[:, pl.ds(n * 256, 256)] = lax.dot_general(
            cot[...], weight, ROWS_BY_COLS, preferred_element_type=F32
        ).astype(BF)
    gn.spread_far()
    w_gu.finish()
    from_sibling(2)
    gn.finish()
    put(normed2, normed2_out, 16)
    for k in range(4):
        for j in range(1, 4):
            first[k, j].wait_send()
        weights[k].drain()
    for copy in core_copies + par_copies:
        copy.wait_send()
    for copy in sib_copies:
        copy.wait()
    for program in (gx, gcot, gn, rs):
        program.drain()
    for copy in outgoing:
        copy.wait()


def front(*operands):
    shape = jax.ShapeDtypeStruct
    vmem = pltpu.VMEM
    return pl.pallas_call(
        front_kernel,
        out_shape=(
            shape((TOK, D), BF),
            shape((8, D), F32),
            shape((TOK, D), BF),
            shape((TOK, WIDE), BF),
            shape((TOK, 256), BF),
            shape((TOK, 128), F32),
            shape((TOK, 128), F32),
            shape((3, TOK, 384), F32),
            shape((OWN, D), BF),
            shape((TOK, 128), F32),
            shape((8, TOK), F32),
            shape((TOK, WIDE), BF),
            shape((OWN, D), F32),
            shape((TOK, D), BF),
            shape((4, 16, 32, WIDE), BF),
            shape((16, 16, D), BF),
            shape((2, 4, 16, 32, WIDE), BF),
            shape((16, 48, D), BF),
            shape((4, TOK, 256), BF),
            shape((TOK, D), BF),
            shape((TOK, 128), BF),
        ),
        in_specs=[IN_ANY] * 2 + [IN_VMEM] * 6 + [IN_ANY] * 4,
        out_specs=(IN_ANY,) * 3
        + (IN_VMEM,) * 4
        + (IN_ANY,) * 2
        + (IN_VMEM,) * 4
        + (IN_ANY,) * 8,
        scratch_shapes=[
            vmem((TOK, D), BF),
            vmem((TOK, D), BF),
            vmem((8, D), F32),
            vmem((8, 256), F32),
            vmem((TOK, WIDE), F32),
            vmem((3, TOK, 384), F32),
            vmem((4, 16, 32, WIDE), BF),
            vmem((16, 16, D), BF),
            vmem((16, 48, D), BF),
            vmem((TOK, D), BF),
            vmem((TOK, D), BF),
            vmem((OWN, D), BF),
            vmem((32, 2, 2816), BF),
            vmem((2, 32, 2816), BF),
        ]
        + scatter_scratch()
        + dma_sems(7)
        + dma_sems(27)
        + dma_sems(12)
        + dma_sems(36)
        + dma_sems(32)
        + dma_sems(6)
        + [pltpu.SemaphoreType.DMA((17,))],
        compiler_params=params(1),
        name="front",
    )(*operands)


def own_rows(at):
    return pl.ds(pl.multiple_of(at.g * OWN, OWN), OWN)


def columns_of(rows, g):
    return rows.at[:, pl.ds(pl.multiple_of(g * 256, 256), 256)]


def start_columns(at, rows, full, sems, base, local):
    pltpu.make_async_copy(columns_of(rows, at.g), full.at[own_rows(at)], local).start()
    for k in range(1, 8):
        g = (at.g + k) % 8
        push(columns_of(rows, g), full.at[own_rows(at)], sems, base + k - 1, at.group(g))


def finish_columns(at, rows, full, sems, base, local):
    pltpu.make_async_copy(columns_of(rows, at.g), full.at[own_rows(at)], local).wait()
    for k in range(7):
        copy = settle(columns_of(rows, at.g), sems, base + k, at.group(at.g))
        copy.wait_send()
        copy.wait_recv()


def norm(value):
    mean = jnp.mean(value, axis=1, keepdims=True)
    square = jnp.mean(value * value, axis=1, keepdims=True)
    inverse = lax.rsqrt(square - mean * mean + EPSILON)
    return (value - mean) * inverse, inverse


def norm_back(grad, scaled, inverse, gain):
    inner = grad * gain
    mean = jnp.mean(inner, axis=1, keepdims=True)
    along = jnp.mean(inner * scaled, axis=1, keepdims=True)
    return inverse * (inner - mean - scaled * along)


def rotary(value, tables, sign):
    width = value.shape[1]
    return (
        value * tables[0]
        + pltpu.roll(value, width - 8, 1) * (sign * tables[1])
        + pltpu.roll(value, 8, 1) * (sign * tables[2])
    )


def make_tables(seg_col, seg_row, tables):
    half = ROT // 2
    for block in range(4):
        rows = pl.ds(block * 128, 128)
        places = lax.broadcasted_iota(jnp.int32, (128, 128), 0) + block * 128
        before = jnp.where(seg_row[0:1, :] < seg_col[rows, 0:1], 1.0, 0.0)
        starts = jnp.sum(before, axis=1, keepdims=True)
        offsets = places.astype(F32) - starts
        lane = lax.broadcasted_iota(jnp.int32, (128, 128), 1)
        entry = lane % HD
        power = (entry % half).astype(F32) * (-2.0 * math.log(10000.0) / ROT)
        angles = offsets * jnp.exp(power)
        cosine, sine = jnp.cos(angles), jnp.sin(angles)
        keep = jnp.where(entry < ROT, cosine, 1.0)
        fore = jnp.where(entry < half, -sine, 0.0)
        back = jnp.where((entry >= half) & (entry < ROT), sine, 0.0)
        for j, (table, rest) in enumerate(((keep, 1.0), (fore, 0.0), (back, 0.0))):
            low = lane < HD
            tables[j, rows, 0:128] = table
            tables[j, rows, 128:256] = jnp.where(low, rest, table)
            tables[j, rows, 256:384] = jnp.where(low, table, rest)


def head_part(value, head, kind):
    start = head * 3 * HD + kind * HD
    return value[:, start : start + HD]


def allowed(seg_col, seg_row, block, keys):
    start = block * 128
    rows = lax.broadcasted_iota(jnp.int32, (128, keys), 0) + start
    cols = lax.broadcasted_iota(jnp.int32, (128, keys), 1)
    same = seg_col[start : start + 128, 0:1] == seg_row[0:1, :keys]
    return (cols <= rows) & same


def attend(proj, tables, seg_col, seg_row, qkv_out, att_out, max_out, sum_out, between):
    scale = 1.0 / math.sqrt(HD)
    for half in range(2):
        cols = pl.ds(half * 384, 384)
        tab = (tables[0], tables[1], tables[2])
        qkv_out[:, cols] = rotary(proj[:, cols], tab, 1.0).astype(BF)
    for block in range(4):
        keys = (block + 1) * 128
        rows = pl.ds(block * 128, 128)
        mask = allowed(seg_col, seg_row, block, keys)
        outs, maxima, totals = [], [], []
        for head in range(HEADS):
            q = head_part(qkv_out[rows, :], head, 0)
            k = head_part(qkv_out[pl.ds(0, keys), :], head, 1)
            v = head_part(qkv_out[pl.ds(0, keys), :], head, 2)
            score = lax.dot_general(q, k, ROWS_BY_COLS, preferred_element_type=F32) * scale
            score = jnp.where(mask, score, -1e30)
            top = jnp.max(score, axis=1, keepdims=True)
            raised = jnp.exp(score - top)
            total = jnp.sum(raised, axis=1, keepdims=True)
            low = (raised / total).astype(BF)
            outs.append(jnp.dot(low, v, preferred_element_type=F32))
            maxima.append(top)
            totals.append(total)
        att_out[rows, :] = jnp.concatenate(outs, axis=1).astype(BF)
        for head in range(HEADS):
            max_out[rows, head : head + 1] = maxima[head]
            sum_out[rows, head : head + 1] = totals[head]
        if block < len(between):
            between[block]()


def attend_back(
    qkv, grad_att, tables, seg_col, seg_row, maxima, totals, grad_out, pieces, between
):
    scale = 1.0 / math.sqrt(HD)
    pieces[...] = jnp.zeros_like(pieces)
    for block in range(4):
        keys = (block + 1) * 128
        rows = pl.ds(block * 128, 128)
        upto = pl.ds(0, keys)
        mask = allowed(seg_col, seg_row, block, keys)
        for head in range(HEADS):
            q = head_part(qkv[rows, :], head, 0)
            k = head_part(qkv[upto, :], head, 1)
            v = head_part(qkv[upto, :], head, 2)
            grad = grad_att[rows, :][:, head * HD : (head + 1) * HD]
            score = lax.dot_general(q, k, ROWS_BY_COLS, preferred_element_type=F32) * scale
            score = jnp.where(mask, score, -1e30)
            probs = jnp.exp(score - maxima[rows, head : head + 1]) / totals[rows, head : head + 1]
            grad_probs = lax.dot_general(grad, v, ROWS_BY_COLS, preferred_element_type=F32)
            delta = jnp.sum(probs * grad_probs, axis=1, keepdims=True)
            grad_score = (probs * (grad_probs - delta)).astype(BF)
            pieces[head, 0, rows, :] = (
                jnp.dot(grad_score, k, preferred_element_type=F32) * scale
            )
            pieces[head, 1, upto, :] += (
                lax.dot_general(grad_score, q, OVER_ROWS, preferred_element_type=F32) * scale
            )
            pieces[head, 2, upto, :] += lax.dot_general(
                probs.astype(BF), grad, OVER_ROWS, preferred_element_type=F32
            )
        between[block]()
    tab = (tables[0], tables[1], tables[2])
    sums = []
    for half in range(2):
        parts = [pieces[half * 2 + j // 3, j % 3] for j in range(6)]
        cols = pl.ds(half * 384, 384)
        low = rotary(jnp.concatenate(parts, axis=1), tab, -1.0).astype(BF)
        grad_out[:, cols] = low
        sums.append(jnp.sum(low.astype(F32), axis=0, keepdims=True))
    return jnp.concatenate(sums, axis=1)


def back_kernel(
    n2_h, gu_h, down_h, out_h, qkvs_h, cot_h, normed_h, tab_h, norm_sib_h, cot_sib_h, att_sib_h,
    hidden_in, par, att, qkv, seg_col, seg_row, maxima, totals, x_own, grad_hidden,
    act_out, input_out, gu_f, qkv_f, down_f, out_f, small_f,
    n2, n2_sib, cot, cot_sib, gb, gb_sib, att_sib,
    hidden, hidden_sib, gg, gg_sib, gate_up_sib, grad_up, gp_sib, grad_att, grad_in,
    out_s, rows, sums, ln_t, small_t,
    part, part2,
    *rest,
):
    at = Place()
    others = [at.replica((at.dp + k) % 16) for k in range(1, 16)]
    core, q, x = at.core, at.q, at.x
    cq = core * 8 + q
    rest = list(rest)

    def take(amount):
        head, rest[:] = rest[:amount], rest[amount:]
        return head

    boxes = [take(6) for _ in range(2)]
    boxes.append(boxes[0])
    arrays = [take(6) for _ in range(4)]
    (gu_a, qkv_a, down_a, out_a) = [a[0] for a in arrays]
    packs = [a[-1] for a in arrays]
    rs_sems, act_sems, sib_sems = take(2), take(2), take(2)
    dps_sems, row_sems, dpg_sems, core_sems = take(2), take(2), take(2), take(2)
    ln_sems, small_sems = take(2), take(2)
    (local,) = take(1)
    finals = (gu_f, qkv_f, down_f, out_f)

    loads = {}

    def load(name, src, dst, index):
        loads[name] = lambda: pltpu.make_async_copy(src, dst, local.at[index])
        loads[name]().start()

    def columns(c, xt):
        return pl.ds(pl.multiple_of(xt * 512 + c * 256, 256), 256)

    exchange = {}

    def to_sibling(name, src, dst, index):
        exchange[name] = (dst, index)
        push(src, inbox(name), sib_sems, index, at.sibling())

    def inbox(name):
        ref = exchange[name][0]
        return ref.at[name[1]] if isinstance(name, tuple) else ref

    def exchanged(name):
        settle(inbox(name), sib_sems, exchange[name][1], at.sibling()).wait_recv()

    def load_cot_sib(a):
        cols = pl.ds(a * 512, 512)
        load(("cot_sib", a), cot_sib_h.at[:, cols], cot_sib.at[a % 2], 3 if a % 2 else 18)

    load("n2", n2_h, n2, 0)
    def pack_for(k, xt):
        if k == 0:
            return packs[0].at[:, xt]
        if k == 1:
            return packs[1].at[xt // 2, xt % 2]
        return packs[k].at[xt // 2, 0, :, pl.ds(pl.multiple_of((xt % 2) * 512, 512), 512)]

    def landing(k, xs, p):
        if k == 0:
            return gu_f.at[xs, :, p]
        if k == 1:
            return qkv_f.at[p, :, pl.ds(pl.multiple_of(xs * WIDE, WIDE), WIDE)]
        return finals[k].at[xs, p]

    def slot(y, zl):
        return core * 8 + y * 2 + zl

    def whole(k):
        def of(y, zl):
            p = slot(y, zl)
            if k == 0:
                return gu_f.at[:, :, p]
            if k == 1:
                return qkv_f.at[p]
            return finals[k].at[:, p]

        return of

    def half(k):
        def of(y, zl, side):
            p = slot(y, zl)
            if k == 0:
                return gu_f.at[pl.ds(side * 2, 2), :, p]
            if k == 1:
                return qkv_f.at[p, :, pl.ds(side * 2 * WIDE, 2 * WIDE)]
            return finals[k].at[pl.ds(side * 2, 2), p]

        return of

    def share(k):
        def on_piece(y, zl, index):
            ref = whole(k)(y, zl)
            push(ref, ref, core_sems, k * 8 + index, at.sibling())

        return on_piece

    scatters = [
        PieceScatter(at, arrays[k][0], arrays[k][1:], dps_sems, k * 9) for k in range(4)
    ]
    s_gu, s_qkv, s_down, s_out = scatters
    gathers = [
        Gather(
            at.y, at.zl, lambda y, zl: ((y * 2 + zl) * 2 + core, x, at.zh), whole(k), half(k),
            dpg_sems, k * 9, share(k),
        )
        for k in range(4)
    ]
    g_gu, g_qkv, g_down, g_out = gathers
    def send_rows(k):
        scatters[k].fourth()
        for j in (2, 1, 3):
            xt = (x + j) % 4
            push(pack_for(k, xt), landing(k, x, cq), row_sems, k * 3 + j - 1, at.row(xt))
        pltpu.make_async_copy(pack_for(k, x), landing(k, x, cq), local.at[12 + k]).start()

    def begin(k, pair=True):
        pltpu.make_async_copy(pack_for(k, x), landing(k, x, cq), local.at[12 + k]).wait()
        for j in range(3):
            settle(pack_for(k, x), row_sems, k * 3 + j, at.row(x)).wait_recv()
        if pair:
            gathers[k].start()
        else:
            gathers[k].start_ring()

    rs1, rs2, rs3 = [
        RowScatter(at, p, *boxes[j], rs_sems, j * 9) for j, p in enumerate((part, part2, part))
    ]
    block_of = lambda xt: pl.ds(pl.multiple_of(xt * 128, 128), 128)
    far, right, left = (x + 2) % 4, (x + 1) % 4, (x + 3) % 4
    g_branch = row_gather(at, gb, act_sems, 0)

    def outer_sum(a, b, a_sib, b_sib):
        return lax.dot_general(
            a, b, OVER_ROWS, preferred_element_type=F32
        ) + lax.dot_general(a_sib, b_sib, OVER_ROWS, preferred_element_type=F32)

    def down_grad(a):
        cols = pl.ds(a * 512, 512)
        mine = hidden[:, pl.ds(pl.multiple_of(core * 384, 128), 384)]
        loads["cot_sib", a]().wait()
        down_a[a // 2, 0, :, :, pl.ds((a % 2) * 512, 512)] = (
            outer_sum(mine, cot[:, cols], hidden_sib[...], cot_sib[a % 2])
            .astype(BF)
            .reshape(8, 48, 512)
        )
        if a < 2:
            load_cot_sib(a + 2)

    def gate_up_grad(xt, carry):
        own, sib = n2[:, columns(core, xt)], n2_sib[xt]
        gu_a[0, xt] = outer_sum(own, gg[...], sib, gg_sib[...]).astype(BF).reshape(8, 32, WIDE)
        gu_a[1, xt] = (
            outer_sum(own, grad_up[...], sib, gate_up_sib[...]).astype(BF).reshape(8, 32, WIDE)
        )
        return carry

    def feed_forward(gu_s, gate_v, up_v):
        load("gate", gu_h.at[0], gu_s.at[0], 7)
        load("up", gu_h.at[1], gu_s.at[1], 8)
        load("cot", cot_h, cot, 1)
        load("out_s", out_h, out_s, 2)
        greet(group_others(at) + others)
        for xt in range(4):
            to_sibling(("n2", xt), n2_h.at[:, columns(1 - core, xt)], n2_sib, xt)
        for name in ("n2", "gate", "up"):
            loads[name]().wait()
        lane = lax.broadcasted_iota(jnp.int32, (1, 256), 1)

        def chunk(n):
            cols = pl.ds(n * 256, 256)
            gate_v[...] = jnp.dot(n2[...], gu_s[0, :, cols], preferred_element_type=F32)
            up_v[...] = jnp.dot(n2[...], gu_s[1, :, cols], preferred_element_type=F32)
            kept = (lane >= (128 if n == 0 else 0)) | (x < 2)

            def gated(i, carry):
                block = pl.ds(pl.multiple_of(i * 64, 64), 64)
                gate, up = gate_v[block, :], up_v[block, :]
                sig = jax.nn.sigmoid(gate)
                act = gate * sig
                grad = jnp.where(kept, grad_hidden[block, cols].astype(F32), 0.0)
                hidden[block, cols] = jnp.where(kept, act * up, 0.0).astype(BF)
                gg[block, cols] = (grad * up * (sig * (1.0 + gate * (1.0 - sig)))).astype(BF)
                grad_up[block, cols] = (grad * act).astype(BF)
                return carry

            lax.fori_loop(0, 8, gated, 0)

        for n in range(3):
            chunk(n)
        to_sibling(
            "hidden",
            hidden.at[:, pl.ds(pl.multiple_of((1 - core) * 384, 128), 384)],
            hidden_sib,
            5,
        )
        to_sibling("gg", gg, gg_sib, 6)
        to_sibling("up", grad_up, gate_up_sib, 7)

        def product(xt):
            block = block_of(xt)
            value = lax.dot_general(
                gg[block, :], gu_s[0], ROWS_BY_COLS, preferred_element_type=F32
            ) + lax.dot_general(
                grad_up[block, :], gu_s[1], ROWS_BY_COLS, preferred_element_type=F32
            )
            part[block, :] = value.astype(BF)

        product(far)
        rs1.zero()
        exchanged("gg")
        exchanged("up")
        for xt in range(4):
            exchanged(("n2", xt))
        lax.fori_loop(0, 4, gate_up_grad, 0)
        s_gu.first()
        product(right)
        product(left)
        rs1.sides()
        rs1.first()
        product(x)

    def down_product(down_s):
        load("down", down_h, down_s, 9)
        loads["down"]().wait()

        def product_two(i, carry):
            block = block_of(i)
            part2[block, :] = jnp.dot(
                hidden[block, :], down_s[...], preferred_element_type=F32
            ).astype(BF)
            return carry

        lax.fori_loop(0, 4, product_two, 0)

    load_cot_sib(0)
    load_cot_sib(1)
    pl.run_scoped(
        feed_forward,
        pltpu.VMEM((2, D, WIDE), BF),
        pltpu.VMEM((TOK, 256), F32),
        pltpu.VMEM((TOK, 256), F32),
    )
    s_gu.second(0)
    s_gu.second(1)
    rs1.third()
    rs1.second()
    load("nh", normed_h, n2, 4)
    load("nh_sib", norm_sib_h, n2_sib, 5)
    load("att_sib", att_sib_h, att_sib, 6)
    loads["cot"]().wait()
    exchanged("hidden")
    down_grad(0)
    down_grad(1)
    down_grad(2)
    down_grad(3)
    s_down.first()
    scaled, inverse = norm(hidden_in[...])
    grad = rs1.fourth()
    value = cot[own_rows(at), :].astype(F32) + norm_back(grad, scaled, inverse, par[2:3, :])
    rows[0] = value.astype(BF)
    gb[own_rows(at), :] = value.astype(BF)
    g_branch.start(rows.at[0])
    grad_in[...] = value
    sums[...] = jnp.zeros_like(sums)
    sums[2:3, :] = jnp.sum(grad * scaled, axis=0, keepdims=True)
    sums[3:4, :] = jnp.sum(grad, axis=0, keepdims=True)
    s_gu.third()
    pl.run_scoped(down_product, pltpu.VMEM((WIDE, D), BF))
    g_branch.forward_ring()
    g_branch.spread_pair()
    s_down.second(0)
    s_down.second(1)
    g_branch.spread_far()
    send_rows(0)
    g_branch.finish()
    to_sibling("gb", gb, gb_sib, 13)
    settle(inbox("gg"), sib_sems, exchange["gg"][1], at.sibling()).wait_send()
    gp = gg

    def qkv_grad(xt, carry):
        qkv_a[xt // 2, xt % 2] = (
            outer_sum(n2[:, columns(core, xt)], gp[...], n2_sib[xt], gp_sib[...])
            .astype(BF)
            .reshape(8, 32, WIDE)
        )
        return carry

    def out_grad():
        exchanged("gb")
        loads["att_sib"]().wait()
        mine = att[:, pl.ds(pl.multiple_of(core * 128, 128), 128)]
        for a in range(2):
            cols = pl.ds(a * 1024, 1024)
            out_a[a, 0] = (
                outer_sum(mine, gb[:, cols], att_sib[...], gb_sib[:, cols])
                .astype(BF)
                .reshape(8, 16, 1024)
            )
        s_out.first()

    def attention(tables, pieces, qkv_s):
        load("tab", tab_h, tables, 10)
        load("qkv_s", qkvs_h, qkv_s, 11)
        loads["out_s"]().wait()
        grad_att[...] = lax.dot_general(
            gb[...], out_s[...].reshape(256, D), ROWS_BY_COLS, preferred_element_type=F32
        ).astype(BF)
        rs2.zero()
        rs2.sides()
        loads["tab"]().wait()

        between = [
            lambda: (begin(0),),
            lambda: (out_grad(),),
            lambda: (rs2.first(), s_down.third()),
            lambda: (g_gu.forward_ring(),),
        ]
        bias_sums = attend_back(
            qkv, grad_att, tables, seg_col, seg_row, maxima, totals, gp, pieces, between
        )
        to_sibling("gp", gp, gp_sib, 14)
        loads["qkv_s"]().wait()
        rs1.drain()

        def product(xt):
            block = block_of(xt)
            weight = qkv_s[...].reshape(D, WIDE)
            part[block, :] = lax.dot_general(
                gp[block, :], weight, ROWS_BY_COLS, preferred_element_type=F32
            ).astype(BF)

        product(far)
        rs3.zero()
        product(right)
        product(left)
        rs3.sides()
        s_out.second(0)
        s_out.second(1)
        exchanged("gp")
        loads["nh"]().wait()
        loads["nh_sib"]().wait()
        lax.fori_loop(0, 4, qkv_grad, 0)
        s_qkv.first()
        product(x)
        g_gu.spread_pair()
        sums[4:7, 0:256] = jnp.concatenate([bias_sums[:, j * 256 : (j + 1) * 256] for j in range(3)])

    pl.run_scoped(
        attention,
        pltpu.VMEM((3, TOK, 384), F32),
        pltpu.VMEM((HEADS, 3, TOK, HD), F32),
        pltpu.VMEM((4, 16, 32, WIDE), BF),
    )
    rs3.first()
    rs3.third()
    send_rows(2)
    s_qkv.second(0)
    s_qkv.second(1)
    rs3.second()
    g_gu.forward_pair()
    begin(2)
    rs2.third()
    rs2.second()
    scaled, inverse = norm(x_own[...].astype(F32))
    grad = rs3.fourth()
    value = grad_in[...] + norm_back(grad, scaled, inverse, par[0:1, :])
    rows[2] = value.astype(BF)
    start_columns(at, rows.at[2], input_out, act_sems, 16, local.at[17])
    sums[0:1, :] = jnp.sum(grad * scaled, axis=0, keepdims=True)
    sums[1:2, :] = jnp.sum(grad, axis=0, keepdims=True)
    own_columns = pl.ds(pl.multiple_of(at.g * 256, 256), 256)
    ln_copies = []
    for j in range(1, 8):
        g = (at.g + j) % 8
        ln_copies.append(
            push(
                sums.at[pl.ds(0, 4), pl.ds(pl.multiple_of(g * 256, 256), 256)],
                ln_t.at[j - 1],
                ln_sems,
                j - 1,
                at.group(g),
            )
        )
    s_qkv.third()
    s_out.third()
    g_down.forward_ring()
    g_down.spread_pair()
    total = sums[0:4, own_columns]
    for j in range(7):
        ln_copies[j].wait_recv()
        total += ln_t[j]
    small_t[pl.ds(at.dp, 1), 0:4] = total[None]
    small_t[pl.ds(at.dp, 1), 4:8] = sums[4:8, 0:256][None]
    small_copies = [
        push(small_t.at[at.dp], small_t.at[at.dp], small_sems, j, device)
        for j, device in enumerate(others)
    ]
    send_rows(1)
    send_rows(3)
    begin(1)
    begin(3)
    total = rs2.fourth() + hidden_in[...]
    rows[1] = total.astype(BF)
    start_columns(at, rows.at[1], act_out, act_sems, 9, local.at[16])
    g_qkv.forward_ring()
    g_qkv.spread_pair()
    g_out.forward_ring()
    g_out.spread_pair()
    g_gu.finish()
    g_down.forward_pair()
    g_qkv.forward_pair()
    g_out.forward_pair()
    g_down.finish()
    for copy in small_copies:
        copy.wait_recv()
    result = small_t[0]
    for j in range(1, 16):
        result += small_t[j]
    small_f[...] = result
    g_out.finish()
    g_qkv.finish()
    for k in range(4):
        ref = whole(k)(at.y, at.zl)
        for index in range(8):
            settle(ref, core_sems, k * 8 + index, at.sibling()).wait_recv()
            settle(ref, core_sems, k * 8 + index, at.sibling()).wait_send()
        scatters[k].drain()
        gathers[k].drain()
        for j in range(3):
            settle(pack_for(k, x), row_sems, k * 3 + j, at.row(x)).wait_send()
    for copy in ln_copies + small_copies:
        copy.wait_send()
    for name in exchange:
        if name == "gg":
            continue
        settle(inbox(name), sib_sems, exchange[name][1], at.sibling()).wait_send()
    g_branch.drain()
    rs2.drain()
    rs3.drain()
    finish_columns(at, rows.at[1], act_out, act_sems, 9, local.at[16])
    finish_columns(at, rows.at[2], input_out, act_sems, 16, local.at[17])


def back(
    n2, gu_s, down_s, out_s, qkv_s, cot, normed, tables, norm_sib, cot_sib, att_sib,
    hidden_in, par, att, qkv, seg_col, seg_row, maxima, totals, x_own, grad_hidden,
):
    shape = jax.ShapeDtypeStruct
    vmem = pltpu.VMEM
    wide = vmem((TOK, D), BF)
    inner = vmem((TOK, WIDE), BF)
    quarters = vmem((4, TOK, 256), BF)
    box = scatter_scratch()[1:7]
    return pl.pallas_call(
        back_kernel,
        out_shape=(
            shape((TOK, 256), BF),
            shape((TOK, 256), BF),
            shape((4, 2, 16, 32, WIDE), BF),
            shape((16, 32, 4 * WIDE), BF),
            shape((4, 16, 48, 512), BF),
            shape((4, 16, 16, 512), BF),
            shape((8, 256), F32),
        ),
        in_specs=[IN_ANY] * 11 + [IN_VMEM] * 10,
        out_specs=(IN_ANY,) * 6 + (IN_VMEM,),
        scratch_shapes=[
            wide, quarters, wide, vmem((2, TOK, 512), BF), wide, wide, vmem((TOK, 128), BF),
            inner, vmem((TOK, 384), BF), inner, inner, inner, inner, inner,
            vmem((TOK, 256), BF), vmem((OWN, D), F32),
            vmem((16, 16, D), BF), vmem((3, OWN, D), BF), vmem((8, D), F32),
            vmem((7, 4, 256), F32), vmem((16, 8, 256), F32),
            wide, wide,
        ]
        + box * 2
        + piece_scratch(4, 32, WIDE)
        + piece_scratch(2, 32, WIDE)
        + piece_scratch(1, 48, 1024)
        + piece_scratch(1, 16, 1024)
        + dma_sems(27)
        + dma_sems(23)
        + dma_sems(15)
        + dma_sems(36)
        + dma_sems(12)
        + dma_sems(36)
        + dma_sems(32)
        + dma_sems(7)
        + dma_sems(15)
        + [pltpu.SemaphoreType.DMA((19,))],
        compiler_params=params(2),
        name="back",
    )(
        n2, gu_s, down_s, out_s, qkv_s, cot, normed, tables, norm_sib, cot_sib, att_sib,
        hidden_in, par, att, qkv, seg_col, seg_row, maxima, totals, x_own, grad_hidden,
    )


def widen_gate_up_kernel(low, out):
    for j in range(2):
        shares = [low[x, j] for x in range(4)]
        out[:, j, 0:768] = shares[0].astype(F32)
        out[:, j, 768:1536] = shares[1].astype(F32)
        out[:, j, 1536:2176] = shares[2][:, 128:].astype(F32)
        out[:, j, 2176:2816] = shares[3][:, 128:].astype(F32)


def widen_gate_up(low):
    return pl.pallas_call(
        widen_gate_up_kernel,
        out_shape=jax.ShapeDtypeStruct((512, 2, 2816), F32),
        grid=(4,),
        in_specs=[pl.BlockSpec((4, 2, 128, WIDE), lambda i: (0, 0, i, 0))],
        out_specs=pl.BlockSpec((128, 2, 2816), lambda i: (i, 0, 0)),
        compiler_params=pltpu.CompilerParams(vmem_limit_bytes=VMEM_LIMIT),
        name="widen_gate_up",
    )(low)


def on_device(
    block_in, segments, ln1_gain, ln1_bias, qkv_weight, qkv_bias, out_weight,
    ln2_gain, ln2_bias, gate_up_weight, down_weight, cotangent,
):
    (
        cot_full, par, normed, qkv, attended, maxima, totals, tables, x_own,
        seg_col, seg_row, grad_hidden,
        hidden_in, normed_two, qkv_s, out_s, gu_s, down_s, norm_sib, cot_sib, att_sib,
    ) = front(
        block_in, cotangent, ln1_gain, ln1_bias, ln2_gain, ln2_bias, qkv_bias, segments,
        qkv_weight, out_weight, gate_up_weight, down_weight,
    )
    activations, input_grad, gu_f, qkv_f, down_f, out_f, small = back(
        normed_two, gu_s.reshape(2, D, WIDE), down_s.reshape(WIDE, D), out_s, qkv_s, cot_full,
        normed, tables, norm_sib, cot_sib, att_sib, hidden_in, par, attended, qkv, seg_col, seg_row, maxima, totals, x_own, grad_hidden,
    )
    gu_grad = widen_gate_up(gu_f.reshape(4, 2, 512, WIDE))
    down_f = down_f.reshape(4, WIDE, 512)
    down_grad = jnp.concatenate(
        [down_f[0], down_f[1], down_f[2, 128:], down_f[3, 128:]], axis=0
    ).astype(F32)
    return (
        activations,
        input_grad,
        small[0],
        small[1],
        qkv_f.reshape(512, 4 * WIDE).astype(F32),
        small[4:7].reshape(WIDE),
        out_f.reshape(1024, 512).astype(F32),
        small[2],
        small[3],
        gu_grad,
        down_grad,
    )


def solution(mesh):
    wide = P("dp", ("row", "col"))
    vector = P(("row", "col"))
    return jax.shard_map(
        on_device,
        mesh=mesh,
        in_specs=(
            wide, P("dp"), vector, vector, P("row", "col"), P(("col", "row")), P("col", "row"),
            vector, vector, P("row", None, "col"), P("col", "row"), wide,
        ),
        out_specs=(
            wide, wide, vector, vector, P("row", "col"), P(("col", "row")), P("col", "row"),
            vector, vector, P("row", None, "col"), P("col", "row"),
        ),
        check_vma=False,
    )
```
